32 devices in a mesh: dp: 8 (over z, y), tensor: 4 (over x, core).
Axes of the slice: x: 2, y: 2, z: 4, core: 2. Of those that a mesh axis runs over, the one named last changes fastest.
Arguments:
- visual: bfloat16 [8, 144, 768], P('dp', 'tensor'), may hold values from -6 to 6
- queries: bfloat16 [8, 800, 768], P('dp', 'tensor'), may hold values from -6 to 6
- valid_windows: int32 [8, 1], P('dp'), may hold values from 0 to 1, as said below
- answer_start: int32 [8], P('dp'), may hold values from 1 to 799
- shifts: int32 [8, 2], P('dp'), may hold values from 1 to 11
- norm_scale: float32 [2, 6, 768], replicated, may hold values from 0.5 to 1.5
- norm_shift: float32 [2, 6, 768], replicated, may hold values from -1.25 to 1.25
- attn_in: bfloat16 [2, 4, 768, 3, 768], P(None, None, None, None, 'tensor'), may hold values from -0.21875 to 0.21875
- attn_out: bfloat16 [2, 4, 768, 768], P(None, None, 'tensor'), may hold values from -0.625 to 0.625
- rel_bias: float32 [2, 12, 529], P(None, 'tensor'), may hold values from -6 to 6
- mlp_in: bfloat16 [2, 2, 768, 3072], P(None, None, None, 'tensor'), may hold values from -0.21875 to 0.21875
- mlp_in_bias: float32 [2, 2, 3072], P(None, None, 'tensor'), may hold values from -3 to 3
- mlp_out: bfloat16 [2, 2, 3072, 768], P(None, None, 'tensor'), may hold values from -0.109375 to 0.109375
- mlp_out_bias: float32 [2, 2, 768], replicated, may hold values from -1.25 to 1.25
- grad_visual_out: float32 [8, 144, 768], P('dp', 'tensor'), may hold values from -6 to 6
- grad_query_out: float32 [8, 800, 768], P('dp', 'tensor'), may hold values from -6 to 6
Outputs:
- visual_out: bfloat16 [8, 144, 768], P('dp', 'tensor')
- query_out: bfloat16 [8, 800, 768], P('dp', 'tensor')
- grad_visual: float32 [8, 144, 768], P('dp', 'tensor')
- grad_query: float32 [8, 800, 768], P('dp', 'tensor')
- grad_norm_scale: float32 [2, 6, 768], replicated
- grad_norm_shift: float32 [2, 6, 768], replicated
- grad_attn_in: float32 [2, 4, 768, 3, 768], P(None, None, 'dp', None, 'tensor')
- grad_attn_out: float32 [2, 4, 768, 768], P(None, None, 'tensor', 'dp')
- grad_rel_bias: float32 [2, 12, 529], P(None, 'tensor')
- grad_mlp_in: float32 [2, 2, 768, 3072], P(None, None, 'dp', 'tensor')
- grad_mlp_in_bias: float32 [2, 2, 3072], P(None, None, 'tensor')
- grad_mlp_out: float32 [2, 2, 3072, 768], P(None, None, 'tensor', 'dp')
- grad_mlp_out_bias: float32 [2, 2, 768], replicated
The draws below stay inside these ranges and needn't reach their ends.
Inputs may be any that keep to these rules, and one draw needn't show every extreme that they name: `valid_windows`: each page has a width w of 1 to 1 window columns; the windows whose column index is below w are 1 in every window row, the others 0; some page has w = 1.
All inputs are finite; a program needn't handle non-finite values.
Results may differ from the reference program's by a relative error of at most 0.029.
Values may be sent and summed in bfloat16 or wider, within the bound.
No kernel may reach another device: no remote copies, remote signals or barrier semaphores. Data moves between devices by JAX's collectives and lax.ppermute only.
A program may use at most 256 MiB of HBM per device.

```python
import jax
import jax.numpy as jnp
from jax import lax

D = 768
HEADS = 12
HDIM = 64
FF = 3072
WIN = 12
QLEN = 800
LAYERS = 2
GH = 1
GW = 1
VIS = 144
RB = 529
GROUPS = 8


def draw_valid_windows(key, part):
    key = jax.random.fold_in(key, 7)
    width_key, widest_key = jax.random.split(key)
    widths = jax.random.randint(width_key, (GROUPS,), 1, GW + 1)
    widest = jax.random.randint(widest_key, (), 0, GROUPS)
    widths = jnp.where(jnp.arange(GROUPS) == widest, GW, widths)
    columns = jnp.arange(GH * GW) % GW
    return (columns[None, :] < widths[:, None]).astype(jnp.int32)


def plant(drawn, rng, low, top_value):
    shape = drawn.shape
    place = [jax.random.randint(jax.random.fold_in(rng, axis), (), 0, shape[axis]) for axis in range(len(shape))]
    drawn = drawn.at[tuple(place)].set(low)
    longest = shape.index(max(shape))
    place[longest] = (place[longest] + 1) % shape[longest]
    return drawn.at[tuple(place)].set(top_value)


def steps_of(key, extent, shards, low, high):
    def one(axis_at, parts):
        heights = jax.random.uniform(jax.random.fold_in(jax.random.fold_in(key, 6), axis_at), (parts,), jnp.float32, low / len(shards), high / len(shards))
        return jnp.repeat(jnp.exp(heights), extent[axis_at] // parts).reshape((-1,) + (1,) * (len(extent) - axis_at - 1))

    loudness = one(*shards[0])
    for cut in shards[1:]:
        loudness = loudness * one(*cut)
    return loudness


def noise(stream_key, shape, width, bound, pieces=(), kind=jnp.bfloat16):
    entries = jax.random.normal(stream_key, shape, jnp.float32) * width
    if len(pieces) > 0:
        entries = steps_of(stream_key, shape, pieces, -0.22, 0.18) * entries
    return jnp.clip(entries, min=-bound, max=bound).astype(kind)


def setup_inputs(seed: int = 0) -> dict:
    arg_keys = jax.random.split(jax.random.key(seed), 17)
    visual = noise(arg_keys[0], (GROUPS, VIS, D), 1.0, 6.0, ((0, 8), (1, 4)))
    queries = noise(arg_keys[1], (GROUPS, QLEN, D), 1.0, 6.0, ((0, 8), (1, 4)))
    valid_windows = draw_valid_windows(jax.random.fold_in(arg_keys[16], 71), 0)
    answer_start = plant(jax.random.randint(arg_keys[3], (GROUPS,), 1, QLEN), jax.random.fold_in(arg_keys[3], 1), 1, QLEN - 1).astype(jnp.int32)
    shifts = plant(jax.random.randint(arg_keys[4], (GROUPS, 2), 1, WIN), jax.random.fold_in(arg_keys[4], 1), 1, WIN - 1).astype(jnp.int32)
    norm_scale = jnp.clip(1.0 + 0.1 * jax.random.normal(arg_keys[5], (LAYERS, 6, D), jnp.float32), 0.5, 1.5)
    norm_shift = noise(arg_keys[6], (LAYERS, 6, D), 0.2, 1.25, (), jnp.float32)
    attn_in = noise(arg_keys[7], (LAYERS, 4, D, 3, D), D ** -0.5, 0.21875, ((4, 4),))
    attn_out = noise(arg_keys[8], (LAYERS, 4, D, D), (D // 8) ** -0.5, 0.625, ((2, 4),))
    rel_bias = noise(arg_keys[9], (LAYERS, HEADS, RB), 1.0, 6.0, ((1, 4),), jnp.float32)
    mlp_in = noise(arg_keys[10], (LAYERS, 2, D, FF), D ** -0.5, 0.21875, ((3, 4),))
    mlp_in_bias = noise(arg_keys[11], (LAYERS, 2, FF), 0.5, 3.0, ((2, 4),), jnp.float32)
    mlp_out = noise(arg_keys[12], (LAYERS, 2, FF, D), FF ** -0.5, 0.109375, ((2, 4),))
    mlp_out_bias = noise(arg_keys[13], (LAYERS, 2, D), 0.2, 1.25, (), jnp.float32)
    grad_visual_out = noise(arg_keys[14], (GROUPS, VIS, D), 1.0, 6.0, ((0, 8), (1, 4)), jnp.float32)
    grad_query_out = noise(arg_keys[15], (GROUPS, QLEN, D), 1.0, 6.0, ((0, 8), (1, 4)), jnp.float32)
    return dict(visual=visual, queries=queries, valid_windows=valid_windows, answer_start=answer_start, shifts=shifts, norm_scale=norm_scale, norm_shift=norm_shift, attn_in=attn_in, attn_out=attn_out, rel_bias=rel_bias, mlp_in=mlp_in, mlp_in_bias=mlp_in_bias, mlp_out=mlp_out, mlp_out_bias=mlp_out_bias, grad_visual_out=grad_visual_out, grad_query_out=grad_query_out)


HIGH = lax.Precision.HIGHEST
NEG = -1000000000.0
EPS = 1e-05

@jax.custom_vjp
def low(v):
    return lax.optimization_barrier(v.astype(jnp.bfloat16)).astype(jnp.float32)

@jax.custom_vjp
def low_back(v):
    return v

def low_keep(v):
    return (low(v), None)

def low_pass(kept, grad):
    return (grad,)

def back_keep(v):
    return (v, None)

def back_low(kept, grad):
    return (low(grad),)
low.defvjp(low_keep, low_pass)
low_back.defvjp(back_keep, back_low)

def both_ways(values):
    return low_back(low(values))

def layer_norm(values, scale_row, shift_row):
    center = values - lax.optimization_barrier(jnp.mean(values, -1, keepdims=True))
    unit_rows = center * lax.rsqrt(lax.optimization_barrier(jnp.mean(center * center, -1, keepdims=True)) + EPS)
    return unit_rows * scale_row + shift_row

def window_cells(field):
    trailing = field.shape[2:]
    blocked = field.reshape((GH, WIN, GW, WIN) + trailing)
    axes_order = (0, 2, 1, 3) + tuple(range(4, 4 + len(trailing)))
    return blocked.transpose(axes_order).reshape((GH * GW, WIN * WIN) + trailing)

def window_parts(tokens, row_shift, col_shift):
    patch_grid = tokens.reshape((GH * WIN, GW * WIN) + tokens.shape[1:])
    patch_grid = jnp.roll(patch_grid, (-row_shift, -col_shift), (0, 1))
    return window_cells(patch_grid)

def window_join(window_rows, row_shift, col_shift):
    trailing = window_rows.shape[2:]
    blocked = window_rows.reshape((GH, GW, WIN, WIN) + trailing)
    axes_order = (0, 2, 1, 3) + tuple(range(4, 4 + len(trailing)))
    patch_grid = blocked.transpose(axes_order).reshape((GH * WIN, GW * WIN) + trailing)
    patch_grid = jnp.roll(patch_grid, (row_shift, col_shift), (0, 1))
    return patch_grid.reshape((GH * WIN * GW * WIN,) + trailing)

def patch_flags(valid_mask, row_shift, col_shift):
    rows_total = GH * WIN
    cols_total = GW * WIN
    source_row = (jnp.arange(rows_total, dtype=jnp.int32)[:, None] + row_shift) % rows_total
    source_col = (jnp.arange(cols_total, dtype=jnp.int32)[None, :] + col_shift) % cols_total
    window_id = source_row // WIN * GW + source_col // WIN
    matches = window_id[:, :, None] == jnp.arange(GH * GW, dtype=jnp.int32)[None, None, :]
    token_ok = lax.optimization_barrier(jnp.sum(jnp.where(matches, valid_mask[None, None, :], 0), -1)) > 0
    wrap_row = jnp.broadcast_to(source_row < row_shift, token_ok.shape)
    wrap_col = jnp.broadcast_to(source_col < col_shift, token_ok.shape)
    return (token_ok, wrap_row, wrap_col)

def window_allowed(valid_mask, row_shift, col_shift):
    token_ok, wrap_row, wrap_col = patch_flags(valid_mask, row_shift, col_shift)
    key_ok = window_cells(token_ok)
    row_class = window_cells(wrap_row)
    col_class = window_cells(wrap_col)
    allowed = key_ok[:, None, :] & (row_class[:, :, None] == row_class[:, None, :]) & (col_class[:, :, None] == col_class[:, None, :])
    return allowed[:, None]

def bias_index():
    places = jnp.arange(WIN * WIN, dtype=jnp.int32)
    row_place = places // WIN
    col_place = places % WIN
    return (row_place[:, None] - row_place[None, :] + WIN - 1) * (2 * WIN - 1) + col_place[:, None] - col_place[None, :] + WIN - 1

def split_heads(values):
    return values.reshape(values.shape[:-1] + (HEADS, HDIM)).swapaxes(-2, -3)

def join_heads(values):
    joined = values.swapaxes(-2, -3)
    return joined.reshape(joined.shape[:-2] + (HEADS * HDIM,))

def attention(source_q, source_kv, weight, addend, allowed):
    queries_h = split_heads(both_ways(jnp.einsum('bsd,de->bse', source_q, weight[:, 0], precision=HIGH)))
    key_rows = split_heads(both_ways(jnp.einsum('bsd,de->bse', source_kv, weight[:, 1], precision=HIGH)))
    value_rows = split_heads(both_ways(jnp.einsum('bsd,de->bse', source_kv, weight[:, 2], precision=HIGH)))
    raw_scores = jnp.einsum('bhqd,bhkd->bhqk', queries_h, key_rows, precision=HIGH) * HDIM ** (-0.5) + addend
    scores = low_back(jnp.where(allowed, raw_scores, NEG))
    attn_probs = low(jax.nn.softmax(scores, axis=-1))
    return join_heads(both_ways(jnp.einsum('bhqk,bhkd->bhqd', attn_probs, value_rows, precision=HIGH)))

def feed_forward(normed, w_up, b_up, w_down, b_down):
    hidden = low_back(jnp.dot(normed, w_up, precision=HIGH) + b_up)
    active = low(jax.nn.gelu(hidden))
    return jnp.dot(active, w_down, precision=HIGH) + b_down

def forward(visual_x, queries_x, valid_mask, answer_from, shift_pair, norm_scale, norm_shift, attn_in, attn_out, rel_bias, mlp_in, mlp_in_bias, mlp_out, mlp_out_bias):
    positions = jnp.arange(QLEN, dtype=jnp.int32)
    before_answer = positions[None, :] < answer_from
    self_allowed = (before_answer | (positions[None, :] <= positions[:, None]))[None, None]
    to_question = before_answer[None, None]
    to_patches = patch_flags(valid_mask, 0, 0)[0].reshape(1, 1, 1, -1)
    table_index = bias_index()
    for layer_index in range(LAYERS):
        row_shift = shift_pair[0] * (layer_index % 2)
        col_shift = shift_pair[1] * (layer_index % 2)
        normed_v = low(layer_norm(visual_x, norm_scale[layer_index, 0], norm_shift[layer_index, 0]))
        normed_q = low(layer_norm(queries_x, norm_scale[layer_index, 1], norm_shift[layer_index, 1]))
        windows = window_parts(normed_v, row_shift, col_shift)
        addend = rel_bias[layer_index][:, table_index][None]
        local_out = attention(windows, windows, attn_in[layer_index, 0], addend, window_allowed(valid_mask, row_shift, col_shift))
        local_out = window_join(local_out, row_shift, col_shift)
        self_out = attention(normed_q[None], normed_q[None], attn_in[layer_index, 1], 0.0, self_allowed)[0]
        visual_x = visual_x + jnp.dot(local_out, attn_out[layer_index, 0], precision=HIGH)
        queries_x = queries_x + jnp.dot(self_out, attn_out[layer_index, 1], precision=HIGH)
        normed_v = low(layer_norm(visual_x, norm_scale[layer_index, 2], norm_shift[layer_index, 2]))
        normed_q = low(layer_norm(queries_x, norm_scale[layer_index, 3], norm_shift[layer_index, 3]))
        query_side = attention(normed_q[None], normed_v[None], attn_in[layer_index, 2], 0.0, to_patches)[0]
        visual_side = attention(normed_v[None], normed_q[None], attn_in[layer_index, 3], 0.0, to_question)[0]
        visual_x = visual_x + jnp.dot(visual_side, attn_out[layer_index, 3], precision=HIGH)
        queries_x = queries_x + jnp.dot(query_side, attn_out[layer_index, 2], precision=HIGH)
        normed_v = low(layer_norm(visual_x, norm_scale[layer_index, 4], norm_shift[layer_index, 4]))
        normed_q = low(layer_norm(queries_x, norm_scale[layer_index, 5], norm_shift[layer_index, 5]))
        visual_x = visual_x + feed_forward(normed_v, mlp_in[layer_index, 0], mlp_in_bias[layer_index, 0], mlp_out[layer_index, 0], mlp_out_bias[layer_index, 0])
        queries_x = queries_x + feed_forward(normed_q, mlp_in[layer_index, 1], mlp_in_bias[layer_index, 1], mlp_out[layer_index, 1], mlp_out_bias[layer_index, 1])
    return (visual_x, queries_x)

def reference(visual, queries, valid_windows, answer_start, shifts, norm_scale, norm_shift, attn_in, attn_out, rel_bias, mlp_in, mlp_in_bias, mlp_out, mlp_out_bias, grad_visual_out, grad_query_out):
    params = tuple((array_in.astype(jnp.float32) for array_in in (norm_scale, norm_shift, attn_in, attn_out, rel_bias, mlp_in, mlp_in_bias, mlp_out, mlp_out_bias)))

    def one_page(carry, page_data):
        visual_page, query_page, valid_page, answer_page, shift_page, grad_vpage, grad_qpage = page_data

        def run_layers(visual_x, queries_x, *weights):
            return forward(visual_x, queries_x, valid_page, answer_page, shift_page, *weights)
        outputs, pull_back = jax.vjp(run_layers, visual_page.astype(jnp.float32), query_page.astype(jnp.float32), *params)
        gradients = pull_back((grad_vpage, grad_qpage))
        carry = tuple((running + gradient for running, gradient in zip(carry, gradients[2:])))
        return (carry, (outputs[0].astype(jnp.bfloat16), outputs[1].astype(jnp.bfloat16), gradients[0], gradients[1]))
    zeros_init = tuple((jnp.zeros_like(param_array) for param_array in params))
    totals, stacked = lax.scan(one_page, zeros_init, (visual, queries, valid_windows, answer_start, shifts, grad_visual_out, grad_query_out))
    return (stacked[0], stacked[1], stacked[2], stacked[3], totals[0], totals[1], totals[2], totals[3], totals[4], totals[5], totals[6], totals[7], totals[8])
```

```python
import jax
import jax.numpy as jnp
from jax import lax
from jax.experimental import pallas as pl
from jax.experimental.pallas import tpu as pltpu
from jax.sharding import PartitionSpec as P

HDIM = 64
WIN = 12
SPAN = 2 * WIN - 1
EPS = 1e-05
NEG = -1000000000.0
OUT = -1e30
F32 = jnp.float32
BF16 = jnp.bfloat16
VMEM_LIMIT = 44 * 2**20


def nn(a, b):
    return lax.dot_general(a, b, (((1,), (0,)), ((), ())), preferred_element_type=F32)


def nt(a, b):
    return lax.dot_general(a, b, (((1,), (1,)), ((), ())), preferred_element_type=F32)


def tn(a, b):
    return lax.dot_general(a, b, (((0,), (0,)), ((), ())), preferred_element_type=F32)


def call(body, outs, scalars, args, flops=0, name=None):
    vmem = pl.BlockSpec(memory_space=pltpu.VMEM)
    smem = pl.BlockSpec(memory_space=pltpu.SMEM)
    moved = sum(a.size * a.dtype.itemsize for a in list(args) + list(outs))
    return pl.pallas_call(
        body,
        out_shape=tuple(outs),
        in_specs=[smem] * len(scalars) + [vmem] * len(args),
        out_specs=tuple(vmem for _ in outs),
        compiler_params=pltpu.CompilerParams(vmem_limit_bytes=VMEM_LIMIT),
        cost_estimate=pl.CostEstimate(flops=flops, bytes_accessed=moved, transcendentals=0),
        name=name,
    )(*scalars, *args)


def shaped(shape, dtype=BF16):
    return jax.ShapeDtypeStruct(shape, dtype)


class Sizes:
    def __init__(self, vis, qlen):
        self.vis, self.qlen = vis, qlen
        self.vh, self.qh = vis // 2, qlen // 2
        self.vp = -(-self.vh // 16) * 16
        self.half = self.vp + self.qh
        self.vquart, self.qquart = vis // 4, qlen // 4


def iota(shape, dim):
    return lax.broadcasted_iota(jnp.int32, shape, dim)


def div12(x):
    return (x * 171) >> 11


def patch_of(index, core, sz):
    second = (index >= sz.vp).astype(jnp.int32)
    row = index - second * sz.vp
    half = second + core - 2 * second * core
    patch = row + jnp.where(row >= sz.vquart, sz.vquart, 0) + half * sz.vquart
    return jnp.where(row < sz.vh, patch, -1)


def query_of(index, core, sz):
    second = (index >= sz.qh).astype(jnp.int32)
    row = index - second * sz.qh
    half = second + core - 2 * second * core
    return row + jnp.where(row >= sz.qquart, sz.qquart, 0) + half * sz.qquart


def window_permutation(sc, sz):
    core, down, right = sc[0], sc[2], sc[3]
    place = iota((sz.vis, sz.vp), 0)
    a = div12(place)
    b = place - a * WIN
    a = a + down
    b = b + right
    a = jnp.where(a >= WIN, a - WIN, a)
    b = jnp.where(b >= WIN, b - WIN, b)
    source = a * WIN + b
    stored = iota((sz.vis, sz.vp), 1)
    mine = (source == patch_of(stored, core, sz)).astype(F32).astype(BF16)
    theirs = (source == patch_of(stored + sz.vp, core, sz)).astype(F32).astype(BF16)
    return mine, theirs


def window_class(index, sc):
    a = div12(index)
    b = index - a * WIN
    return jnp.where(a >= WIN - sc[2], 2, 0) + jnp.where(b >= WIN - sc[3], 1, 0)


def window_mask(sc, sz):
    keys = window_class(iota((sz.vis, 1), 0), sc)
    asks = window_class(iota((1, sz.vis), 1), sc)
    keys = jnp.where(sc[4] > 0, keys, -1)
    return keys == asks


def self_mask(sc, sz):
    keys = query_of(iota((sz.qlen, 1), 0), sc[0], sz)
    asks = query_of(iota((1, sz.qlen), 1), sc[0], sz)
    return keys <= jnp.maximum(asks, sc[1] - 1)


def question_mask(sc, sz):
    return query_of(iota((sz.qlen, 1), 0), sc[0], sz) < sc[1]


def patch_pad(sc, sz):
    return patch_of(iota((2 * sz.vp, 1), 0), sc[0], sz) >= 0


def masked(scores, kind, sc, sz):
    if kind == "self":
        return jnp.where(self_mask(sc, sz), scores, NEG)
    if kind == "question":
        return jnp.where(question_mask(sc, sz), scores, NEG)
    if kind == "window":
        return jnp.where(window_mask(sc, sz), scores, NEG)
    real = patch_pad(sc, sz)
    return jnp.where(real & (sc[4] > 0), scores, jnp.where(real, NEG, OUT))


def allowed(kind, sc, sz):
    if kind == "self":
        return self_mask(sc, sz)
    if kind == "question":
        return question_mask(sc, sz)
    if kind == "window":
        return window_mask(sc, sz)
    return patch_pad(sc, sz) & (sc[4] > 0)


SCALE = HDIM**-0.5


def attend(q, k, v, addend, kind, sc, sz):
    scores = nt(k, q) * SCALE
    if addend is not None:
        scores = scores + addend
    scores = masked(scores, kind, sc, sz)
    top = jnp.max(scores, 0, keepdims=True)
    e = jnp.exp(scores - top)
    inv = 1.0 / jnp.sum(e, 0, keepdims=True)
    o_t = tn(v, (e * inv).astype(BF16))
    return o_t, top, inv


def attend_back(q, k, v, addend, kind, sc, sz, top, inv, do):
    scores = nt(k, q) * SCALE
    if addend is not None:
        scores = scores + addend
    scores = masked(scores, kind, sc, sz)
    p = jnp.exp(scores - top) * inv
    dv = nn(p.astype(BF16), do)
    dp = nt(v, do)
    ds = p * (dp - jnp.sum(p * dp, 0, keepdims=True))
    ds = jnp.where(allowed(kind, sc, sz), ds, 0.0).astype(BF16)
    dk = nn(ds, q) * SCALE
    dq = tn(k, ds) * SCALE
    return dq, dk, dv, ds


def head(ref, part, h, heads):
    start = (part * heads + h) * HDIM
    return ref[:, start : start + HDIM]


def run_heads(q_of, k_of, v_of, bias, kind, sc, sz, o_ref, st_ref, heads):
    outs = []
    for h in range(heads):
        o_t, top, inv = attend(
            q_of(h), k_of(h), v_of(h), None if bias is None else bias[h], kind, sc, sz
        )
        outs.append(o_t)
        st_ref[h : h + 1, :] = top
        st_ref[heads + h : heads + h + 1, :] = inv
    o_ref[...] = jnp.concatenate(outs, 0).T.astype(BF16)


def section1(sz, heads, sc, nm, nth, w0, w1, wo0, wo1, bias, pm, pt, nvw, qkvv, ov, stv, qkvq, oq, stq, ow):
    vp, qh = sz.vp, sz.qh
    mine, theirs = window_permutation(sc, sz)
    nv = (nn(mine, nm[0:vp, :]) + nn(theirs, nth[0:vp, :])).astype(BF16)
    nvw[...] = nv
    qkvv[...] = nt(nv, w0[...]).astype(BF16)
    run_heads(
        lambda h: head(qkvv, 0, h, heads),
        lambda h: head(qkvv, 1, h, heads),
        lambda h: head(qkvv, 2, h, heads),
        bias, "window", sc, sz, ow, stv, heads,
    )
    ov[0:vp, :] = tn(mine, ow[...]).astype(BF16)
    ov[vp : 2 * vp, :] = tn(theirs, ow[...]).astype(BF16)
    pm[0:vp, :] = nn(ov[0:vp, :], wo0[...]).astype(BF16)
    pt[0:vp, :] = nn(ov[vp : 2 * vp, :], wo0[...]).astype(BF16)
    qkvq[0:qh, :] = nt(nm[vp:, :], w1[...]).astype(BF16)
    qkvq[qh:, :] = nt(nth[vp:, :], w1[...]).astype(BF16)
    run_heads(
        lambda h: head(qkvq, 0, h, heads),
        lambda h: head(qkvq, 1, h, heads),
        lambda h: head(qkvq, 2, h, heads),
        None, "self", sc, sz, oq, stq, heads,
    )
    pm[vp:, :] = nn(oq[0:qh, :], wo1[...]).astype(BF16)
    pt[vp:, :] = nn(oq[qh:, :], wo1[...]).astype(BF16)


def section2(sz, heads, sc, nm, nth, w2, w3, wo2, wo3, pm, pt, qq, kvv, oq, stq, qv, kvq, ov, stv):
    vp, qh = sz.vp, sz.qh
    e = heads * HDIM
    for rows, ref in ((slice(0, qh), nm), (slice(qh, 2 * qh), nth)):
        x = ref[vp:, :]
        qq[rows, :] = nt(x, w2[0:e, :]).astype(BF16)
        kvq[rows, :] = nt(x, w3[e:, :]).astype(BF16)
    for rows, ref in ((slice(0, vp), nm), (slice(vp, 2 * vp), nth)):
        x = ref[0:vp, :]
        qv[rows, :] = nt(x, w3[0:e, :]).astype(BF16)
        kvv[rows, :] = nt(x, w2[e:, :]).astype(BF16)
    run_heads(
        lambda h: head(qq, 0, h, heads),
        lambda h: head(kvv, 0, h, heads),
        lambda h: head(kvv, 1, h, heads),
        None, "patch", sc, sz, oq, stq, heads,
    )
    run_heads(
        lambda h: head(qv, 0, h, heads),
        lambda h: head(kvq, 0, h, heads),
        lambda h: head(kvq, 1, h, heads),
        None, "question", sc, sz, ov, stv, heads,
    )
    pm[0:vp, :] = nn(ov[0:vp, :], wo3[...]).astype(BF16)
    pt[0:vp, :] = nn(ov[vp:, :], wo3[...]).astype(BF16)
    pm[vp:, :] = nn(oq[0:qh, :], wo2[...]).astype(BF16)
    pt[vp:, :] = nn(oq[qh:, :], wo2[...]).astype(BF16)


GELU_C = 0.7978845608028654
GELU_A = 0.044715


def section3(sz, nm, nth, wi, bi, wo, pm, pt, g, gp):
    vp, half = sz.vp, sz.half
    for ref, out, base in ((nm, pm, 0), (nth, pt, half)):
        for lo, hi, e in ((0, vp, 0), (vp, half, 1)):
            h = nn(ref[lo:hi, :], wi[e]) + bi[e : e + 1, :]
            h2 = h * h
            t = jnp.tanh(GELU_C * h * (1.0 + GELU_A * h2))
            half_t = 0.5 + 0.5 * t
            act = (h * half_t).astype(BF16)
            slope = half_t + (0.5 * GELU_C) * h * (1.0 - t * t) * (1.0 + 3.0 * GELU_A * h2)
            g[base + lo : base + hi, :] = act
            gp[base + lo : base + hi, :] = slope.astype(BF16)
            out[lo:hi, :] = nn(act, wo[e]).astype(BF16)


def section3_back(sz, dm, dt, wi, wo, gp, pm, pt, dh):
    vp, half = sz.vp, sz.half
    for ref, out, base in ((dm, pm, 0), (dt, pt, half)):
        for lo, hi, e in ((0, vp, 0), (vp, half, 1)):
            dg = nt(ref[lo:hi, :], wo[e])
            d = (dg * gp[base + lo : base + hi, :].astype(F32)).astype(BF16)
            dh[base + lo : base + hi, :] = d
            out[lo:hi, :] = nt(d, wi[e]).astype(BF16)


def back_heads(q_of, k_of, v_of, bias, kind, sc, sz, st, do_of, ds_ref, heads):
    dqs, dks, dvs = [], [], []
    for h in range(heads):
        dq, dk, dv, ds = attend_back(
            q_of(h), k_of(h), v_of(h), None if bias is None else bias[h], kind, sc, sz,
            st[h : h + 1, :], st[heads + h : heads + h + 1, :], do_of(h),
        )
        dqs.append(dq)
        dks.append(dk)
        dvs.append(dv)
        if ds_ref is not None:
            ds_ref[h] = ds
    dq = jnp.concatenate(dqs, 0).T.astype(BF16)
    dkv = jnp.concatenate(dks + dvs, 1).astype(BF16)
    return dq, dkv


def section2_back(sz, heads, sc, dm, dt, w2, w3, wo2, wo3, qq, kvv, stq, qv, kvq, stv, pm, pt, dqq, dkvv, dqv, dkvq, doq, dov):
    vp, qh = sz.vp, sz.qh
    e = heads * HDIM
    doq[0:qh, :] = nt(dm[vp:, :], wo2[...]).astype(BF16)
    doq[qh:, :] = nt(dt[vp:, :], wo2[...]).astype(BF16)
    dov[0:vp, :] = nt(dm[0:vp, :], wo3[...]).astype(BF16)
    dov[vp:, :] = nt(dt[0:vp, :], wo3[...]).astype(BF16)
    dq, dkv = back_heads(
        lambda h: head(qq, 0, h, heads),
        lambda h: head(kvv, 0, h, heads),
        lambda h: head(kvv, 1, h, heads),
        None, "patch", sc, sz, stq, lambda h: head(doq, 0, h, heads), None, heads,
    )
    dqq[...] = dq
    dkvv[...] = dkv
    dq, dkv = back_heads(
        lambda h: head(qv, 0, h, heads),
        lambda h: head(kvq, 0, h, heads),
        lambda h: head(kvq, 1, h, heads),
        None, "question", sc, sz, stv, lambda h: head(dov, 0, h, heads), None, heads,
    )
    dqv[...] = dq
    dkvq[...] = dkv
    for out, qrow, vrow in ((pm, slice(0, qh), slice(0, vp)), (pt, slice(qh, 2 * qh), slice(vp, 2 * vp))):
        out[vp:, :] = (nn(dqq[qrow, :], w2[0:e, :]) + nn(dkvq[qrow, :], w3[e:, :])).astype(BF16)
        out[0:vp, :] = (nn(dqv[vrow, :], w3[0:e, :]) + nn(dkvv[vrow, :], w2[e:, :])).astype(BF16)


def section1_back(sz, heads, sc, dm, dt, w0, w1, wo0, wo1, bias, qkvv, stv, qkvq, stq, pm, pt, dqkvv, dqkvq, ds, doq, dov):
    vp, qh = sz.vp, sz.qh
    e = heads * HDIM
    mine, theirs = window_permutation(sc, sz)
    do_m = nt(dm[0:vp, :], wo0[...]).astype(BF16)
    do_t = nt(dt[0:vp, :], wo0[...]).astype(BF16)
    dov[...] = (nn(mine, do_m) + nn(theirs, do_t)).astype(BF16)
    dq, dkv = back_heads(
        lambda h: head(qkvv, 0, h, heads),
        lambda h: head(qkvv, 1, h, heads),
        lambda h: head(qkvv, 2, h, heads),
        bias, "window", sc, sz, stv, lambda h: head(dov, 0, h, heads), ds, heads,
    )
    dqkvv[:, 0:e] = dq
    dqkvv[:, e:] = dkv
    dn = nn(dqkvv[...], w0[...]).astype(BF16)
    pm[0:vp, :] = tn(mine, dn).astype(BF16)
    pt[0:vp, :] = tn(theirs, dn).astype(BF16)
    doq[0:qh, :] = nt(dm[vp:, :], wo1[...]).astype(BF16)
    doq[qh:, :] = nt(dt[vp:, :], wo1[...]).astype(BF16)
    dq, dkv = back_heads(
        lambda h: head(qkvq, 0, h, heads),
        lambda h: head(qkvq, 1, h, heads),
        lambda h: head(qkvq, 2, h, heads),
        None, "self", sc, sz, stq, lambda h: head(doq, 0, h, heads), None, heads,
    )
    dqkvq[:, 0:e] = dq
    dqkvq[:, e:] = dkv
    pm[vp:, :] = nn(dqkvq[0:qh, :], w1[...]).astype(BF16)
    pt[vp:, :] = nn(dqkvq[qh:, :], w1[...]).astype(BF16)


def store_blocks(sc, out, col, value):
    value = value.astype(BF16)
    blocks, rows = out.shape[0], out.shape[1]
    width = value.shape[1]
    ring = blocks // 2
    for d in range(blocks):
        if blocks == 1:
            slot = 0
        else:
            flip = (d % 2) + sc[5] - 2 * (d % 2) * sc[5]
            away = d // 2 - sc[6]
            away = jnp.where(away < 0, away + ring, away)
            slot = flip * ring + away
        out[slot, :, col : col + width] = value[d * rows : (d + 1) * rows, :]


def section3_weights(sz, sc, nm, nth, dm, dt, g, dh, out, db):
    vp, half = sz.vp, sz.half
    hid = g.shape[1]
    for e, lo, hi in ((0, 0, vp), (1, vp, half)):
        store_blocks(sc, out, e * hid, tn(nm[lo:hi, :], dh[lo:hi, :]) + tn(nth[lo:hi, :], dh[half + lo : half + hi, :]))
        store_blocks(
            sc, out, (2 + e) * hid, tn(dm[lo:hi, :], g[lo:hi, :]) + tn(dt[lo:hi, :], g[half + lo : half + hi, :])
        )
        db[e : e + 1, :] = jnp.sum(dh[lo:hi, :].astype(F32), 0, keepdims=True) + jnp.sum(
            dh[half + lo : half + hi, :].astype(F32), 0, keepdims=True
        )


def section2_weights(sz, heads, sc, nm, nth, dm, dt, dqq, dkvv, dqv, dkvq, oq, ov, out):
    vp, qh = sz.vp, sz.qh
    e = heads * HDIM

    def both(a_m, a_t, b, cut, lo, hi):
        return tn(a_m[lo:hi, :], b[0:cut, :]) + tn(a_t[lo:hi, :], b[cut:, :])

    store_blocks(sc, out, 0, both(nm, nth, dqq, qh, vp, sz.half))
    store_blocks(sc, out, e, both(nm, nth, dkvv, vp, 0, vp))
    store_blocks(sc, out, 3 * e, both(nm, nth, dqv, vp, 0, vp))
    store_blocks(sc, out, 4 * e, both(nm, nth, dkvq, qh, vp, sz.half))
    store_blocks(sc, out, 6 * e, both(dm, dt, oq, qh, vp, sz.half))
    store_blocks(sc, out, 7 * e, both(dm, dt, ov, vp, 0, vp))


def section1_weights(sz, heads, sc, nm, nth, dm, dt, nvw, dqkvv, dqkvq, oq, ov, out):
    vp, qh = sz.vp, sz.qh
    e = heads * HDIM

    def both(a_m, a_t, b, cut, lo, hi):
        return tn(a_m[lo:hi, :], b[0:cut, :]) + tn(a_t[lo:hi, :], b[cut:, :])

    store_blocks(sc, out, 0, tn(nvw[...], dqkvv[...]))
    store_blocks(sc, out, 3 * e, both(nm, nth, dqkvq, qh, vp, sz.half))
    store_blocks(sc, out, 6 * e, both(dm, dt, ov, vp, 0, vp))
    store_blocks(sc, out, 7 * e, both(dm, dt, oq, qh, vp, sz.half))


def norm_rows(x):
    center = x - jnp.mean(x, -1, keepdims=True)
    inv = lax.rsqrt(jnp.mean(center * center, -1, keepdims=True) + EPS)
    return center * inv, inv


def first_norm(sz, x, scale, shift, n):
    for lo, hi, e in ((0, sz.vp, 0), (sz.vp, sz.half, 1)):
        n[lo:hi, :] = (norm_rows(x[lo:hi, :])[0] * scale[e : e + 1, :] + shift[e : e + 1, :]).astype(BF16)


def add_norm(sz, x, a, b, extra, scale, shift, y, n):
    for lo, hi, e in ((0, sz.vp, 0), (sz.vp, sz.half, 1)):
        value = x[lo:hi, :] + (a[lo:hi, :].astype(F32) + b[lo:hi, :].astype(F32)) + extra[e : e + 1, :]
        y[lo:hi, :] = value
        n[lo:hi, :] = (norm_rows(value)[0] * scale[e : e + 1, :] + shift[e : e + 1, :]).astype(BF16)


def norm_back(sz, d, a, b, x, scale, out, dy, sums):
    for lo, hi, e in ((0, sz.vp, 0), (sz.vp, sz.half, 1)):
        dn = a[lo:hi, :].astype(F32) + b[lo:hi, :].astype(F32)
        unit, inv = norm_rows(x[lo:hi, :])
        du = dn * scale[e : e + 1, :]
        dnu = dn * unit
        dx = inv * (
            du
            - jnp.mean(du, -1, keepdims=True)
            - unit * jnp.mean(du * unit, -1, keepdims=True)
        )
        value = d[lo:hi, :] + dx
        out[lo:hi, :] = value
        dy[lo:hi, :] = value.astype(BF16)
        sums[e : e + 1, :] = jnp.sum(dnu, 0, keepdims=True)
        sums[2 + e : 3 + e, :] = jnp.sum(dn, 0, keepdims=True)
        sums[4 + e : 5 + e, :] = jnp.sum(value, 0, keepdims=True)


def table_bias(table):
    heads = table.shape[0]
    grid = table.reshape(heads, SPAN, SPAN)
    cols = jnp.stack([grid[:, :, WIN - 1 - u : SPAN - u] for u in range(WIN)], 1)
    cols = cols.reshape(heads, WIN, SPAN * WIN)
    first = [(WIN - 1 - u) * WIN for u in range(WIN)]
    rows = jnp.stack([cols[:, :, f : f + WIN * WIN] for f in first], 1)
    return rows.reshape(heads, WIN * WIN, WIN * WIN)


def table_grad(ds):
    heads = ds.shape[0]
    rows = ds.astype(F32).reshape(heads, WIN, WIN, WIN * WIN)
    total = SPAN * WIN
    cols = sum(
        jnp.pad(rows[:, u], ((0, 0), (0, 0), ((WIN - 1 - u) * WIN, total - (WIN - 1 - u) * WIN - WIN * WIN)))
        for u in range(WIN)
    )
    cols = cols.reshape(heads, WIN, SPAN, WIN)
    grid = sum(jnp.pad(cols[:, u], ((0, 0), (0, 0), (WIN - 1 - u, u))) for u in range(WIN))
    return grid.reshape(heads, SPAN * SPAN)


def on_device(
    dp_size,
    visual,
    queries,
    valid_windows,
    answer_start,
    shifts,
    norm_scale,
    norm_shift,
    attn_in,
    attn_out,
    rel_bias,
    mlp_in,
    mlp_in_bias,
    mlp_out,
    mlp_out_bias,
    grad_visual_out,
    grad_query_out,
):
    layers, width = attn_in.shape[0], attn_in.shape[2]
    edev = attn_in.shape[4]
    heads = edev // HDIM
    hid = mlp_in.shape[3]
    sz = Sizes(4 * visual.shape[1], 4 * queries.shape[1])
    half, vp, qh = sz.half, sz.vp, sz.qh
    vq, qq_ = sz.vquart, sz.qquart
    t_index = lax.axis_index("tensor")
    d_index = lax.axis_index("dp")
    core, chip = t_index % 2, t_index // 2
    swap = [(i, i ^ 1) for i in range(4)]
    cross = [(i, i ^ 2) for i in range(4)]
    block_rows = width // dp_size
    ring_ok = dp_size % 2 == 0 and block_rows % 16 == 0
    blocks = dp_size if ring_ok else 1
    ring = dp_size // 2

    def scalars(layer):
        on = layer % 2
        return jnp.stack(
            [
                core,
                answer_start[0],
                shifts[0, 0] * on,
                shifts[0, 1] * on,
                valid_windows[0, 0],
                d_index % 2,
                d_index // 2,
                0,
            ]
        ).astype(jnp.int32)

    w_in = attn_in.transpose(0, 1, 3, 4, 2).reshape(layers, 4, 3 * edev, width)

    def to_half(own_v, own_q):
        packed = jnp.concatenate([own_v, own_q], 0)
        other = lax.ppermute(packed, "tensor", cross)
        first = jnp.where(chip == 0, packed, other)
        second = jnp.where(chip == 0, other, packed)
        pad = jnp.zeros((vp - 2 * vq, width), packed.dtype)
        return jnp.concatenate([first[:vq], second[:vq], pad, first[vq:], second[vq:]], 0)

    def own_rows(rows):
        v = jnp.where(chip == 0, rows[0:vq], rows[vq : 2 * vq])
        q = jnp.where(chip == 0, rows[vp : vp + qq_], rows[vp + qq_ :])
        return v, q

    def total(mine, theirs):
        got = lax.ppermute(theirs, "tensor", swap)
        kept = (mine.astype(F32) + got.astype(F32)).astype(BF16)
        return kept, lax.ppermute(kept, "tensor", cross)

    stream = to_half(visual[0], queries[0]).astype(F32)
    grad_rounded = [lax.reduce_precision(g[0], 8, 7) for g in (grad_visual_out, grad_query_out)]
    scal = [scalars(layer) for layer in range(layers)]
    biases = [table_bias(rel_bias[layer]) for layer in range(layers)]
    rows_bf = shaped((half, width))
    rows_f = shaped((half, width), F32)
    mac = 2 * half * width

    def pair(x):
        return x, lax.ppermute(x, "tensor", swap)

    zero_bias = jnp.zeros((2, width), F32)
    (normed,) = call(
        lambda *r: first_norm(sz, *r),
        [rows_bf],
        [],
        [stream, norm_scale[0, 0:2], norm_shift[0, 0:2]],
        name="norm",
    )
    saved = []
    for layer in range(layers):
        sc = scal[layer]
        nm, nth = pair(normed)
        part = call(
            lambda *r: section1(sz, heads, *r),
            [
                rows_bf,
                rows_bf,
                shaped((sz.vis, width)),
                shaped((sz.vis, 3 * edev)),
                shaped((2 * vp, edev)),
                shaped((8, sz.vis), F32),
                shaped((sz.qlen, 3 * edev)),
                shaped((sz.qlen, edev)),
                shaped((8, sz.qlen), F32),
                shaped((sz.vis, edev)),
            ],
            [sc],
            [nm, nth, w_in[layer, 0], w_in[layer, 1], attn_out[layer, 0], attn_out[layer, 1], biases[layer]],
            flops=mac * 4 * edev * 2 + 8 * heads * HDIM * sz.qlen * sz.qlen,
            name="section1",
        )
        kept1 = (stream, nm, nth) + tuple(part[2:9])
        a, b = total(part[0], part[1])
        stream, normed = call(
            lambda *r: add_norm(sz, *r),
            [rows_f, rows_bf],
            [],
            [stream, a, b, zero_bias, norm_scale[layer, 2:4], norm_shift[layer, 2:4]],
            name="norm",
        )
        nm, nth = pair(normed)
        part = call(
            lambda *r: section2(sz, heads, *r),
            [
                rows_bf,
                rows_bf,
                shaped((sz.qlen, edev)),
                shaped((2 * vp, 2 * edev)),
                shaped((sz.qlen, edev)),
                shaped((8, sz.qlen), F32),
                shaped((2 * vp, edev)),
                shaped((sz.qlen, 2 * edev)),
                shaped((2 * vp, edev)),
                shaped((8, 2 * vp), F32),
            ],
            [sc],
            [nm, nth, w_in[layer, 2], w_in[layer, 3], attn_out[layer, 2], attn_out[layer, 3]],
            flops=mac * 4 * edev * 2,
            name="section2",
        )
        kept2 = (stream, nm, nth) + tuple(part[2:])
        a, b = total(part[0], part[1])
        stream, normed = call(
            lambda *r: add_norm(sz, *r),
            [rows_f, rows_bf],
            [],
            [stream, a, b, zero_bias, norm_scale[layer, 4:6], norm_shift[layer, 4:6]],
            name="norm",
        )
        nm, nth = pair(normed)
        part = call(
            lambda *r: section3(sz, *r),
            [rows_bf, rows_bf, shaped((2 * half, hid)), shaped((2 * half, hid))],
            [],
            [nm, nth, mlp_in[layer], mlp_in_bias[layer], mlp_out[layer]],
            flops=mac * hid * 4,
            name="section3",
        )
        kept3 = (stream, nm, nth) + tuple(part[2:])
        saved.append((kept1, kept2, kept3))
        a, b = total(part[0], part[1])
        if layer + 1 < layers:
            stream, normed = call(
                lambda *r: add_norm(sz, *r),
                [rows_f, rows_bf],
                [],
                [stream, a, b, mlp_out_bias[layer], norm_scale[layer + 1, 0:2], norm_shift[layer + 1, 0:2]],
                name="norm",
            )
        else:
            added = stream + (a.astype(F32) + b.astype(F32))
            out_v, out_q = own_rows(added)
            out_v = (out_v + mlp_out_bias[layer, 0]).astype(BF16)
            out_q = (out_q + mlp_out_bias[layer, 1]).astype(BF16)

    dy = to_half(*(g.astype(BF16) for g in grad_rounded))
    grad = dy.astype(F32)
    bias_sums = jnp.stack([jnp.sum(grad[:vp], 0), jnp.sum(grad[vp:], 0)])

    def reduce_weights(parts):
        if not ring_ok:
            return lax.psum_scatter(parts[0].astype(F32), "dp", scatter_dimension=0, tiled=True)
        flip = [(i, i ^ 1) for i in range(dp_size)]
        onward = [(i, (i + 2) % dp_size) for i in range(dp_size)]
        got = lax.ppermute(parts[ring:], "dp", flip)
        if ring == 1:
            return parts[0].astype(F32) + got[0].astype(F32)
        moving = parts[ring - 1].astype(F32) + got[ring - 1].astype(F32)
        for away in reversed(range(ring - 1)):
            moving = lax.ppermute(moving.astype(BF16), "dp", onward).astype(F32)
            moving = moving + (parts[away].astype(F32) + got[away].astype(F32))
        return moving

    def close(grad, a, b, kept, layer, first):
        return call(
            lambda *r: norm_back(sz, *r),
            [rows_f, rows_bf, shaped((8, width), F32)],
            [],
            [grad, a, b, kept[0], norm_scale[layer, first : first + 2]],
            name="norm_back",
        )

    grads = [None] * layers
    for layer in reversed(range(layers)):
        sc = scal[layer]
        kept1, kept2, kept3 = saved[layer]
        dm, dt = pair(dy)
        _, nm, nth, act, slope = kept3
        pm, pt, dh = call(
            lambda *r: section3_back(sz, *r),
            [rows_bf, rows_bf, shaped((2 * half, hid))],
            [],
            [dm, dt, mlp_in[layer], mlp_out[layer], slope],
            flops=mac * hid * 4,
            name="section3_back",
        )
        a, b = total(pm, pt)
        w3, db = call(
            lambda *r: section3_weights(sz, *r),
            [shaped((blocks, width // blocks, 4 * hid)), shaped((2, hid), F32)],
            [sc],
            [nm, nth, dm, dt, act, dh],
            flops=mac * hid * 4,
            name="section3_weights",
        )
        out_bias_sums = bias_sums
        grad, dy, sums3 = close(grad, a, b, kept3, layer, 4)

        dm, dt = pair(dy)
        _, nm, nth, qq, kvv, oq, stq, qv, kvq, ov, stv = kept2
        part = call(
            lambda *r: section2_back(sz, heads, *r),
            [
                rows_bf,
                rows_bf,
                shaped((sz.qlen, edev)),
                shaped((2 * vp, 2 * edev)),
                shaped((2 * vp, edev)),
                shaped((sz.qlen, 2 * edev)),
                shaped((sz.qlen, edev)),
                shaped((2 * vp, edev)),
            ],
            [sc],
            [dm, dt, w_in[layer, 2], w_in[layer, 3], attn_out[layer, 2], attn_out[layer, 3], qq, kvv, stq, qv, kvq, stv],
            flops=mac * 4 * edev * 2,
            name="section2_back",
        )
        a, b = total(part[0], part[1])
        (w2,) = call(
            lambda *r: section2_weights(sz, heads, *r),
            [shaped((blocks, width // blocks, 8 * edev))],
            [sc],
            [nm, nth, dm, dt, part[2], part[3], part[4], part[5], oq, ov],
            flops=mac * 4 * edev * 2,
            name="section2_weights",
        )
        grad, dy, sums2 = close(grad, a, b, kept2, layer, 2)

        dm, dt = pair(dy)
        _, nm, nth, nvw, qkvv, ov, stv, qkvq, oq, stq = kept1
        part = call(
            lambda *r: section1_back(sz, heads, *r),
            [
                rows_bf,
                rows_bf,
                shaped((sz.vis, 3 * edev)),
                shaped((sz.qlen, 3 * edev)),
                shaped((heads, sz.vis, sz.vis)),
                shaped((sz.qlen, edev)),
                shaped((sz.vis, edev)),
            ],
            [sc],
            [
                dm, dt, w_in[layer, 0], w_in[layer, 1], attn_out[layer, 0], attn_out[layer, 1],
                biases[layer], qkvv, stv, qkvq, stq,
            ],
            flops=mac * 4 * edev * 2 + 20 * heads * HDIM * sz.qlen * sz.qlen,
            name="section1_back",
        )
        a, b = total(part[0], part[1])
        (w1,) = call(
            lambda *r: section1_weights(sz, heads, *r),
            [shaped((blocks, width // blocks, 8 * edev))],
            [sc],
            [nm, nth, dm, dt, nvw, part[2], part[3], oq, ov],
            flops=mac * 4 * edev * 2,
            name="section1_weights",
        )
        table = table_grad(part[4])
        grad, dy, sums1 = close(grad, a, b, kept1, layer, 0)
        bias_sums = sums1[4:6]

        w3, w2, w1 = reduce_weights(w3), reduce_weights(w2), reduce_weights(w1)
        grads[layer] = (w3, w2, w1, db, table, sums1, sums2, sums3, out_bias_sums)

    rest_v = grad_visual_out[0] - grad_rounded[0]
    rest_q = grad_query_out[0] - grad_rounded[1]
    own_v, own_q = own_rows(grad)
    grad_v, grad_q = own_v + rest_v, own_q + rest_q

    def summed(x, axis, size, bits):
        for bit in bits:
            x = x + lax.ppermute(x, axis, [(i, i ^ bit) for i in range(size)])
        return x

    dp_bits = [1 << k for k in range(dp_size.bit_length() - 1)]
    norms = jnp.stack(
        [
            jnp.concatenate([g[5][0:4], g[6][0:4], g[7][0:4], g[8]], 0)
            for g in grads
        ]
    )
    norms = summed(norms, "tensor", 4, [1])
    local = jnp.concatenate([jnp.concatenate([g[3].reshape(-1), g[4].reshape(-1)]) for g in grads])
    packed = jnp.concatenate([norms.reshape(-1), local])
    packed = summed(packed, "dp", dp_size, dp_bits)
    norms = packed[: norms.size].reshape(norms.shape)
    local = packed[norms.size :].reshape(layers, -1)
    scale_total = jnp.concatenate([norms[:, 0:2], norms[:, 4:6], norms[:, 8:10]], 1)
    shift_total = jnp.concatenate([norms[:, 2:4], norms[:, 6:8], norms[:, 10:12]], 1)
    out_bias_total = norms[:, 12:14]
    in_bias_total = local[:, : 2 * hid].reshape(layers, 2, hid)
    rel_total = local[:, 2 * hid :].reshape(layers, heads, SPAN * SPAN)

    def projections(w):
        return [w[:, k * edev : (k + 1) * edev] for k in range(8)]

    d_in, d_out, d_up, d_down = [], [], [], []
    for g in grads:
        one, two = projections(g[2]), projections(g[1])
        d_in.append(
            jnp.stack([jnp.stack(p, 0) for p in (one[0:3], one[3:6], two[0:3], two[3:6])])
        )
        d_out.append(jnp.stack([one[6].T, one[7].T, two[6].T, two[7].T]))
        d_up.append(jnp.stack([g[0][:, 0:hid], g[0][:, hid : 2 * hid]]))
        d_down.append(jnp.stack([g[0][:, 2 * hid : 3 * hid], g[0][:, 3 * hid :]]))
    return (
        out_v[None],
        out_q[None],
        grad_v[None],
        grad_q[None],
        scale_total,
        shift_total,
        jnp.stack(d_in).transpose(0, 1, 3, 2, 4),
        jnp.stack(d_out),
        rel_total,
        jnp.stack(d_up),
        in_bias_total,
        jnp.stack(d_down).transpose(0, 1, 3, 2),
        out_bias_total,
    )


def solution(mesh):
    dp_size = mesh.shape["dp"]
    return jax.shard_map(
        lambda *args: on_device(dp_size, *args),
        mesh=mesh,
        in_specs=(
            P("dp", "tensor", None),
            P("dp", "tensor", None),
            P("dp", None),
            P("dp"),
            P("dp", None),
            P(),
            P(),
            P(None, None, None, None, "tensor"),
            P(None, None, "tensor", None),
            P(None, "tensor", None),
            P(None, None, None, "tensor"),
            P(None, None, "tensor"),
            P(None, None, "tensor", None),
            P(),
            P("dp", "tensor", None),
            P("dp", "tensor", None),
        ),
        out_specs=(
            P("dp", "tensor", None),
            P("dp", "tensor", None),
            P("dp", "tensor", None),
            P("dp", "tensor", None),
            P(),
            P(),
            P(None, None, "dp", None, "tensor"),
            P(None, None, "tensor", "dp"),
            P(None, "tensor", None),
            P(None, None, "dp", "tensor"),
            P(None, None, "tensor"),
            P(None, None, "tensor", "dp"),
            P(),
        ),
        check_vma=False,
    )
```

```python
import jax
import jax.numpy as jnp
from jax import lax
from jax.experimental import pallas as pl
from jax.experimental.pallas import tpu as pltpu
from jax.sharding import PartitionSpec as P

HDIM = 64
WIN = 12
SPAN = 2 * WIN - 1
EPS = 1e-05
NEG = -1000000000.0
OUT = -1e30
F32 = jnp.float32
BF16 = jnp.bfloat16
VMEM_LIMIT = 20 * 2**20


def nn(a, b):
    return lax.dot_general(a, b, (((1,), (0,)), ((), ())), preferred_element_type=F32)


def nt(a, b):
    return lax.dot_general(a, b, (((1,), (1,)), ((), ())), preferred_element_type=F32)


def tn(a, b):
    return lax.dot_general(a, b, (((0,), (0,)), ((), ())), preferred_element_type=F32)


class Part:
    def __init__(self, array, *lead):
        self.array, self.lead = array, lead
        self.rest = array.shape[len(lead) :]
        self.dtype = array.dtype
        self.size = 1
        for n in self.rest:
            self.size *= n


class Arriving:
    def __init__(self, ref, copy):
        self.ref, self.copy, self.shape = ref, copy, ref.shape

    def __getitem__(self, at):
        if self.copy is not None:
            self.copy.wait()
            self.copy = None
        return self.ref[at]


def call(body, outs, scalars, args, flops=0, name=None, scratch=()):
    vmem = pl.BlockSpec(memory_space=pltpu.VMEM)
    smem = pl.BlockSpec(memory_space=pltpu.SMEM)
    anywhere = pl.BlockSpec(memory_space=pltpu.HBM)
    moved = sum(a.size * a.dtype.itemsize for a in list(args) + list(outs))
    parts = [i for i, a in enumerate(args) if isinstance(a, Part)]
    specs = [anywhere if isinstance(a, Part) else vmem for a in args]
    arrays = [a.array if isinstance(a, Part) else a for a in args]
    landing = [pltpu.VMEM(args[i].rest, args[i].dtype) for i in parts]
    if parts:
        landing.append(pltpu.SemaphoreType.DMA((len(parts),)))
    first, end = len(scalars), len(scalars) + len(args) + len(outs) + len(scratch)

    def wrapped(*refs):
        refs = list(refs)
        buffers = refs[end:]
        coming = []
        for k, i in enumerate(parts):
            source = refs[first + i]
            if args[i].lead:
                source = source.at[args[i].lead]
            copy = pltpu.make_async_copy(source, buffers[k], buffers[-1].at[k])
            copy.start()
            coming.append(Arriving(buffers[k], copy))
            refs[first + i] = coming[-1]
        body(*refs[:end])
        for piece in coming:
            if piece.copy is not None:
                piece.copy.wait()

    return pl.pallas_call(
        wrapped,
        out_shape=tuple(outs),
        in_specs=[smem] * len(scalars) + specs,
        out_specs=tuple(vmem for _ in outs),
        scratch_shapes=list(scratch) + landing,
        compiler_params=pltpu.CompilerParams(vmem_limit_bytes=VMEM_LIMIT),
        cost_estimate=pl.CostEstimate(flops=1, bytes_accessed=1, transcendentals=0),
        name=name,
    )(*scalars, *arrays)


def tie(*groups):
    return lax.optimization_barrier(groups)


def shaped(shape, dtype=BF16):
    return jax.ShapeDtypeStruct(shape, dtype)


class Sizes:
    def __init__(self, vis, qlen):
        self.vis, self.qlen = vis, qlen
        self.qh = qlen // 2
        self.vquart, self.qquart = vis // 4, qlen // 4
        self.vpiece = -(-self.vquart // 8) * 8
        self.vp = 2 * self.vpiece
        self.piece = self.vpiece + self.qquart
        self.half = 2 * self.piece


def iota(shape, dim):
    return lax.broadcasted_iota(jnp.int32, shape, dim)


def div12(x):
    return (x * 171) >> 11


def patch_of(index, core, sz):
    second = (index >= sz.vp).astype(jnp.int32)
    row = index - second * sz.vp
    half = second + core - 2 * second * core
    late = (row >= sz.vpiece).astype(jnp.int32)
    row = row - late * sz.vpiece
    return jnp.where(row < sz.vquart, row + (2 * late + half) * sz.vquart, -1)


def query_of(index, core, sz):
    second = (index >= sz.qh).astype(jnp.int32)
    row = index - second * sz.qh
    half = second + core - 2 * second * core
    return row + jnp.where(row >= sz.qquart, sz.qquart, 0) + half * sz.qquart


def window_permutation(sc, sz):
    core, down, right = sc[0], sc[2], sc[3]
    place = iota((sz.vis, sz.vp), 0)
    a = div12(place)
    b = place - a * WIN
    a = a + down
    b = b + right
    a = jnp.where(a >= WIN, a - WIN, a)
    b = jnp.where(b >= WIN, b - WIN, b)
    source = a * WIN + b
    stored = iota((sz.vis, sz.vp), 1)
    mine = (source == patch_of(stored, core, sz)).astype(F32).astype(BF16)
    theirs = (source == patch_of(stored + sz.vp, core, sz)).astype(F32).astype(BF16)
    return mine, theirs


def window_class(index, sc):
    a = div12(index)
    b = index - a * WIN
    return jnp.where(a >= WIN - sc[2], 2, 0) + jnp.where(b >= WIN - sc[3], 1, 0)


def window_mask(sc, sz):
    keys = window_class(iota((sz.vis, 1), 0), sc)
    asks = window_class(iota((1, sz.vis), 1), sc)
    keys = jnp.where(sc[4] > 0, keys, -1)
    return keys == asks


def self_mask(sc, sz):
    keys = query_of(iota((sz.qlen, 1), 0), sc[0], sz)
    asks = query_of(iota((1, sz.qlen), 1), sc[0], sz)
    return keys <= jnp.maximum(asks, sc[1] - 1)


def question_mask(sc, sz):
    return query_of(iota((sz.qlen, 1), 0), sc[0], sz) < sc[1]


def patch_pad(sc, sz):
    return patch_of(iota((2 * sz.vp, 1), 0), sc[0], sz) >= 0


def masked(scores, kind, sc, sz):
    if kind == "self":
        return jnp.where(self_mask(sc, sz), scores, NEG)
    if kind == "question":
        return jnp.where(question_mask(sc, sz), scores, NEG)
    if kind == "window":
        return jnp.where(window_mask(sc, sz), scores, NEG)
    real = patch_pad(sc, sz)
    return jnp.where(real & (sc[4] > 0), scores, jnp.where(real, NEG, OUT))


def allowed(kind, sc, sz):
    if kind == "self":
        return self_mask(sc, sz)
    if kind == "question":
        return question_mask(sc, sz)
    if kind == "window":
        return window_mask(sc, sz)
    return patch_pad(sc, sz) & (sc[4] > 0)


SCALE = HDIM**-0.5


def attend(q, k, v, addend, kind, sc, sz):
    scores = nt(k, q) * SCALE
    if addend is not None:
        scores = scores + addend
    scores = masked(scores, kind, sc, sz)
    top = jnp.max(scores, 0, keepdims=True)
    e = jnp.exp(scores - top)
    inv = 1.0 / jnp.sum(e, 0, keepdims=True)
    o_t = tn(v, (e * inv).astype(BF16))
    return o_t, top, inv


def attend_back(q, k, v, addend, kind, sc, sz, top, inv, do):
    scores = nt(k, q) * SCALE
    if addend is not None:
        scores = scores + addend
    scores = masked(scores, kind, sc, sz)
    p = jnp.exp(scores - top) * inv
    dv = nn(p.astype(BF16), do)
    dp = nt(v, do)
    ds = p * (dp - jnp.sum(p * dp, 0, keepdims=True))
    ds = jnp.where(allowed(kind, sc, sz), ds, 0.0).astype(BF16)
    dk = nn(ds, q) * SCALE
    dq = tn(k, ds) * SCALE
    return dq, dk, dv, ds


def head(ref, part, h, heads):
    start = (part * heads + h) * HDIM
    return ref[:, start : start + HDIM]


def run_heads(q_of, k_of, v_of, bias, kind, sc, sz, o_ref, st_ref, heads):
    outs = []
    for h in range(heads):
        o_t, top, inv = attend(
            q_of(h), k_of(h), v_of(h), None if bias is None else bias[h], kind, sc, sz
        )
        outs.append(o_t)
        st_ref[h : h + 1, :] = top
        st_ref[heads + h : heads + h + 1, :] = inv
    o_ref[...] = jnp.concatenate(outs, 0).T.astype(BF16)


def section1(sz, heads, sc, nm, nth, w0, w1, wo0, wo1, bias, pm, pt, nvw, qkvv, ov, stv, qkvq, oq, stq, ow):
    vp, qh = sz.vp, sz.qh
    mine, theirs = window_permutation(sc, sz)
    nv = (nn(mine, nm[0:vp, :]) + nn(theirs, nth[0:vp, :])).astype(BF16)
    nvw[...] = nv
    qkvv[...] = nt(nv, w0[...]).astype(BF16)
    run_heads(
        lambda h: head(qkvv, 0, h, heads),
        lambda h: head(qkvv, 1, h, heads),
        lambda h: head(qkvv, 2, h, heads),
        bias, "window", sc, sz, ow, stv, heads,
    )
    ov[0:vp, :] = tn(mine, ow[...]).astype(BF16)
    ov[vp : 2 * vp, :] = tn(theirs, ow[...]).astype(BF16)
    pm[0:vp, :] = nn(ov[0:vp, :], wo0[...]).astype(BF16)
    pt[0:vp, :] = nn(ov[vp : 2 * vp, :], wo0[...]).astype(BF16)
    qkvq[0:qh, :] = nt(nm[vp:, :], w1[...]).astype(BF16)
    qkvq[qh:, :] = nt(nth[vp:, :], w1[...]).astype(BF16)
    run_heads(
        lambda h: head(qkvq, 0, h, heads),
        lambda h: head(qkvq, 1, h, heads),
        lambda h: head(qkvq, 2, h, heads),
        None, "self", sc, sz, oq, stq, heads,
    )
    pm[vp:, :] = nn(oq[0:qh, :], wo1[...]).astype(BF16)
    pt[vp:, :] = nn(oq[qh:, :], wo1[...]).astype(BF16)


def section2(sz, heads, sc, nm, nth, w2, w3, wo2, wo3, pm, pt, qq, kvv, oq, stq, qv, kvq, ov, stv):
    vp, qh = sz.vp, sz.qh
    e = heads * HDIM
    for rows, ref in ((slice(0, qh), nm), (slice(qh, 2 * qh), nth)):
        x = ref[vp:, :]
        qq[rows, :] = nt(x, w2[0:e, :]).astype(BF16)
        kvq[rows, :] = nt(x, w3[e:, :]).astype(BF16)
    for rows, ref in ((slice(0, vp), nm), (slice(vp, 2 * vp), nth)):
        x = ref[0:vp, :]
        qv[rows, :] = nt(x, w3[0:e, :]).astype(BF16)
        kvv[rows, :] = nt(x, w2[e:, :]).astype(BF16)
    run_heads(
        lambda h: head(qq, 0, h, heads),
        lambda h: head(kvv, 0, h, heads),
        lambda h: head(kvv, 1, h, heads),
        None, "patch", sc, sz, oq, stq, heads,
    )
    run_heads(
        lambda h: head(qv, 0, h, heads),
        lambda h: head(kvq, 0, h, heads),
        lambda h: head(kvq, 1, h, heads),
        None, "question", sc, sz, ov, stv, heads,
    )
    pm[0:vp, :] = nn(ov[0:vp, :], wo3[...]).astype(BF16)
    pt[0:vp, :] = nn(ov[vp:, :], wo3[...]).astype(BF16)
    pm[vp:, :] = nn(oq[0:qh, :], wo2[...]).astype(BF16)
    pt[vp:, :] = nn(oq[qh:, :], wo2[...]).astype(BF16)


GELU_C = 0.7978845608028654
GELU_A = 0.044715


def section3(sz, layer, nm, nth, wi, bi, wo, pm, pt, g, gp):
    vp, half = sz.vp, sz.half
    for ref, out, base in ((nm, pm, 0), (nth, pt, half)):
        for lo, hi, e in ((0, vp, 0), (vp, half, 1)):
            h = nn(ref[lo:hi, :], wi[e]) + bi[layer, e : e + 1, :]
            h2 = h * h
            t = jnp.tanh(GELU_C * h * (1.0 + GELU_A * h2))
            half_t = 0.5 + 0.5 * t
            act = (h * half_t).astype(BF16)
            slope = half_t + (0.5 * GELU_C) * h * (1.0 - t * t) * (1.0 + 3.0 * GELU_A * h2)
            g[base + lo : base + hi, :] = act
            gp[base + lo : base + hi, :] = slope.astype(BF16)
            out[lo:hi, :] = nn(act, wo[e]).astype(BF16)


def section3_back(sz, dm, dt, wi, wo, gp, pm, pt, dh):
    vp, half = sz.vp, sz.half
    for ref, out, base in ((dm, pm, 0), (dt, pt, half)):
        for lo, hi, e in ((0, vp, 0), (vp, half, 1)):
            dg = nt(ref[lo:hi, :], wo[e])
            d = (dg * gp[base + lo : base + hi, :].astype(F32)).astype(BF16)
            dh[base + lo : base + hi, :] = d
            out[lo:hi, :] = nt(d, wi[e]).astype(BF16)


def back_heads(q_of, k_of, v_of, bias, kind, sc, sz, st, do_of, ds_ref, heads):
    dqs, dks, dvs = [], [], []
    for h in range(heads):
        dq, dk, dv, ds = attend_back(
            q_of(h), k_of(h), v_of(h), None if bias is None else bias[h], kind, sc, sz,
            st[h : h + 1, :], st[heads + h : heads + h + 1, :], do_of(h),
        )
        dqs.append(dq)
        dks.append(dk)
        dvs.append(dv)
        if ds_ref is not None:
            ds_ref[h] = ds
    dq = jnp.concatenate(dqs, 0).T.astype(BF16)
    dkv = jnp.concatenate(dks + dvs, 1).astype(BF16)
    return dq, dkv


def section2_back(sz, heads, sc, dm, dt, w2, w3, wo2, wo3, qq, kvv, stq, qv, kvq, stv, pm, pt, dqq, dkvv, dqv, dkvq, doq, dov):
    vp, qh = sz.vp, sz.qh
    e = heads * HDIM
    doq[0:qh, :] = nt(dm[vp:, :], wo2[...]).astype(BF16)
    doq[qh:, :] = nt(dt[vp:, :], wo2[...]).astype(BF16)
    dov[0:vp, :] = nt(dm[0:vp, :], wo3[...]).astype(BF16)
    dov[vp:, :] = nt(dt[0:vp, :], wo3[...]).astype(BF16)
    dq, dkv = back_heads(
        lambda h: head(qq, 0, h, heads),
        lambda h: head(kvv, 0, h, heads),
        lambda h: head(kvv, 1, h, heads),
        None, "patch", sc, sz, stq, lambda h: head(doq, 0, h, heads), None, heads,
    )
    dqq[...] = dq
    dkvv[...] = dkv
    dq, dkv = back_heads(
        lambda h: head(qv, 0, h, heads),
        lambda h: head(kvq, 0, h, heads),
        lambda h: head(kvq, 1, h, heads),
        None, "question", sc, sz, stv, lambda h: head(dov, 0, h, heads), None, heads,
    )
    dqv[...] = dq
    dkvq[...] = dkv
    for out, qrow, vrow in ((pm, slice(0, qh), slice(0, vp)), (pt, slice(qh, 2 * qh), slice(vp, 2 * vp))):
        out[vp:, :] = (nn(dqq[qrow, :], w2[0:e, :]) + nn(dkvq[qrow, :], w3[e:, :])).astype(BF16)
        out[0:vp, :] = (nn(dqv[vrow, :], w3[0:e, :]) + nn(dkvv[vrow, :], w2[e:, :])).astype(BF16)


def section1_back(sz, heads, sc, dm, dt, w0, w1, wo0, wo1, bias, qkvv, stv, qkvq, stq, pm, pt, dqkvv, dqkvq, ds, doq, dov):
    vp, qh = sz.vp, sz.qh
    e = heads * HDIM
    mine, theirs = window_permutation(sc, sz)
    do_m = nt(dm[0:vp, :], wo0[...]).astype(BF16)
    do_t = nt(dt[0:vp, :], wo0[...]).astype(BF16)
    dov[...] = (nn(mine, do_m) + nn(theirs, do_t)).astype(BF16)
    dq, dkv = back_heads(
        lambda h: head(qkvv, 0, h, heads),
        lambda h: head(qkvv, 1, h, heads),
        lambda h: head(qkvv, 2, h, heads),
        bias, "window", sc, sz, stv, lambda h: head(dov, 0, h, heads), ds, heads,
    )
    dqkvv[:, 0:e] = dq
    dqkvv[:, e:] = dkv
    dn = nn(dqkvv[...], w0[...]).astype(BF16)
    pm[0:vp, :] = tn(mine, dn).astype(BF16)
    pt[0:vp, :] = tn(theirs, dn).astype(BF16)
    doq[0:qh, :] = nt(dm[vp:, :], wo1[...]).astype(BF16)
    doq[qh:, :] = nt(dt[vp:, :], wo1[...]).astype(BF16)
    dq, dkv = back_heads(
        lambda h: head(qkvq, 0, h, heads),
        lambda h: head(qkvq, 1, h, heads),
        lambda h: head(qkvq, 2, h, heads),
        None, "self", sc, sz, stq, lambda h: head(doq, 0, h, heads), None, heads,
    )
    dqkvq[:, 0:e] = dq
    dqkvq[:, e:] = dkv
    pm[vp:, :] = nn(dqkvq[0:qh, :], w1[...]).astype(BF16)
    pt[vp:, :] = nn(dqkvq[qh:, :], w1[...]).astype(BF16)


def kept_order(order):
    return sorted(range(1 << len(order)), key=lambda r: [(r >> k) & 1 for k in order])


def store_blocks(sc, store, col, value):
    keep, send, scr, order = store
    width = value.shape[1]
    value = value.astype(BF16)
    cols = slice(col, col + width)
    if send is None:
        keep[0, :, cols] = value
        return
    count, rows = keep.shape[0], keep.shape[1]
    scr[:, 0:width] = value
    for slot, relative in enumerate(kept_order(order)):
        owner = relative ^ sc[5]
        block = scr[pl.ds(pl.multiple_of(owner * rows, 16), rows), 0:width]
        if slot < count:
            keep[slot, :, cols] = block
        else:
            send[slot - count, :, cols] = block


def section3_weights(sz, sc, nm, nth, dm, dt, g, dh, db, out):
    vp, half = sz.vp, sz.half
    hid = g.shape[1]
    for e, lo, hi in ((0, 0, vp), (1, vp, half)):
        into = tn(nm[lo:hi, :], dh[lo:hi, :]) + tn(nth[lo:hi, :], dh[half + lo : half + hi, :])
        away = tn(dm[lo:hi, :], g[lo:hi, :]) + tn(dt[lo:hi, :], g[half + lo : half + hi, :])
        out[:, e * hid : (e + 1) * hid] = into.astype(BF16)
        out[:, (2 + e) * hid : (3 + e) * hid] = away.astype(BF16)
        db[e : e + 1, :] = jnp.sum(dh[lo:hi, :].astype(F32), 0, keepdims=True) + jnp.sum(
            dh[half + lo : half + hi, :].astype(F32), 0, keepdims=True
        )


def section2_weights(sz, heads, sc, nm, nth, dm, dt, dqq, dkvv, dqv, dkvq, oq, ov, store):
    vp, qh = sz.vp, sz.qh
    e = heads * HDIM

    def both(a_m, a_t, b, cut, lo, hi):
        return tn(a_m[lo:hi, :], b[0:cut, :]) + tn(a_t[lo:hi, :], b[cut:, :])

    store_blocks(sc, store, 0, both(nm, nth, dqq, qh, vp, sz.half))
    store_blocks(sc, store, e, both(nm, nth, dkvv, vp, 0, vp))
    store_blocks(sc, store, 3 * e, both(nm, nth, dqv, vp, 0, vp))
    store_blocks(sc, store, 4 * e, both(nm, nth, dkvq, qh, vp, sz.half))
    store_blocks(sc, store, 6 * e, both(dm, dt, oq, qh, vp, sz.half))
    store_blocks(sc, store, 7 * e, both(dm, dt, ov, vp, 0, vp))


def section1_weights(sz, heads, sc, nm, nth, dm, dt, nvw, dqkvv, dqkvq, oq, ov, store):
    vp, qh = sz.vp, sz.qh
    e = heads * HDIM

    def both(a_m, a_t, b, cut, lo, hi):
        return tn(a_m[lo:hi, :], b[0:cut, :]) + tn(a_t[lo:hi, :], b[cut:, :])

    store_blocks(sc, store, 0, tn(nvw[...], dqkvv[...]))
    store_blocks(sc, store, 3 * e, both(nm, nth, dqkvq, qh, vp, sz.half))
    store_blocks(sc, store, 6 * e, both(dm, dt, ov, vp, 0, vp))
    store_blocks(sc, store, 7 * e, both(dm, dt, oq, qh, vp, sz.half))


def in_order(sz, chip, own, other, out):
    v, piece = sz.vpiece, sz.piece
    mine, theirs = own[...].astype(F32), other[...].astype(F32)
    first = jnp.where(chip == 0, mine, theirs)
    second = jnp.where(chip == 0, theirs, mine)
    out[0:v, :] = first[0:v]
    out[v : 2 * v, :] = second[0:v]
    out[2 * v : v + piece, :] = first[v:]
    out[v + piece :, :] = second[v:]


def norm_rows(x):
    center = x - jnp.mean(x, -1, keepdims=True)
    inv = lax.rsqrt(jnp.mean(center * center, -1, keepdims=True) + EPS)
    return center * inv, inv


def open_stream(sz, sc, own, other, scale, shift, x, n):
    layer = first = 0
    in_order(sz, sc[6], own, other, x)
    for lo, hi, e in ((0, sz.vp, 0), (sz.vp, sz.half, 1)):
        gain, bias = scale[first + e, layer : layer + 1, :], shift[first + e, layer : layer + 1, :]
        n[lo:hi, :] = (norm_rows(x[lo:hi, :])[0] * gain + bias).astype(BF16)


def open_grad(sz, sc, own, other, grad, dy, sums):
    in_order(sz, sc[6], own, other, grad)
    dy[...] = grad[...].astype(BF16)
    for lo, hi, e in ((0, sz.vp, 0), (sz.vp, sz.half, 1)):
        sums[4 + e : 5 + e, :] = jnp.sum(grad[lo:hi, :], 0, keepdims=True)


def add_norm(sz, layer, first, x, a, b, extra, scale, shift, y, n):
    for lo, hi, e in ((0, sz.vp, 0), (sz.vp, sz.half, 1)):
        gain, bias = scale[first + e, layer : layer + 1, :], shift[first + e, layer : layer + 1, :]
        value = x[lo:hi, :] + (a[lo:hi, :].astype(F32) + b[lo:hi, :].astype(F32))
        if extra is not None:
            value = value + extra[layer - 1, e : e + 1, :]
        y[lo:hi, :] = value
        n[lo:hi, :] = (norm_rows(value)[0] * gain + bias).astype(BF16)


def norm_back(sz, layer, first, d, a, b, x, scale, out, dy, sums):
    for lo, hi, e in ((0, sz.vp, 0), (sz.vp, sz.half, 1)):
        dn = a[lo:hi, :].astype(F32) + b[lo:hi, :].astype(F32)
        unit, inv = norm_rows(x[lo:hi, :])
        du = dn * scale[first + e, layer : layer + 1, :]
        dx = inv * (
            du
            - jnp.mean(du, -1, keepdims=True)
            - unit * jnp.mean(du * unit, -1, keepdims=True)
        )
        value = d[lo:hi, :] + dx
        out[lo:hi, :] = value
        dy[lo:hi, :] = value.astype(BF16)
        sums[e : e + 1, :] = jnp.sum(dn * unit, 0, keepdims=True)
        sums[2 + e : 3 + e, :] = jnp.sum(dn, 0, keepdims=True)
        sums[4 + e : 5 + e, :] = jnp.sum(value, 0, keepdims=True)


TABLE = SPAN * SPAN
TABLE_PAD = -(-TABLE // 128) * 128
CELLS_PAD = -(-SPAN * WIN // 128) * 128


def spread_matrix():
    cell = iota((TABLE_PAD, CELLS_PAD), 1)
    row = (cell * 171) >> 11
    place = row * SPAN + cell - row * WIN
    return ((iota((TABLE_PAD, CELLS_PAD), 0) == place) & (cell < SPAN * WIN)).astype(F32)


def table_bias(tables, out, spread, rows):
    spread[...] = spread_matrix()
    count = out.shape[0]
    for i in range(count):
        table = tables[i : i + 1, :]
        for b in range(WIN):
            at = i * WIN + b
            rows[at : at + 1, :] = pltpu.roll(table, (TABLE_PAD - (WIN - 1 - b)) % TABLE_PAD, 1)
    cells = jnp.dot(rows[...], spread[...], precision=lax.Precision.HIGHEST, preferred_element_type=F32)
    for a in range(WIN):
        moved = pltpu.roll(cells, (CELLS_PAD - WIN * (WIN - 1 - a)) % CELLS_PAD, 1)
        for i in range(count):
            out[i, WIN * a : WIN * (a + 1), :] = moved[WIN * i : WIN * (i + 1), 0 : WIN * WIN]


def table_grad(ds, spread, out):
    heads = ds.shape[0]
    rows = jnp.zeros((WIN, CELLS_PAD - WIN * WIN), F32)
    every = []
    for h in range(heads):
        grad = ds[h].astype(F32)
        cells = jnp.zeros((WIN, CELLS_PAD), F32)
        for a in range(WIN):
            part = jnp.concatenate([grad[WIN * a : WIN * (a + 1), :], rows], 1)
            cells = cells + pltpu.roll(part, WIN * (WIN - 1 - a), 1)
        every.append(cells)
    places = lax.dot_general(
        jnp.concatenate(every, 0),
        spread[...],
        (((1,), (1,)), ((), ())),
        precision=lax.Precision.HIGHEST,
        preferred_element_type=F32,
    )
    for h in range(heads):
        total = jnp.zeros((1, TABLE_PAD), F32)
        for b in range(WIN):
            total = total + pltpu.roll(places[h * WIN + b : h * WIN + b + 1, :], WIN - 1 - b, 1)
        out[h : h + 1, :] = total


def collect(layers, heads, *refs):
    out = refs[-1]
    out[...] = jnp.zeros(out.shape, F32)
    row = 0
    for layer in range(layers):
        sums1, sums2, sums3, after = refs[6 * layer : 6 * layer + 4]
        for ref, lo, count in ((sums1, 0, 4), (sums2, 0, 4), (sums3, 0, 4), (after, 4, 2)):
            out[row : row + count, :] = ref[lo : lo + count, :]
            row += count
    for layer in range(layers):
        db, table = refs[6 * layer + 4 : 6 * layer + 6]
        out[row : row + 2, :] = db[...]
        row += 2
        out[row : row + heads, 0:TABLE_PAD] = table[0:heads, :]
        row += heads


def deal(layers, heads, rows, scale, shift, out_bias, in_bias, rel):
    for layer in range(layers):
        at = 14 * layer
        for section in range(3):
            for e in range(2):
                scale[2 * section + e, layer : layer + 1, :] = rows[at + 4 * section + e : at + 4 * section + e + 1, :]
                row = at + 4 * section + 2 + e
                shift[2 * section + e, layer : layer + 1, :] = rows[row : row + 1, :]
        out_bias[layer] = rows[at + 12 : at + 14, :]
        at = 14 * layers + (2 + heads) * layer
        in_bias[layer] = rows[at : at + 2, :]
        for h in range(heads):
            rel[h, layer : layer + 1, :] = rows[at + 2 + h : at + 3 + h, 0:TABLE]


def finish_mlp(layers, *refs):
    up, down = refs[layers:]
    hid = up.shape[3]
    for layer in range(layers):
        total = refs[layer][...].astype(F32)
        for e in range(2):
            up[layer, e] = total[:, e * hid : (e + 1) * hid]
            down[layer, e] = total[:, (2 + e) * hid : (3 + e) * hid]


def finish_attn(layers, *refs):
    d_in, d_out = refs[8 * layers :]
    e = d_in.shape[4]
    for layer in range(layers):
        for pair in range(2):
            first = 8 * layer + 4 * pair
            total = sum(r[...].astype(F32) for r in refs[first : first + 4])
            for which in range(2):
                for c in range(3):
                    col = (3 * which + c) * e
                    d_in[layer, 2 * pair + which, c] = total[:, col : col + e]
                col = (6 + which) * e
                d_out[layer, 2 * pair + which] = total[:, col : col + e].T


def on_device(
    dp_size,
    visual,
    queries,
    valid_windows,
    answer_start,
    shifts,
    norm_scale,
    norm_shift,
    attn_in,
    attn_out,
    rel_bias,
    mlp_in,
    mlp_in_bias,
    mlp_out,
    mlp_out_bias,
    grad_visual_out,
    grad_query_out,
):
    layers, width = attn_in.shape[0], attn_in.shape[2]
    edev = attn_in.shape[4]
    heads = edev // HDIM
    hid = mlp_in.shape[3]
    sz = Sizes(4 * visual.shape[1], 4 * queries.shape[1])
    half, vp, qh = sz.half, sz.vp, sz.qh
    vq, qq_ = sz.vquart, sz.qquart
    t_index = lax.axis_index("tensor")
    d_index = lax.axis_index("dp")
    core, chip = t_index % 2, t_index // 2
    swap = [(i, i ^ 1) for i in range(4)]
    cross = [(i, i ^ 2) for i in range(4)]
    block_rows = width // dp_size
    halving = dp_size > 1 and dp_size & (dp_size - 1) == 0 and block_rows % 16 == 0
    bits = dp_size.bit_length() - 1

    def scalars(layer):
        on = layer % 2
        values = [core, answer_start[0], shifts[0, 0] * on, shifts[0, 1] * on, valid_windows[0, 0], d_index, chip, 0]
        return jnp.stack(values).astype(jnp.int32)

    w_in = attn_in.transpose(0, 1, 3, 4, 2).reshape(layers, 4, 3 * edev, width)
    scale, shift = norm_scale.transpose(1, 0, 2), norm_shift.transpose(1, 0, 2)

    def packed(own_v, own_q):
        pad = jnp.zeros((sz.vpiece - vq, width), own_v.dtype)
        return jnp.concatenate([own_v, pad, own_q], 0)

    def piece_of(rows, place):
        v = jnp.where(place == 0, rows[0 : sz.vpiece], rows[sz.vpiece : vp])
        q = jnp.where(place == 0, rows[vp : vp + qq_], rows[vp + qq_ :])
        return jnp.concatenate([v, q], 0)

    def pair_sum(mine, theirs):
        got = lax.ppermute(theirs, "tensor", swap)
        return (mine.astype(F32) + got.astype(F32)).astype(BF16)

    def pair(x):
        return x, lax.ppermute(x, "tensor", swap)

    rows_bf = shaped((half, width))
    rows_f = shaped((half, width), F32)
    mac = 2 * half * width

    own = packed(visual[0], queries[0])
    other = lax.ppermute(own, "tensor", cross)
    tables = jnp.pad(rel_bias.reshape(layers * heads, TABLE), ((0, 0), (0, TABLE_PAD - TABLE)))
    bias_all, spread = call(
        table_bias,
        [shaped((layers * heads, sz.vis, sz.vis), F32), shaped((TABLE_PAD, CELLS_PAD), F32)],
        [],
        [tables],
        name="table_bias",
        scratch=[pltpu.VMEM((layers * heads * WIN, TABLE_PAD), F32)],
    )
    bias_all = bias_all.reshape(layers, heads, sz.vis, sz.vis)
    scal = [scalars(layer) for layer in range(layers)]
    own_grad = packed(grad_visual_out[0], grad_query_out[0])
    rounded_grad = lax.reduce_precision(own_grad, 8, 7)

    def next_norm(stream, a, b, layer, first, extra):
        args = [stream, a, b] + ([mlp_out_bias] if extra else []) + [scale, shift]

        def body(x, a, b, *rest):
            if not extra:
                rest = (None,) + rest
            add_norm(sz, layer, first, x, a, b, *rest)

        return call(body, [rows_f, rows_bf], [], args, name="norm")

    def shares(kept):
        return kept, lax.ppermute(kept, "tensor", cross)

    fetched = {}

    def fetch(layer, section, after):
        if section == 3:
            arrays = [mlp_in, mlp_out]
            blocks = [(0, (layer,)), (1, (layer,))]
        else:
            arrays = [w_in, attn_out]
            first = 2 * (section - 1)
            blocks = [(0, (layer, first)), (0, (layer, first + 1)), (1, (layer, first)), (1, (layer, first + 1))]
        arrays = tie(after, arrays)[1]
        outs = [shaped(arrays[k].shape[len(lead) :]) for k, lead in blocks]

        def body(one, two, *refs):
            copies = [
                pltpu.make_async_copy((one, two)[k].at[lead], refs[j], refs[-1].at[j])
                for j, (k, lead) in enumerate(blocks)
            ]
            for copy in copies:
                copy.start()
            for copy in copies:
                copy.wait()

        fetched[layer, section] = pl.pallas_call(
            body,
            out_shape=outs,
            in_specs=[pl.BlockSpec(memory_space=pltpu.HBM)] * 2,
            out_specs=[pl.BlockSpec(memory_space=pltpu.VMEM)] * len(outs),
            scratch_shapes=[pltpu.SemaphoreType.DMA((len(outs),))],
            compiler_params=pltpu.CompilerParams(vmem_limit_bytes=VMEM_LIMIT),
            name="fetch",
        )(*arrays)

    def fetch_beside(layer, section, a, b):
        fetch(layer, section, a)
        b, fetched[layer, section] = tie(b, fetched[layer, section])
        return b

    fetch(0, 1, own)
    other, fetched[0, 1] = tie(other, fetched[0, 1])
    stream, normed = call(
        lambda *r: open_stream(sz, *r), [rows_f, rows_bf], scal[0:1], [own, other, scale, shift], name="open_stream"
    )

    saved = []
    for layer in range(layers):
        sc = scal[layer]
        nm, nth = pair(normed)
        if layer == 0:
            sent_grad, nth = tie(rounded_grad.astype(BF16), nth)
            other_grad = lax.ppermute(sent_grad, "tensor", cross)
        part = call(
            lambda *r: section1(sz, heads, *r),
            [
                rows_bf,
                rows_bf,
                shaped((sz.vis, width)),
                shaped((sz.vis, 3 * edev)),
                shaped((2 * vp, edev)),
                shaped((8, sz.vis), F32),
                shaped((sz.qlen, 3 * edev)),
                shaped((sz.qlen, edev)),
                shaped((8, sz.qlen), F32),
            ],
            [sc],
            [
                nm, nth, *fetched[layer, 1], Part(bias_all, layer),
            ],
            flops=mac * 4 * edev * 2 + 8 * heads * HDIM * sz.qlen * sz.qlen,
            name="section1",
            scratch=[pltpu.VMEM((sz.vis, edev), BF16)],
        )
        kept1 = (stream, nm, nth) + tuple(part[2:9])
        kept = pair_sum(part[0], part[1])
        if layer == 0:
            kept, other_grad = tie(kept, other_grad)
        a, b = shares(kept)
        if layer == 0:
            other_grad, sent_grad, a2 = tie(other_grad, sent_grad, a)
            grad, dy, grad_sums = call(
                lambda *r: open_grad(sz, *r),
                [rows_f, rows_bf, shaped((8, width), F32)],
                scal[0:1],
                [sent_grad, other_grad],
                name="open_grad",
            )
            b, grad, dy = tie(b, grad, dy)
        b = fetch_beside(layer, 2, a, b)
        stream, normed = next_norm(stream, a, b, layer, 2, False)
        nm, nth = pair(normed)
        part = call(
            lambda *r: section2(sz, heads, *r),
            [
                rows_bf,
                rows_bf,
                shaped((sz.qlen, edev)),
                shaped((2 * vp, 2 * edev)),
                shaped((sz.qlen, edev)),
                shaped((8, sz.qlen), F32),
                shaped((2 * vp, edev)),
                shaped((sz.qlen, 2 * edev)),
                shaped((2 * vp, edev)),
                shaped((8, 2 * vp), F32),
            ],
            [sc],
            [nm, nth, *fetched[layer, 2]],
            flops=mac * 4 * edev * 2,
            name="section2",
        )
        kept2 = (stream, nm, nth) + tuple(part[2:])
        a, b = shares(pair_sum(part[0], part[1]))
        b = fetch_beside(layer, 3, a, b)
        stream, normed = next_norm(stream, a, b, layer, 4, False)
        nm, nth = pair(normed)
        part = call(
            lambda *r: section3(sz, layer, *r),
            [rows_bf, rows_bf, shaped((2 * half, hid)), shaped((2 * half, hid))],
            [],
            [nm, nth, fetched[layer, 3][0], mlp_in_bias, fetched[layer, 3][1]],
            flops=mac * hid * 4,
            name="section3",
        )
        kept3 = (stream, nm, nth) + tuple(part[2:])
        saved.append((kept1, kept2, kept3))
        if layer + 1 < layers:
            a, b = shares(pair_sum(part[0], part[1]))
            b = fetch_beside(layer + 1, 1, a, b)
            stream, normed = next_norm(stream, a, b, layer + 1, 0, True)
    last = pair_sum(part[0], part[1])
    away = lax.ppermute(piece_of(last, 1 - chip), "tensor", cross)
    out = piece_of(stream, chip) + (piece_of(last, chip).astype(F32) + away.astype(F32))
    out_v = (out[0:vq] + mlp_out_bias[layers - 1, 0]).astype(BF16)
    out_q = (out[sz.vpiece :] + mlp_out_bias[layers - 1, 1]).astype(BF16)

    bias_sums = grad_sums

    def whole_sum(rows):
        return lax.psum_scatter(rows, "dp", scatter_dimension=0, tiled=True)

    class Reduction:
        def __init__(self, outs, order):
            self.order = order
            if halving:
                self.parts, self.step = [outs[0]], 0
                self.ready = outs[1]
                self.move()
            else:
                self.sum = whole_sum(outs[0][0])
                self.step = bits

        def move(self):
            bit = 1 << self.order[self.step]
            got = lax.ppermute(self.ready, "dp", [(i, i ^ bit) for i in range(dp_size)])
            self.parts.append(got)
            self.step += 1

        def advance(self):
            count = 1 << (bits - 1 - self.step)
            self.ready = sum(p[count : 2 * count].astype(F32) for p in self.parts).astype(BF16)
            self.move()

        def pieces(self):
            if not halving:
                zero = jnp.zeros_like(self.sum)
                return [self.sum, zero, zero, zero]
            lead = [Part(p, 0) for p in self.parts]
            while len(lead) < 4:
                lead.append(jnp.zeros(lead[0].rest, BF16))
            return lead

    def close(grad, a, b, kept, layer, first):
        return call(
            lambda *r: norm_back(sz, layer, first, *r),
            [rows_f, rows_bf, shaped((8, width), F32)],
            [],
            [grad, a, b, kept[0], scale],
            name="norm_back",
        )

    straight = tuple(range(bits))
    turned = straight[1:] + straight[:1]

    def weights(body, extra_outs, orders, columns, args, wide, name):
        outs = []
        for _ in orders:
            if halving:
                outs += [shaped((dp_size // 2, block_rows, columns))] * 2
            else:
                outs += [shaped((1, width, columns))]
        lead = 1 + len(args) + len(extra_outs)
        each = 2 if halving else 1

        def wrapped(*refs):
            stores = []
            for k, order in enumerate(orders):
                given = refs[lead + k * each : lead + (k + 1) * each]
                stores.append((given[0], given[1] if halving else None, refs[-1], order))
            body(*refs[:lead], *stores)

        got = call(
            wrapped,
            list(extra_outs) + outs,
            [scal[0]],
            args,
            name=name,
            scratch=[pltpu.VMEM((width, wide), BF16)],
        )
        extra, rest = got[: len(extra_outs)], got[len(extra_outs) :]
        return extra, [Reduction(rest[k * each : (k + 1) * each], order) for k, order in enumerate(orders)]

    reductions = []
    feeds = []
    arrivals = {}
    if halving and bits == 3 and layers == 2:
        arrivals = {2: [0], 3: [0, 1], 4: [1], 5: [2]}

    def window(kept, args):
        return tie(kept, list(args))[1]

    def seal(index, got, extra, made):
        due = [reductions[g] for g in arrivals.get(index, ()) if reductions[g].step < bits]
        firsts = [r.parts[0] for r in made] if halving else []
        extra, firsts, parts = tie(list(extra), firsts, [r.parts for r in due])
        for r, p in zip(due, parts):
            r.parts = list(p)
            r.advance()
        got, extra, firsts = tie(got, extra, firsts)
        for r, part in zip(made, firsts):
            r.parts[0] = part
        reductions.extend(made)
        return got, extra

    grads = [None] * layers
    index = 0
    for layer in reversed(range(layers)):
        sc = scal[layer]
        kept1, kept2, kept3 = saved[layer]
        dm, dt = pair(dy)
        _, nm, nth, act, slope = kept3
        up, down = fetched[layer, 3]
        pm, pt, dh = call(
            lambda *r: section3_back(sz, *r),
            [rows_bf, rows_bf, shaped((2 * half, hid))],
            [],
            [dm, dt, up, down, slope],
            flops=mac * hid * 4,
            name="section3_back",
        )
        a, b = shares(pair_sum(pm, pt))
        args = window(a, [nm, nth, dm, dt, act, dh])
        db, feed = call(
            lambda *r: section3_weights(sz, *r),
            [shaped((2, hid), F32), shaped((width, 4 * hid))],
            [sc],
            args,
            name="section3_weights",
        )
        feeds.append(whole_sum(feed))
        b, (db,) = seal(index, b, [db], [])
        index += 1
        out_bias_sums = bias_sums
        grad, dy, sums3 = close(grad, a, b, kept3, layer, 4)

        dm, dt = pair(dy)
        _, nm, nth, qq, kvv, oq, stq, qv, kvq, ov, stv = kept2
        part = call(
            lambda *r: section2_back(sz, heads, *r),
            [
                rows_bf,
                rows_bf,
                shaped((sz.qlen, edev)),
                shaped((2 * vp, 2 * edev)),
                shaped((2 * vp, edev)),
                shaped((sz.qlen, 2 * edev)),
            ],
            [sc],
            [
                dm, dt, *fetched[layer, 2],
                qq, kvv, stq, qv, kvq, stv,
            ],
            flops=mac * 4 * edev * 2,
            name="section2_back",
            scratch=[pltpu.VMEM((sz.qlen, edev), BF16), pltpu.VMEM((2 * vp, edev), BF16)],
        )
        a, b = shares(pair_sum(part[0], part[1]))
        args = window(a, [nm, nth, dm, dt, part[2], part[3], part[4], part[5], oq, ov])
        _, made = weights(
            lambda *r: section2_weights(sz, heads, *r), [], [straight], 8 * edev, args, 2 * edev, "section2_weights"
        )
        b, _ = seal(index, b, [], made)
        index += 1
        grad, dy, sums2 = close(grad, a, b, kept2, layer, 2)

        dm, dt = pair(dy)
        _, nm, nth, nvw, qkvv, ov, stv, qkvq, oq, stq = kept1
        part = call(
            lambda *r: section1_back(sz, heads, *r),
            [
                rows_bf,
                rows_bf,
                shaped((sz.vis, 3 * edev)),
                shaped((sz.qlen, 3 * edev)),
                shaped((heads, sz.vis, sz.vis)),
            ],
            [sc],
            [
                dm, dt, *fetched[layer, 1],
                Part(bias_all, layer), qkvv, stv, qkvq, stq,
            ],
            flops=mac * 4 * edev * 2 + 20 * heads * HDIM * sz.qlen * sz.qlen,
            name="section1_back",
            scratch=[pltpu.VMEM((sz.qlen, edev), BF16), pltpu.VMEM((sz.vis, edev), BF16)],
        )
        a, b = shares(pair_sum(part[0], part[1]))
        args = window(a, [nm, nth, dm, dt, nvw, part[2], part[3], oq, ov])
        _, made = weights(
            lambda *r: section1_weights(sz, heads, *r), [], [straight], 8 * edev, args, 3 * edev, "section1_weights"
        )
        b, _ = seal(index, b, [], made)
        (table,) = call(table_grad, [shaped((8, TABLE_PAD), F32)], [], [part[4], spread], name="table_grad")
        index += 1
        grad, dy, sums1 = close(grad, a, b, kept1, layer, 0)
        bias_sums = sums1
        grads[layer] = (sums1, sums2, sums3, out_bias_sums, db, table)

    if halving:
        for r in reductions:
            while r.step < bits:
                r.advance()

    own_total = piece_of(grad, chip) + (own_grad - rounded_grad)
    grad_v, grad_q = own_total[0:vq], own_total[sz.vpiece :]

    def summed(x, axis, size, steps):
        for bit in steps:
            x = x + lax.ppermute(x, axis, [(i, i ^ bit) for i in range(size)])
        return x

    per_norm = 14 * layers
    count = -(-(per_norm + (2 + heads) * layers) // 8) * 8
    (rows,) = call(
        lambda *r: collect(layers, heads, *r),
        [shaped((count, width), F32)],
        [],
        [x for g in grads for x in g],
        name="collect",
    )
    twice = lax.ppermute(rows, "tensor", swap)
    rows = rows + jnp.where(iota((count, 1), 0) < per_norm, twice, 0.0)
    rows = summed(rows, "dp", dp_size, [1 << k for k in range(bits)])
    scale_total, shift_total, out_bias_total, in_bias_total, rel_total = call(
        lambda *r: deal(layers, heads, *r),
        [shaped((6, layers, width), F32)] * 2
        + [shaped((layers, 2, width), F32), shaped((layers, 2, hid), F32), shaped((heads, layers, TABLE), F32)],
        [],
        [rows],
        name="deal",
    )

    d_up, d_down = call(
        lambda *r: finish_mlp(layers, *r),
        [shaped((layers, 2, block_rows, hid), F32)] * 2,
        [],
        feeds[::-1],
        name="finish_mlp",
    )
    sums = [reductions[2 * (layers - 1 - layer) : 2 * (layers - layer)] for layer in range(layers)]
    d_in, d_out = call(
        lambda *r: finish_attn(layers, *r),
        [shaped((layers, 4, 3, block_rows, edev), F32), shaped((layers, 4, edev, block_rows), F32)],
        [],
        [p for r in sums for p in r[1].pieces() + r[0].pieces()],
        name="finish_attn",
    )
    return (
        out_v[None],
        out_q[None],
        grad_v[None],
        grad_q[None],
        scale_total.transpose(1, 0, 2),
        shift_total.transpose(1, 0, 2),
        d_in.transpose(0, 1, 3, 2, 4),
        d_out,
        rel_total.transpose(1, 0, 2),
        d_up,
        in_bias_total,
        d_down.transpose(0, 1, 3, 2),
        out_bias_total,
    )


def solution(mesh):
    dp_size = mesh.shape["dp"]
    return jax.shard_map(
        lambda *args: on_device(dp_size, *args),
        mesh=mesh,
        in_specs=(
            P("dp", "tensor", None),
            P("dp", "tensor", None),
            P("dp", None),
            P("dp"),
            P("dp", None),
            P(),
            P(),
            P(None, None, None, None, "tensor"),
            P(None, None, "tensor", None),
            P(None, "tensor", None),
            P(None, None, None, "tensor"),
            P(None, None, "tensor"),
            P(None, None, "tensor", None),
            P(),
            P("dp", "tensor", None),
            P("dp", "tensor", None),
        ),
        out_specs=(
            P("dp", "tensor", None),
            P("dp", "tensor", None),
            P("dp", "tensor", None),
            P("dp", "tensor", None),
            P(),
            P(),
            P(None, None, "dp", None, "tensor"),
            P(None, None, "tensor", "dp"),
            P(None, "tensor", None),
            P(None, None, "dp", "tensor"),
            P(None, None, "tensor"),
            P(None, None, "tensor", "dp"),
            P(),
        ),
        check_vma=False,
    )
```

```python
import jax
import jax.numpy as jnp
from jax import lax
from jax.experimental import pallas as pl
from jax.experimental.pallas import tpu as pltpu
from jax.sharding import PartitionSpec as P

HDIM = 64
WIN = 12
SPAN = 2 * WIN - 1
EPS = 1e-05
NEG = -1000000000.0
OUT = -1e30
F32 = jnp.float32
BF16 = jnp.bfloat16
VMEM_LIMIT = 20 * 2**20


def nn(a, b):
    return lax.dot_general(a, b, (((1,), (0,)), ((), ())), preferred_element_type=F32)


def nt(a, b):
    return lax.dot_general(a, b, (((1,), (1,)), ((), ())), preferred_element_type=F32)


def tn(a, b):
    return lax.dot_general(a, b, (((0,), (0,)), ((), ())), preferred_element_type=F32)


class Part:
    def __init__(self, array, *lead):
        self.array, self.lead = array, lead
        self.rest = array.shape[len(lead) :]
        self.dtype = array.dtype
        self.size = 1
        for n in self.rest:
            self.size *= n


class Arriving:
    def __init__(self, ref, copy):
        self.ref, self.copy, self.shape = ref, copy, ref.shape

    def __getitem__(self, at):
        if self.copy is not None:
            self.copy.wait()
            self.copy = None
        return self.ref[at]


class Rows:
    def __init__(self, refs):
        self.spans = [r if isinstance(r, tuple) else (r, 0, r.shape[0]) for r in refs]

    def pieces(self, at):
        rows = at[0] if isinstance(at, tuple) else slice(None)
        total = sum(end - start for _, start, end in self.spans)
        lo, hi, _ = rows.indices(total)
        base = 0
        for ref, start, end in self.spans:
            first, last = max(lo - base, 0), min(hi - base, end - start)
            if first < last:
                yield ref, start + first, start + last, base + first - lo
            base += end - start

    def __getitem__(self, at):
        cols = at[1] if isinstance(at, tuple) else slice(None)
        parts = [ref[first:last, cols] for ref, first, last, _ in self.pieces(at)]
        return parts[0] if len(parts) == 1 else jnp.concatenate(parts, 0)

    def __setitem__(self, at, value):
        for ref, first, last, place in self.pieces(at):
            ref[first:last, :] = value[place : place + last - first, :]


def call(body, outs, scalars, args, name=None, scratch=()):
    vmem = pl.BlockSpec(memory_space=pltpu.VMEM)
    smem = pl.BlockSpec(memory_space=pltpu.SMEM)
    hbm = pl.BlockSpec(memory_space=pltpu.HBM)
    flat = [x for a in args for x in (a if isinstance(a, list) else [a])]
    flat_outs = [x for o in outs for x in (o if isinstance(o, list) else [o])]
    parts = [i for i, a in enumerate(flat) if isinstance(a, Part)]
    specs = [hbm if isinstance(a, Part) else vmem for a in flat]
    arrays = [a.array if isinstance(a, Part) else a for a in flat]
    landing = [pltpu.VMEM(flat[i].rest, flat[i].dtype) for i in parts]
    if parts:
        landing.append(pltpu.SemaphoreType.DMA((len(parts),)))
    first, end = len(scalars), len(scalars) + len(flat) + len(flat_outs) + len(scratch)

    def wrapped(*refs):
        refs = list(refs)
        buffers = refs[end:]
        coming = []
        for k, i in enumerate(parts):
            source = refs[first + i]
            if flat[i].lead:
                source = source.at[flat[i].lead]
            copy = pltpu.make_async_copy(source, buffers[k], buffers[-1].at[k])
            copy.start()
            coming.append(Arriving(buffers[k], copy))
            refs[first + i] = coming[-1]
        given = iter(refs[:end])
        grouped = [next(given) for _ in scalars]
        for x in list(args) + list(outs):
            grouped.append(Rows([next(given) for _ in x]) if isinstance(x, list) else next(given))
        body(*grouped, *given)
        for piece in coming:
            if piece.copy is not None:
                piece.copy.wait()

    got = iter(
        pl.pallas_call(
            wrapped,
            out_shape=tuple(flat_outs),
            in_specs=[smem] * len(scalars) + specs,
            out_specs=tuple(vmem for _ in flat_outs),
            scratch_shapes=list(scratch) + landing,
            compiler_params=pltpu.CompilerParams(vmem_limit_bytes=VMEM_LIMIT),
            cost_estimate=pl.CostEstimate(flops=1, bytes_accessed=1, transcendentals=0),
            name=name,
        )(*scalars, *arrays)
    )
    return [[next(got) for _ in o] if isinstance(o, list) else next(got) for o in outs]


def tie(*groups):
    return lax.optimization_barrier(groups)


def shaped(shape, dtype=BF16):
    return jax.ShapeDtypeStruct(shape, dtype)


class Sizes:
    def __init__(self, vis, qlen):
        self.vis, self.qlen = vis, qlen
        self.qh = qlen // 2
        self.vquart, self.qquart = vis // 4, qlen // 4
        self.vpiece = -(-self.vquart // 8) * 8
        self.vp = 2 * self.vpiece
        self.piece = self.vpiece + self.qquart
        self.half = 2 * self.piece
        self.near = self.half // 2
        self.q1 = self.near - self.vp
        self.q2 = self.half - self.near


def iota(shape, dim):
    return lax.broadcasted_iota(jnp.int32, shape, dim)


def div12(x):
    return (x * 171) >> 11


def patch_of(index, core, sz):
    second = (index >= sz.vp).astype(jnp.int32)
    row = index - second * sz.vp
    half = second + core - 2 * second * core
    late = (row >= sz.vpiece).astype(jnp.int32)
    row = row - late * sz.vpiece
    return jnp.where(row < sz.vquart, row + (2 * late + half) * sz.vquart, -1)


def query_of(index, core, sz):
    far = (index >= 2 * sz.q1).astype(jnp.int32)
    row = index - far * 2 * sz.q1
    size = sz.q1 + far * (sz.q2 - sz.q1)
    second = (row >= size).astype(jnp.int32)
    row = row - second * size + far * sz.q1
    half = second + core - 2 * second * core
    return row + jnp.where(row >= sz.qquart, sz.qquart, 0) + half * sz.qquart


def patch_rows(mine, theirs, sz):
    return jnp.concatenate([mine[0 : sz.vp, :], theirs[0 : sz.vp, :]], 0)


def near_rows(mine, theirs, sz):
    return jnp.concatenate([mine[sz.vp : sz.near, :], theirs[sz.vp : sz.near, :]], 0)


def far_rows(mine, theirs, sz):
    return jnp.concatenate([mine[sz.near :, :], theirs[sz.near :, :]], 0)


def query_rows(mine, theirs, sz):
    return jnp.concatenate([near_rows(mine, theirs, sz), far_rows(mine, theirs, sz)], 0)


def give_patches(mine, theirs, value, sz):
    mine[0 : sz.vp, :] = value[0 : sz.vp]
    theirs[0 : sz.vp, :] = value[sz.vp :]


def give_near(mine, theirs, value, sz):
    mine[sz.vp : sz.near, :] = value[0 : sz.q1]
    theirs[sz.vp : sz.near, :] = value[sz.q1 : 2 * sz.q1]


def window_permutation(sc, sz):
    core, down, right = sc[0], sc[2], sc[3]
    place = iota((sz.vis, sz.vp), 0)
    a = div12(place)
    b = place - a * WIN
    a = a + down
    b = b + right
    a = jnp.where(a >= WIN, a - WIN, a)
    b = jnp.where(b >= WIN, b - WIN, b)
    source = a * WIN + b
    stored = iota((sz.vis, sz.vp), 1)
    mine = (source == patch_of(stored, core, sz)).astype(F32).astype(BF16)
    theirs = (source == patch_of(stored + sz.vp, core, sz)).astype(F32).astype(BF16)
    return mine, theirs


def window_class(index, sc):
    a = div12(index)
    b = index - a * WIN
    return jnp.where(a >= WIN - sc[2], 2, 0) + jnp.where(b >= WIN - sc[3], 1, 0)


def window_mask(sc, sz):
    keys = window_class(iota((sz.vis, 1), 0), sc)
    asks = window_class(iota((1, sz.vis), 1), sc)
    keys = jnp.where(sc[4] > 0, keys, -1)
    return keys == asks


def self_mask(sc, sz, count, base):
    keys = query_of(iota((sz.qlen, 1), 0), sc[0], sz)
    asks = query_of(iota((1, count), 1) + base, sc[0], sz)
    return keys <= jnp.maximum(asks, sc[1] - 1)


def question_mask(sc, sz):
    return query_of(iota((sz.qlen, 1), 0), sc[0], sz) < sc[1]


def patch_pad(sc, sz):
    return patch_of(iota((2 * sz.vp, 1), 0), sc[0], sz) >= 0


def masked(scores, kind, sc, sz, base=0):
    if kind == "self":
        return jnp.where(self_mask(sc, sz, scores.shape[1], base), scores, NEG)
    if kind == "question":
        return jnp.where(question_mask(sc, sz), scores, NEG)
    if kind == "window":
        return jnp.where(window_mask(sc, sz), scores, NEG)
    real = patch_pad(sc, sz)
    return jnp.where(real & (sc[4] > 0), scores, jnp.where(real, NEG, OUT))


def allowed(kind, sc, sz):
    if kind == "self":
        return self_mask(sc, sz, sz.qlen, 0)
    if kind == "question":
        return question_mask(sc, sz)
    if kind == "window":
        return window_mask(sc, sz)
    return patch_pad(sc, sz) & (sc[4] > 0)


SCALE = HDIM**-0.5


def attend(q, k, v, addend, kind, sc, sz, base):
    scores = nt(k, q) * SCALE
    if addend is not None:
        scores = scores + addend
    scores = masked(scores, kind, sc, sz, base)
    top = jnp.max(scores, 0, keepdims=True)
    e = jnp.exp(scores - top)
    inv = 1.0 / jnp.sum(e, 0, keepdims=True)
    o_t = tn(v, (e * inv).astype(BF16))
    return o_t, top, inv


def attend_back(q, k, v, addend, kind, sc, sz, top, inv, do):
    scores = nt(k, q) * SCALE
    if addend is not None:
        scores = scores + addend
    scores = masked(scores, kind, sc, sz)
    p = jnp.exp(scores - top) * inv
    dv = nn(p.astype(BF16), do)
    dp = nt(v, do)
    ds = p * (dp - jnp.sum(p * dp, 0, keepdims=True))
    ds = jnp.where(allowed(kind, sc, sz), ds, 0.0).astype(BF16)
    dk = nn(ds, q) * SCALE
    dq = tn(k, ds) * SCALE
    return dq, dk, dv, ds


def head(ref, part, h, heads):
    start = (part * heads + h) * HDIM
    return ref[:, start : start + HDIM]


def run_heads(q_of, k_of, v_of, bias, kind, sc, sz, o_ref, st_ref, heads, base=0):
    outs = []
    for h in range(heads):
        o_t, top, inv = attend(
            q_of(h), k_of(h), v_of(h), None if bias is None else bias[h], kind, sc, sz, base
        )
        outs.append(o_t)
        st_ref[h : h + 1, :] = top
        st_ref[heads + h : heads + h + 1, :] = inv
    o_ref[...] = jnp.concatenate(outs, 0).T.astype(BF16)


def section1_far(sz, sc, nm, nth, w1, qkvf):
    qkvf[0 : sz.q2, :] = nt(nm[...], w1[...]).astype(BF16)
    qkvf[sz.q2 :, :] = nt(nth[...], w1[...]).astype(BF16)


def section1_near(sz, heads, sc, nm, nth, qkvf, w0, w1, wo0, wo1, bias, pm, pt, nvw, qkvv, ov, stv, qkvn, on, stn, ow):
    vp = sz.vp
    mine, theirs = window_permutation(sc, sz)
    nv = (nn(mine, nm[0:vp, :]) + nn(theirs, nth[0:vp, :])).astype(BF16)
    nvw[...] = nv
    qkvv[...] = nt(nv, w0[...]).astype(BF16)
    run_heads(
        lambda h: head(qkvv, 0, h, heads),
        lambda h: head(qkvv, 1, h, heads),
        lambda h: head(qkvv, 2, h, heads),
        bias, "window", sc, sz, ow, stv, heads,
    )
    ov[0:vp, :] = tn(mine, ow[...]).astype(BF16)
    ov[vp : 2 * vp, :] = tn(theirs, ow[...]).astype(BF16)
    give_patches(pm, pt, nn(ov[...], wo0[...]).astype(BF16), sz)
    qkvn[0 : sz.q1, :] = nt(nm[vp:, :], w1[...]).astype(BF16)
    qkvn[sz.q1 :, :] = nt(nth[vp:, :], w1[...]).astype(BF16)
    every = Rows([qkvn, qkvf])
    run_heads(
        lambda h: head(qkvn, 0, h, heads),
        lambda h: head(every, 1, h, heads),
        lambda h: head(every, 2, h, heads),
        None, "self", sc, sz, on, stn, heads,
    )
    give_near(pm, pt, nn(on[...], wo1[...]).astype(BF16), sz)


def section1_rest(sz, heads, sc, qkvn, qkvf, wo1, pm, pt, of, stf):
    every = Rows([qkvn, qkvf])
    run_heads(
        lambda h: head(qkvf, 0, h, heads),
        lambda h: head(every, 1, h, heads),
        lambda h: head(every, 2, h, heads),
        None, "self", sc, sz, of, stf, heads, 2 * sz.q1,
    )
    pm[...] = nn(of[0 : sz.q2, :], wo1[...]).astype(BF16)
    pt[...] = nn(of[sz.q2 :, :], wo1[...]).astype(BF16)


def section2_near(sz, heads, sc, nm, nth, w2, w3, qv, kvv, qn, kvn, on, stn):
    e = heads * HDIM
    v = patch_rows(nm, nth, sz)
    q = near_rows(nm, nth, sz)
    qv[...] = nt(v, w3[0:e, :]).astype(BF16)
    kvv[...] = nt(v, w2[e:, :]).astype(BF16)
    qn[...] = nt(q, w2[0:e, :]).astype(BF16)
    kvn[...] = nt(q, w3[e:, :]).astype(BF16)
    run_heads(
        lambda h: head(qn, 0, h, heads),
        lambda h: head(kvv, 0, h, heads),
        lambda h: head(kvv, 1, h, heads),
        None, "patch", sc, sz, on, stn, heads,
    )


def section2_far(sz, heads, sc, nm, nth, kvv, w2, w3, wo2, pm, pt, qf, kvf, of, stf):
    e = heads * HDIM
    x = jnp.concatenate([nm[...], nth[...]], 0)
    qf[...] = nt(x, w2[0:e, :]).astype(BF16)
    kvf[...] = nt(x, w3[e:, :]).astype(BF16)
    run_heads(
        lambda h: head(qf, 0, h, heads),
        lambda h: head(kvv, 0, h, heads),
        lambda h: head(kvv, 1, h, heads),
        None, "patch", sc, sz, of, stf, heads,
    )
    pm[...] = nn(of[0 : sz.q2, :], wo2[...]).astype(BF16)
    pt[...] = nn(of[sz.q2 :, :], wo2[...]).astype(BF16)


def section2_rest(sz, heads, sc, qv, kvn, kvf, on, wo2, wo3, pm, pt, ov, stv):
    every = Rows([kvn, kvf])
    give_near(pm, pt, nn(on[...], wo2[...]).astype(BF16), sz)
    run_heads(
        lambda h: head(qv, 0, h, heads),
        lambda h: head(every, 0, h, heads),
        lambda h: head(every, 1, h, heads),
        None, "question", sc, sz, ov, stv, heads,
    )
    give_patches(pm, pt, nn(ov[...], wo3[...]).astype(BF16), sz)


GELU_C = 0.7978845608028654
GELU_A = 0.044715


def section3(sz, layer, spans, nm, nth, wi, bi, wo, pm, pt, g, gp):
    count = g.shape[0] // 2
    for ref, out, base in ((nm, pm, 0), (nth, pt, count)):
        for lo, hi, e in spans:
            h = nn(ref[lo:hi, :], wi[e]) + bi[layer, e : e + 1, :]
            h2 = h * h
            t = jnp.tanh(GELU_C * h * (1.0 + GELU_A * h2))
            half_t = 0.5 + 0.5 * t
            act = (h * half_t).astype(BF16)
            slope = half_t + (0.5 * GELU_C) * h * (1.0 - t * t) * (1.0 + 3.0 * GELU_A * h2)
            g[base + lo : base + hi, :] = act
            gp[base + lo : base + hi, :] = slope.astype(BF16)
            out[lo:hi, :] = nn(act, wo[e]).astype(BF16)


def section3_back(sz, dm, dt, wi, wo, gp, pm, pt, dh):
    vp, half = sz.vp, sz.half
    for ref, out, base in ((dm, pm, 0), (dt, pt, half)):
        for lo, hi, e in ((0, vp, 0), (vp, half, 1)):
            dg = nt(ref[lo:hi, :], wo[e])
            d = (dg * gp[base + lo : base + hi, :].astype(F32)).astype(BF16)
            dh[base + lo : base + hi, :] = d
            out[lo:hi, :] = nt(d, wi[e]).astype(BF16)


def back_heads(q_of, k_of, v_of, bias, kind, sc, sz, st, do_of, ds_ref, heads):
    dqs, dks, dvs = [], [], []
    for h in range(heads):
        dq, dk, dv, ds = attend_back(
            q_of(h), k_of(h), v_of(h), None if bias is None else bias[h], kind, sc, sz,
            st[h : h + 1, :], st[heads + h : heads + h + 1, :], do_of(h),
        )
        dqs.append(dq)
        dks.append(dk)
        dvs.append(dv)
        if ds_ref is not None:
            ds_ref[h] = ds
    dq = jnp.concatenate(dqs, 0).T.astype(BF16)
    dkv = jnp.concatenate(dks + dvs, 1).astype(BF16)
    return dq, dkv


def stats(near, far):
    return jnp.concatenate([near[...], far[...]], 1)


def give_queries(mine, theirs, value, sz):
    give_near(mine, theirs, value[0 : 2 * sz.q1], sz)
    mine[sz.near :, :] = value[2 * sz.q1 : 2 * sz.q1 + sz.q2]
    theirs[sz.near :, :] = value[2 * sz.q1 + sz.q2 :]


def section2_back(
    sz, heads, sc, dm, dt, w2, w3, wo2, wo3, qq, kvv, stn, stf, qv, kvq, stv, pm, pt, dqq, dkvv, dqv, dkvq, doq, dov
):
    e = heads * HDIM
    doq[...] = nt(query_rows(dm, dt, sz), wo2[...]).astype(BF16)
    dov[...] = nt(patch_rows(dm, dt, sz), wo3[...]).astype(BF16)
    dq, dkv = back_heads(
        lambda h: head(qq, 0, h, heads),
        lambda h: head(kvv, 0, h, heads),
        lambda h: head(kvv, 1, h, heads),
        None, "patch", sc, sz, stats(stn, stf), lambda h: head(doq, 0, h, heads), None, heads,
    )
    dqq[...] = dq
    dkvv[...] = dkv
    dq, dkv = back_heads(
        lambda h: head(qv, 0, h, heads),
        lambda h: head(kvq, 0, h, heads),
        lambda h: head(kvq, 1, h, heads),
        None, "question", sc, sz, stv, lambda h: head(dov, 0, h, heads), None, heads,
    )
    dqv[...] = dq
    dkvq[...] = dkv
    give_queries(pm, pt, (nn(dqq[...], w2[0:e, :]) + nn(dkvq[...], w3[e:, :])).astype(BF16), sz)
    give_patches(pm, pt, (nn(dqv[...], w3[0:e, :]) + nn(dkvv[...], w2[e:, :])).astype(BF16), sz)


def section1_back(
    sz, heads, sc, dm, dt, w0, w1, wo0, wo1, bias, qkvv, stv, qkvq, stn, stf, pm, pt, dqkvv, dqkvq, ds, doq, dov
):
    vp = sz.vp
    e = heads * HDIM
    mine, theirs = window_permutation(sc, sz)
    do_m = nt(dm[0:vp, :], wo0[...]).astype(BF16)
    do_t = nt(dt[0:vp, :], wo0[...]).astype(BF16)
    dov[...] = (nn(mine, do_m) + nn(theirs, do_t)).astype(BF16)
    dq, dkv = back_heads(
        lambda h: head(qkvv, 0, h, heads),
        lambda h: head(qkvv, 1, h, heads),
        lambda h: head(qkvv, 2, h, heads),
        bias, "window", sc, sz, stv, lambda h: head(dov, 0, h, heads), ds, heads,
    )
    dqkvv[:, 0:e] = dq
    dqkvv[:, e:] = dkv
    dn = nn(dqkvv[...], w0[...]).astype(BF16)
    pm[0:vp, :] = tn(mine, dn).astype(BF16)
    pt[0:vp, :] = tn(theirs, dn).astype(BF16)
    doq[...] = nt(query_rows(dm, dt, sz), wo1[...]).astype(BF16)
    dq, dkv = back_heads(
        lambda h: head(qkvq, 0, h, heads),
        lambda h: head(qkvq, 1, h, heads),
        lambda h: head(qkvq, 2, h, heads),
        None, "self", sc, sz, stats(stn, stf), lambda h: head(doq, 0, h, heads), None, heads,
    )
    dqkvq[:, 0:e] = dq
    dqkvq[:, e:] = dkv
    give_queries(pm, pt, nn(dqkvq[...], w1[...]).astype(BF16), sz)


def kept_order(order):
    return sorted(range(1 << len(order)), key=lambda r: [(r >> k) & 1 for k in order])


def store_blocks(sc, store, col, value):
    keep, send, scr, order = store
    width = value.shape[1]
    value = value.astype(BF16)
    cols = slice(col, col + width)
    if send is None:
        keep[0, :, cols] = value
        return
    count, rows = keep.shape[0], keep.shape[1]
    scr[:, 0:width] = value
    for slot, relative in enumerate(kept_order(order)):
        owner = relative ^ sc[5]
        block = scr[pl.ds(pl.multiple_of(owner * rows, 16), rows), 0:width]
        if slot < count:
            keep[slot, :, cols] = block
        else:
            send[slot - count, :, cols] = block


def section3_weights(sz, sc, nm, nth, dm, dt, g, dh, db, out):
    vp, half = sz.vp, sz.half
    hid = dh.shape[1]
    for e, lo, hi in ((0, 0, vp), (1, vp, half)):
        into = tn(nm[lo:hi, :], dh[lo:hi, :]) + tn(nth[lo:hi, :], dh[half + lo : half + hi, :])
        away = tn(dm[lo:hi, :], g[lo:hi, :]) + tn(dt[lo:hi, :], g[half + lo : half + hi, :])
        out[:, e * hid : (e + 1) * hid] = into.astype(BF16)
        out[:, (2 + e) * hid : (3 + e) * hid] = away.astype(BF16)
        db[e : e + 1, :] = jnp.sum(dh[lo:hi, :].astype(F32), 0, keepdims=True) + jnp.sum(
            dh[half + lo : half + hi, :].astype(F32), 0, keepdims=True
        )


def section2_weights(sz, heads, sc, nm, nth, dm, dt, dqq, dkvv, dqv, dkvq, oq, ov, store):
    e = heads * HDIM
    nq, nv = query_rows(nm, nth, sz), patch_rows(nm, nth, sz)
    store_blocks(sc, store, 0, tn(nq, dqq[...]))
    store_blocks(sc, store, e, tn(nv, dkvv[...]))
    store_blocks(sc, store, 3 * e, tn(nv, dqv[...]))
    store_blocks(sc, store, 4 * e, tn(nq, dkvq[...]))
    store_blocks(sc, store, 6 * e, tn(query_rows(dm, dt, sz), oq[...]))
    store_blocks(sc, store, 7 * e, tn(patch_rows(dm, dt, sz), ov[...]))


def section1_weights(sz, heads, sc, nm, nth, dm, dt, nvw, dqkvv, dqkvq, oq, ov, store):
    e = heads * HDIM
    store_blocks(sc, store, 0, tn(nvw[...], dqkvv[...]))
    store_blocks(sc, store, 3 * e, tn(query_rows(nm, nth, sz), dqkvq[...]))
    store_blocks(sc, store, 6 * e, tn(patch_rows(dm, dt, sz), ov[...]))
    store_blocks(sc, store, 7 * e, tn(query_rows(dm, dt, sz), oq[...]))


def in_order(sz, chip, own, other, out):
    v, piece = sz.vpiece, sz.piece
    mine, theirs = own[...].astype(F32), other[...].astype(F32)
    first = jnp.where(chip == 0, mine, theirs)
    second = jnp.where(chip == 0, theirs, mine)
    out[0:v, :] = first[0:v]
    out[v : 2 * v, :] = second[0:v]
    out[2 * v : v + piece, :] = first[v:]
    out[v + piece :, :] = second[v:]


def norm_rows(x):
    center = x - jnp.mean(x, -1, keepdims=True)
    inv = lax.rsqrt(jnp.mean(center * center, -1, keepdims=True) + EPS)
    return center * inv, inv


def open_stream(sz, sc, own, other, scale, shift, x, n):
    layer = first = 0
    in_order(sz, sc[6], own, other, x)
    for lo, hi, e in ((0, sz.vp, 0), (sz.vp, sz.half, 1)):
        gain, bias = scale[first + e, layer : layer + 1, :], shift[first + e, layer : layer + 1, :]
        n[lo:hi, :] = (norm_rows(x[lo:hi, :])[0] * gain + bias).astype(BF16)


def open_grad(sz, sc, own, other, grad, dy, sums):
    in_order(sz, sc[6], own, other, grad)
    dy[...] = grad[...].astype(BF16)
    for lo, hi, e in ((0, sz.vp, 0), (sz.vp, sz.half, 1)):
        sums[4 + e : 5 + e, :] = jnp.sum(grad[lo:hi, :], 0, keepdims=True)


def add_norm(spans, layer, first, x, a, b, extra, scale, shift, y, n):
    for lo, hi, e in spans:
        gain, bias = scale[first + e, layer : layer + 1, :], shift[first + e, layer : layer + 1, :]
        value = x[lo:hi, :] + (a[lo:hi, :].astype(F32) + b[lo:hi, :].astype(F32))
        if extra is not None:
            value = value + extra[layer - 1, e : e + 1, :]
        y[lo:hi, :] = value
        n[lo:hi, :] = (norm_rows(value)[0] * gain + bias).astype(BF16)


def norm_back(sz, layer, first, d, a, b, x, scale, out, dy, sums):
    for lo, hi, e in ((0, sz.vp, 0), (sz.vp, sz.half, 1)):
        dn = a[lo:hi, :].astype(F32) + b[lo:hi, :].astype(F32)
        unit, inv = norm_rows(x[lo:hi, :])
        du = dn * scale[first + e, layer : layer + 1, :]
        dx = inv * (
            du
            - jnp.mean(du, -1, keepdims=True)
            - unit * jnp.mean(du * unit, -1, keepdims=True)
        )
        value = d[lo:hi, :] + dx
        out[lo:hi, :] = value
        dy[lo:hi, :] = value.astype(BF16)
        sums[e : e + 1, :] = jnp.sum(dn * unit, 0, keepdims=True)
        sums[2 + e : 3 + e, :] = jnp.sum(dn, 0, keepdims=True)
        sums[4 + e : 5 + e, :] = jnp.sum(value, 0, keepdims=True)


TABLE = SPAN * SPAN
TABLE_PAD = -(-TABLE // 128) * 128
CELLS_PAD = -(-SPAN * WIN // 128) * 128


def spread_matrix():
    cell = iota((TABLE_PAD, CELLS_PAD), 1)
    row = (cell * 171) >> 11
    place = row * SPAN + cell - row * WIN
    return ((iota((TABLE_PAD, CELLS_PAD), 0) == place) & (cell < SPAN * WIN)).astype(F32)


def table_bias(tables, out, spread, rows):
    spread[...] = spread_matrix()
    count = out.shape[0]
    for i in range(count):
        table = tables[i : i + 1, :]
        for b in range(WIN):
            at = i * WIN + b
            rows[at : at + 1, :] = pltpu.roll(table, (TABLE_PAD - (WIN - 1 - b)) % TABLE_PAD, 1)
    cells = jnp.dot(rows[...], spread[...], precision=lax.Precision.HIGHEST, preferred_element_type=F32)
    for a in range(WIN):
        moved = pltpu.roll(cells, (CELLS_PAD - WIN * (WIN - 1 - a)) % CELLS_PAD, 1)
        for i in range(count):
            out[i, WIN * a : WIN * (a + 1), :] = moved[WIN * i : WIN * (i + 1), 0 : WIN * WIN]


def table_grad(ds, spread, out):
    heads = ds.shape[0]
    rows = jnp.zeros((WIN, CELLS_PAD - WIN * WIN), F32)
    every = []
    for h in range(heads):
        grad = ds[h].astype(F32)
        cells = jnp.zeros((WIN, CELLS_PAD), F32)
        for a in range(WIN):
            part = jnp.concatenate([grad[WIN * a : WIN * (a + 1), :], rows], 1)
            cells = cells + pltpu.roll(part, WIN * (WIN - 1 - a), 1)
        every.append(cells)
    places = lax.dot_general(
        jnp.concatenate(every, 0),
        spread[...],
        (((1,), (1,)), ((), ())),
        precision=lax.Precision.HIGHEST,
        preferred_element_type=F32,
    )
    for h in range(heads):
        total = jnp.zeros((1, TABLE_PAD), F32)
        for b in range(WIN):
            total = total + pltpu.roll(places[h * WIN + b : h * WIN + b + 1, :], WIN - 1 - b, 1)
        out[h : h + 1, :] = total


def collect(layers, heads, *refs):
    out = refs[-1]
    out[...] = jnp.zeros(out.shape, F32)
    row = 0
    for layer in range(layers):
        sums1, sums2, sums3, after = refs[6 * layer : 6 * layer + 4]
        for ref, lo, count in ((sums1, 0, 4), (sums2, 0, 4), (sums3, 0, 4), (after, 4, 2)):
            out[row : row + count, :] = ref[lo : lo + count, :]
            row += count
    for layer in range(layers):
        db, table = refs[6 * layer + 4 : 6 * layer + 6]
        out[row : row + 2, :] = db[...]
        row += 2
        out[row : row + heads, 0:TABLE_PAD] = table[0:heads, :]
        row += heads


def deal(layers, heads, rows, scale, shift, out_bias, in_bias, rel):
    for layer in range(layers):
        at = 14 * layer
        for section in range(3):
            for e in range(2):
                scale[2 * section + e, layer : layer + 1, :] = rows[at + 4 * section + e : at + 4 * section + e + 1, :]
                row = at + 4 * section + 2 + e
                shift[2 * section + e, layer : layer + 1, :] = rows[row : row + 1, :]
        out_bias[layer] = rows[at + 12 : at + 14, :]
        at = 14 * layers + (2 + heads) * layer
        in_bias[layer] = rows[at : at + 2, :]
        for h in range(heads):
            rel[h, layer : layer + 1, :] = rows[at + 2 + h : at + 3 + h, 0:TABLE]


def finish_mlp(layers, *refs):
    up, down = refs[layers:]
    hid = up.shape[3]
    for layer in range(layers):
        total = refs[layer][...].astype(F32)
        for e in range(2):
            up[layer, e] = total[:, e * hid : (e + 1) * hid]
            down[layer, e] = total[:, (2 + e) * hid : (3 + e) * hid]


def finish_attn(layers, *refs):
    d_in, d_out = refs[8 * layers :]
    e = d_in.shape[4]
    for layer in range(layers):
        for pair in range(2):
            first = 8 * layer + 4 * pair
            total = sum(r[...].astype(F32) for r in refs[first : first + 4])
            for which in range(2):
                for c in range(3):
                    col = (3 * which + c) * e
                    d_in[layer, 2 * pair + which, c] = total[:, col : col + e]
                col = (6 + which) * e
                d_out[layer, 2 * pair + which] = total[:, col : col + e].T


def on_device(
    dp_size,
    visual,
    queries,
    valid_windows,
    answer_start,
    shifts,
    norm_scale,
    norm_shift,
    attn_in,
    attn_out,
    rel_bias,
    mlp_in,
    mlp_in_bias,
    mlp_out,
    mlp_out_bias,
    grad_visual_out,
    grad_query_out,
):
    layers, width = attn_in.shape[0], attn_in.shape[2]
    edev = attn_in.shape[4]
    heads = edev // HDIM
    hid = mlp_in.shape[3]
    sz = Sizes(4 * visual.shape[1], 4 * queries.shape[1])
    half, vp, qh = sz.half, sz.vp, sz.qh
    vq, qq_ = sz.vquart, sz.qquart
    t_index = lax.axis_index("tensor")
    d_index = lax.axis_index("dp")
    core, chip = t_index % 2, t_index // 2
    swap = [(i, i ^ 1) for i in range(4)]
    cross = [(i, i ^ 2) for i in range(4)]
    block_rows = width // dp_size
    halving = dp_size > 1 and dp_size & (dp_size - 1) == 0 and block_rows % 16 == 0
    bits = dp_size.bit_length() - 1

    def scalars(layer):
        on = layer % 2
        values = [core, answer_start[0], shifts[0, 0] * on, shifts[0, 1] * on, valid_windows[0, 0], d_index, chip, 0]
        return jnp.stack(values).astype(jnp.int32)

    w_in = attn_in.transpose(0, 1, 3, 4, 2).reshape(layers, 4, 3 * edev, width)
    scale, shift = norm_scale.transpose(1, 0, 2), norm_shift.transpose(1, 0, 2)

    def packed(own_v, own_q):
        pad = jnp.zeros((sz.vpiece - vq, width), own_v.dtype)
        return jnp.concatenate([own_v, pad, own_q], 0)

    def piece_of(rows, place):
        v = jnp.where(place == 0, rows[0 : sz.vpiece], rows[sz.vpiece : vp])
        q = jnp.where(place == 0, rows[vp : vp + qq_], rows[vp + qq_ :])
        return jnp.concatenate([v, q], 0)

    def core_swap(x):
        if isinstance(x, list):
            return [core_swap(p) for p in x]
        return lax.ppermute(x, "tensor", swap)

    def across(x):
        return lax.ppermute(x, "tensor", cross)

    def pair_sum(mine, theirs):
        got = core_swap(theirs)
        if not isinstance(got, list):
            return (mine.astype(F32) + got.astype(F32)).astype(BF16)

        def body(a, b, out):
            out[...] = (a[...].astype(F32) + b[...].astype(F32)).astype(BF16)

        return call(body, [shaped(mine.shape)], [], [mine, got], name="pair_sum")[0]

    def pair(x):
        return x, core_swap(x)

    far = half - sz.near
    near_bf, far_bf = shaped((sz.near, width)), shaped((far, width))

    def halved(rows):
        first = -(-rows // 32) * 16
        return [shaped((first, width)), shaped((rows - first, width))]

    near_two, far_two = halved(sz.near), halved(far)
    rows_bf = [shaped((half, width))]
    rows_f = shaped((half, width), F32)
    near_spans = ((0, vp, 0), (vp, sz.near, 1))
    far_spans = ((0, far, 1),)

    def natural(near_part, far_part):
        return Rows(
            [
                (near_part, 0, sz.near),
                (far_part, 0, far),
                (near_part, sz.near, 2 * sz.near),
                (far_part, far, 2 * far),
            ]
        )

    own = packed(visual[0], queries[0])
    other = lax.ppermute(own, "tensor", cross)
    tables = jnp.pad(rel_bias.reshape(layers * heads, TABLE), ((0, 0), (0, TABLE_PAD - TABLE)))
    bias_all, spread = call(
        table_bias,
        [shaped((layers * heads, sz.vis, sz.vis), F32), shaped((TABLE_PAD, CELLS_PAD), F32)],
        [],
        [tables],
        name="table_bias",
        scratch=[pltpu.VMEM((layers * heads * WIN, TABLE_PAD), F32)],
    )
    bias_all = bias_all.reshape(layers, heads, sz.vis, sz.vis)
    scal = [scalars(layer) for layer in range(layers)]
    own_grad = packed(grad_visual_out[0], grad_query_out[0])
    rounded_grad = lax.reduce_precision(own_grad, 8, 7)

    def next_norm(spans, x, a, b, layer, first, extra=False):
        args = [x, a, b] + ([mlp_out_bias] if extra else []) + [scale, shift]

        def body(x, a, b, *rest):
            if not extra:
                rest = (None,) + rest
            add_norm(spans, layer, first, x, a, b, *rest)

        return call(body, [shaped(x.shape, F32), halved(x.shape[0])], [], args, name="norm")

    fetched = {}

    def fetch(layer, section, after):
        if section == 3:
            arrays = [mlp_in, mlp_out]
            blocks = [(0, (layer,)), (1, (layer,))]
        else:
            arrays = [w_in, attn_out]
            first = 2 * (section - 1)
            blocks = [(0, (layer, first)), (0, (layer, first + 1)), (1, (layer, first)), (1, (layer, first + 1))]
        arrays = tie(after, arrays)[1]
        outs = [shaped(arrays[k].shape[len(lead) :]) for k, lead in blocks]

        def body(one, two, *refs):
            copies = [
                pltpu.make_async_copy((one, two)[k].at[lead], refs[j], refs[-1].at[j])
                for j, (k, lead) in enumerate(blocks)
            ]
            for copy in copies:
                copy.start()
            for copy in copies:
                copy.wait()

        fetched[layer, section] = pl.pallas_call(
            body,
            out_shape=outs,
            in_specs=[pl.BlockSpec(memory_space=pltpu.HBM)] * 2,
            out_specs=[pl.BlockSpec(memory_space=pltpu.VMEM)] * len(outs),
            scratch_shapes=[pltpu.SemaphoreType.DMA((len(outs),))],
            compiler_params=pltpu.CompilerParams(vmem_limit_bytes=VMEM_LIMIT),
            name="fetch",
        )(*arrays)

    def fetch_beside(layer, section, a, b):
        fetch(layer, section, a)
        b, fetched[layer, section] = tie(b, fetched[layer, section])
        return b

    fetch(0, 1, own)
    other, fetched[0, 1] = tie(other, fetched[0, 1])
    (x_near, x_far), pieces = call(
        lambda *r: open_stream(sz, *r),
        [[shaped((sz.near, width), F32), shaped((far, width), F32)], near_two + far_two],
        scal[0:1],
        [own, other, scale, shift],
        name="open_stream",
    )
    n_near, n_far = pieces[0:2], pieces[2:4]

    saved = []
    for layer in range(layers):
        sc = scal[layer]
        w0, w1, wo0, wo1 = fetched[layer, 1]
        if layer > 0:
            got_far, _ = tie(got_far, kept_near)
            got_far, fetched[layer, 1] = tie(got_far, fetched[layer, 1])
            w0, w1, wo0, wo1 = fetched[layer, 1]
            x_far, n_far = next_norm(far_spans, x_far, kept_far, got_far, layer, 0, True)
        t_far = core_swap(n_far)
        (qkvf,) = call(
            lambda *r: section1_far(sz, *r), [shaped((2 * far, 3 * edev))], [sc], [n_far, t_far, w1], name="section1"
        )
        if layer > 0:
            got_near, qkvf = tie(got_near, qkvf)
            x_near, n_near = next_norm(near_spans, x_near, kept_near, got_near, layer, 0, True)
        t_near = core_swap(n_near)
        if layer == 0:
            sent_grad, _ = tie(rounded_grad.astype(BF16), t_far)
            other_grad = across(sent_grad)
            other_grad, qkvf = tie(other_grad, qkvf)
        x1, n1, t1 = [x_near, x_far], n_near + n_far, t_near + t_far
        pm, pt, nvw, qkvv, ov, stv, qkvn, on, stn = call(
            lambda *r: section1_near(sz, heads, *r),
            [
                near_bf,
                near_two,
                shaped((sz.vis, width)),
                shaped((sz.vis, 3 * edev)),
                shaped((2 * vp, edev)),
                shaped((8, sz.vis), F32),
                shaped((2 * sz.q1, 3 * edev)),
                shaped((2 * sz.q1, edev)),
                shaped((8, 2 * sz.q1), F32),
            ],
            [sc],
            [n_near, t_near, qkvf, w0, w1, wo0, wo1, Part(bias_all, layer)],
            name="section1",
            scratch=[pltpu.VMEM((sz.vis, edev), BF16)],
        )
        kept_near = pair_sum(pm, pt)
        got_near = across(kept_near)
        _, later = tie(kept_near, qkvn)
        pm, pt, of, stf = call(
            lambda *r: section1_rest(sz, heads, *r),
            [far_bf, far_two, shaped((2 * far, edev)), shaped((8, 2 * far), F32)],
            [sc],
            [later, qkvf, wo1],
            name="section1",
        )
        saved1 = (x1, n1, t1, nvw, qkvv, ov, stv, [qkvn, qkvf], [on, of], stn, stf)
        kept_far = pair_sum(pm, pt)
        got_far = across(kept_far)

        fetch(layer, 2, kept_near)
        got_near, fetched[layer, 2], _ = tie(got_near, fetched[layer, 2], kept_far)
        if layer == 0:
            other_grad, sent_grad, _ = tie(other_grad, sent_grad, kept_far)
            grad, dy, grad_sums = call(
                lambda *r: open_grad(sz, *r),
                [rows_f, rows_bf, shaped((8, width), F32)],
                scal[0:1],
                [sent_grad, other_grad],
                name="open_grad",
            )
            got_near, grad, dy = tie(got_near, grad, dy)
        w2, w3, wo2, wo3 = fetched[layer, 2]
        x_near, n_near = next_norm(near_spans, x_near, kept_near, got_near, layer, 2)
        t_near = core_swap(n_near)
        qv, kvv, qn, kvn, on, stn = call(
            lambda *r: section2_near(sz, heads, *r),
            [
                shaped((2 * vp, edev)),
                shaped((2 * vp, 2 * edev)),
                shaped((2 * sz.q1, edev)),
                shaped((2 * sz.q1, 2 * edev)),
                shaped((2 * sz.q1, edev)),
                shaped((8, 2 * sz.q1), F32),
            ],
            [sc],
            [n_near, t_near, w2, w3],
            name="section2",
        )
        got_far, kvv = tie(got_far, kvv)
        x_far, n_far = next_norm(far_spans, x_far, kept_far, got_far, layer, 2)
        t_far = core_swap(n_far)
        pm, pt, qf, kvf, of, stf = call(
            lambda *r: section2_far(sz, heads, *r),
            [
                far_bf,
                far_two,
                shaped((2 * far, edev)),
                shaped((2 * far, 2 * edev)),
                shaped((2 * far, edev)),
                shaped((8, 2 * far), F32),
            ],
            [sc],
            [n_far, t_far, kvv, w2, w3, wo2],
            name="section2",
        )
        x2, n2, t2 = [x_near, x_far], n_near + n_far, t_near + t_far
        kept_far = pair_sum(pm, pt)
        got_far = across(kept_far)
        _, later = tie(kept_far, qv)
        pm, pt, ov, stv = call(
            lambda *r: section2_rest(sz, heads, *r),
            [near_bf, near_two, shaped((2 * vp, edev)), shaped((8, 2 * vp), F32)],
            [sc],
            [later, kvn, kvf, on, wo2, wo3],
            name="section2",
        )
        saved2 = (x2, n2, t2, [qn, qf], kvv, [on, of], stn, stf, qv, [kvn, kvf], ov, stv)
        kept_near = pair_sum(pm, pt)
        got_near = across(kept_near)

        fetch(layer, 3, kept_far)
        got_far, fetched[layer, 3], _ = tie(got_far, fetched[layer, 3], kept_near)
        up, down = fetched[layer, 3]

        def feed_forward(spans, n, t):
            rows = sum(p.shape[0] for p in n)
            return call(
                lambda *r: section3(sz, layer, spans, *r),
                [shaped((rows, width)), halved(rows)] + [shaped((2 * rows, hid))] * 2,
                [],
                [n, t, up, mlp_in_bias, down],
                name="section3",
            )

        x_far, n_far = next_norm(far_spans, x_far, kept_far, got_far, layer, 4)
        t_far = core_swap(n_far)
        pm, pt, act_far, slope_far = feed_forward(far_spans, n_far, t_far)
        kept_far = pair_sum(pm, pt)
        if layer + 1 < layers:
            got_far = across(kept_far)
        got_near, _ = tie(got_near, kept_far)
        x_near, n_near = next_norm(near_spans, x_near, kept_near, got_near, layer, 4)
        t_near = core_swap(n_near)
        pm, pt, act_near, slope_near = feed_forward(near_spans, n_near, t_near)
        kept_near = pair_sum(pm, pt)
        if layer + 1 < layers:
            got_near = across(kept_near)
            fetch(layer + 1, 1, kept_far)
        x3, n3, t3 = [x_near, x_far], n_near + n_far, t_near + t_far
        saved3 = (x3, n3, t3, (act_near, act_far), (slope_near, slope_far))
        saved.append((saved1, saved2, saved3))
    stream = jnp.concatenate([x_near, x_far], 0)
    last = jnp.concatenate([kept_near, kept_far], 0)
    away = lax.ppermute(piece_of(last, 1 - chip), "tensor", cross)
    out = piece_of(stream, chip) + (piece_of(last, chip).astype(F32) + away.astype(F32))
    out_v = (out[0:vq] + mlp_out_bias[layers - 1, 0]).astype(BF16)
    out_q = (out[sz.vpiece :] + mlp_out_bias[layers - 1, 1]).astype(BF16)

    bias_sums = grad_sums

    def whole_sum(rows):
        return lax.psum_scatter(rows, "dp", scatter_dimension=0, tiled=True)

    def shares(mine, theirs):
        kept = [pair_sum(m, t) for m, t in zip(mine, theirs)]
        return kept, [across(k) for k in kept]

    class Reduction:
        def __init__(self, outs, order):
            self.order = order
            if halving:
                self.parts, self.step = [outs[0]], 0
                self.ready = outs[1]
                self.move()
            else:
                self.sum = whole_sum(outs[0][0])
                self.step = bits

        def move(self):
            bit = 1 << self.order[self.step]
            got = lax.ppermute(self.ready, "dp", [(i, i ^ bit) for i in range(dp_size)])
            self.parts.append(got)
            self.step += 1

        def advance(self):
            count = 1 << (bits - 1 - self.step)
            self.ready = sum(p[count : 2 * count].astype(F32) for p in self.parts).astype(BF16)
            self.move()

        def pieces(self):
            if not halving:
                zero = jnp.zeros_like(self.sum)
                return [self.sum, zero, zero, zero]
            lead = [Part(p, 0) for p in self.parts]
            while len(lead) < 4:
                lead.append(jnp.zeros(lead[0].rest, BF16))
            return lead

    def close(grad, a, b, kept, layer, first):
        return call(
            lambda *r: norm_back(sz, layer, first, *r),
            [rows_f, rows_bf, shaped((8, width), F32)],
            [],
            [grad, a, b, kept[0], scale],
            name="norm_back",
        )

    straight = tuple(range(bits))
    turned = straight[1:] + straight[:1]

    def weights(body, extra_outs, orders, columns, args, wide, name):
        outs = []
        for _ in orders:
            if halving:
                outs += [shaped((dp_size // 2, block_rows, columns))] * 2
            else:
                outs += [shaped((1, width, columns))]
        lead = 1 + len(args) + len(extra_outs)
        each = 2 if halving else 1

        def wrapped(*refs):
            stores = []
            for k, order in enumerate(orders):
                given = refs[lead + k * each : lead + (k + 1) * each]
                stores.append((given[0], given[1] if halving else None, refs[-1], order))
            body(*refs[:lead], *stores)

        got = call(
            wrapped,
            list(extra_outs) + outs,
            [scal[0]],
            args,
            name=name,
            scratch=[pltpu.VMEM((width, wide), BF16)],
        )
        extra, rest = got[: len(extra_outs)], got[len(extra_outs) :]
        return extra, [Reduction(rest[k * each : (k + 1) * each], order) for k, order in enumerate(orders)]

    reductions = []
    feeds = []
    arrivals = {}
    if halving and bits == 3 and layers == 2:
        arrivals = {2: [0], 3: [0, 1], 4: [1], 5: [2]}

    def window(kept, args):
        return tie(kept, list(args))[1]

    def seal(index, got, extra, made):
        due = [reductions[g] for g in arrivals.get(index, ()) if reductions[g].step < bits]
        firsts = [r.parts[0] for r in made] if halving else []
        extra, firsts, parts = tie(list(extra), firsts, [r.parts for r in due])
        for r, p in zip(due, parts):
            r.parts = list(p)
            r.advance()
        got, extra, firsts = tie(got, extra, firsts)
        for r, part in zip(made, firsts):
            r.parts[0] = part
        reductions.extend(made)
        return got, extra

    grads = [None] * layers
    index = 0
    for layer in reversed(range(layers)):
        sc = scal[layer]
        kept1, kept2, kept3 = saved[layer]
        dm, dt = pair(dy)
        _, nm, nth, act, slope = kept3
        up, down = fetched[layer, 3]
        pm, pt, dh = call(
            lambda dm, dt, wi, wo, near_part, far_part, *r: section3_back(
                sz, dm, dt, wi, wo, natural(near_part, far_part), *r
            ),
            [rows_bf, rows_bf, shaped((2 * half, hid))],
            [],
            [dm, dt, up, down, *slope],
            name="section3_back",
        )
        a, b = shares(pm, pt)
        args = window(a, [nm, nth, dm, dt, *act, dh])
        db, feed = call(
            lambda sc, nm, nth, dm, dt, near_part, far_part, *r: section3_weights(
                sz, sc, nm, nth, dm, dt, natural(near_part, far_part), *r
            ),
            [shaped((2, hid), F32), shaped((width, 4 * hid))],
            [sc],
            args,
            name="section3_weights",
        )
        feeds.append(whole_sum(feed))
        b, (db,) = seal(index, b, [db], [])
        index += 1
        out_bias_sums = bias_sums
        grad, dy, sums3 = close(grad, a, b, kept3, layer, 4)

        dm, dt = pair(dy)
        _, nm, nth, qq, kvv, oq, stn, stf, qv, kvq, ov, stv = kept2
        part = call(
            lambda *r: section2_back(sz, heads, *r),
            [
                rows_bf,
                rows_bf,
                shaped((sz.qlen, edev)),
                shaped((2 * vp, 2 * edev)),
                shaped((2 * vp, edev)),
                shaped((sz.qlen, 2 * edev)),
            ],
            [sc],
            [
                dm, dt, *fetched[layer, 2],
                qq, kvv, stn, stf, qv, kvq, stv,
            ],
            name="section2_back",
            scratch=[pltpu.VMEM((sz.qlen, edev), BF16), pltpu.VMEM((2 * vp, edev), BF16)],
        )
        a, b = shares(part[0], part[1])
        args = window(a, [nm, nth, dm, dt, part[2], part[3], part[4], part[5], oq, ov])
        _, made = weights(
            lambda *r: section2_weights(sz, heads, *r), [], [straight], 8 * edev, args, 2 * edev, "section2_weights"
        )
        b, _ = seal(index, b, [], made)
        index += 1
        grad, dy, sums2 = close(grad, a, b, kept2, layer, 2)

        dm, dt = pair(dy)
        _, nm, nth, nvw, qkvv, ov, stv, qkvq, oq, stn, stf = kept1
        part = call(
            lambda *r: section1_back(sz, heads, *r),
            [
                rows_bf,
                rows_bf,
                shaped((sz.vis, 3 * edev)),
                shaped((sz.qlen, 3 * edev)),
                shaped((heads, sz.vis, sz.vis)),
            ],
            [sc],
            [
                dm, dt, *fetched[layer, 1],
                Part(bias_all, layer), qkvv, stv, qkvq, stn, stf,
            ],
            name="section1_back",
            scratch=[pltpu.VMEM((sz.qlen, edev), BF16), pltpu.VMEM((sz.vis, edev), BF16)],
        )
        a, b = shares(part[0], part[1])
        args = window(a, [nm, nth, dm, dt, nvw, part[2], part[3], oq, ov])
        _, made = weights(
            lambda *r: section1_weights(sz, heads, *r), [], [straight], 8 * edev, args, 3 * edev, "section1_weights"
        )
        b, _ = seal(index, b, [], made)
        (table,) = call(table_grad, [shaped((8, TABLE_PAD), F32)], [], [part[4], spread], name="table_grad")
        index += 1
        grad, dy, sums1 = close(grad, a, b, kept1, layer, 0)
        bias_sums = sums1
        grads[layer] = (sums1, sums2, sums3, out_bias_sums, db, table)

    if halving:
        for r in reductions:
            while r.step < bits:
                r.advance()

    own_total = piece_of(grad, chip) + (own_grad - rounded_grad)
    grad_v, grad_q = own_total[0:vq], own_total[sz.vpiece :]

    def summed(x, axis, size, steps):
        for bit in steps:
            x = x + lax.ppermute(x, axis, [(i, i ^ bit) for i in range(size)])
        return x

    per_norm = 14 * layers
    count = -(-(per_norm + (2 + heads) * layers) // 8) * 8
    (rows,) = call(
        lambda *r: collect(layers, heads, *r),
        [shaped((count, width), F32)],
        [],
        [x for g in grads for x in g],
        name="collect",
    )
    twice = lax.ppermute(rows, "tensor", swap)
    rows = rows + jnp.where(iota((count, 1), 0) < per_norm, twice, 0.0)
    rows = summed(rows, "dp", dp_size, [1 << k for k in range(bits)])
    scale_total, shift_total, out_bias_total, in_bias_total, rel_total = call(
        lambda *r: deal(layers, heads, *r),
        [shaped((6, layers, width), F32)] * 2
        + [shaped((layers, 2, width), F32), shaped((layers, 2, hid), F32), shaped((heads, layers, TABLE), F32)],
        [],
        [rows],
        name="deal",
    )

    d_up, d_down = call(
        lambda *r: finish_mlp(layers, *r),
        [shaped((layers, 2, block_rows, hid), F32)] * 2,
        [],
        feeds[::-1],
        name="finish_mlp",
    )
    sums = [reductions[2 * (layers - 1 - layer) : 2 * (layers - layer)] for layer in range(layers)]
    d_in, d_out = call(
        lambda *r: finish_attn(layers, *r),
        [shaped((layers, 4, 3, block_rows, edev), F32), shaped((layers, 4, edev, block_rows), F32)],
        [],
        [p for r in sums for p in r[1].pieces() + r[0].pieces()],
        name="finish_attn",
    )
    return (
        out_v[None],
        out_q[None],
        grad_v[None],
        grad_q[None],
        scale_total.transpose(1, 0, 2),
        shift_total.transpose(1, 0, 2),
        d_in.transpose(0, 1, 3, 2, 4),
        d_out,
        rel_total.transpose(1, 0, 2),
        d_up,
        in_bias_total,
        d_down.transpose(0, 1, 3, 2),
        out_bias_total,
    )


def solution(mesh):
    dp_size = mesh.shape["dp"]
    return jax.shard_map(
        lambda *args: on_device(dp_size, *args),
        mesh=mesh,
        in_specs=(
            P("dp", "tensor", None),
            P("dp", "tensor", None),
            P("dp", None),
            P("dp"),
            P("dp", None),
            P(),
            P(),
            P(None, None, None, None, "tensor"),
            P(None, None, "tensor", None),
            P(None, "tensor", None),
            P(None, None, None, "tensor"),
            P(None, None, "tensor"),
            P(None, None, "tensor", None),
            P(),
            P("dp", "tensor", None),
            P("dp", "tensor", None),
        ),
        out_specs=(
            P("dp", "tensor", None),
            P("dp", "tensor", None),
            P("dp", "tensor", None),
            P("dp", "tensor", None),
            P(),
            P(),
            P(None, None, "dp", None, "tensor"),
            P(None, None, "tensor", "dp"),
            P(None, "tensor", None),
            P(None, None, "dp", "tensor"),
            P(None, None, "tensor"),
            P(None, None, "tensor", "dp"),
            P(),
        ),
        check_vma=False,
    )
```

```python
import jax
import jax.numpy as jnp
from jax import lax
from jax.experimental import pallas as pl
from jax.experimental.pallas import tpu as pltpu
from jax.sharding import PartitionSpec as P

HDIM = 64
WIN = 12
SPAN = 2 * WIN - 1
EPS = 1e-05
NEG = -1000000000.0
OUT = -1e30
F32 = jnp.float32
BF16 = jnp.bfloat16
VMEM_LIMIT = 20 * 2**20


def nn(a, b):
    return lax.dot_general(a, b, (((1,), (0,)), ((), ())), preferred_element_type=F32)


def nt(a, b):
    return lax.dot_general(a, b, (((1,), (1,)), ((), ())), preferred_element_type=F32)


def tn(a, b):
    return lax.dot_general(a, b, (((0,), (0,)), ((), ())), preferred_element_type=F32)


class Part:
    def __init__(self, array, *lead):
        self.array, self.lead = array, lead
        self.rest = array.shape[len(lead) :]
        self.dtype = array.dtype
        self.size = 1
        for n in self.rest:
            self.size *= n


class Arriving:
    def __init__(self, ref, copy):
        self.ref, self.copy, self.shape = ref, copy, ref.shape

    def __getitem__(self, at):
        if self.copy is not None:
            self.copy.wait()
            self.copy = None
        return self.ref[at]


class Rows:
    def __init__(self, refs):
        self.spans = [r if isinstance(r, tuple) else (r, 0, r.shape[0]) for r in refs]

    def pieces(self, at):
        rows = at[0] if isinstance(at, tuple) else slice(None)
        total = sum(end - start for _, start, end in self.spans)
        lo, hi, _ = rows.indices(total)
        base = 0
        for ref, start, end in self.spans:
            first, last = max(lo - base, 0), min(hi - base, end - start)
            if first < last:
                yield ref, start + first, start + last, base + first - lo
            base += end - start

    def __getitem__(self, at):
        cols = at[1] if isinstance(at, tuple) else slice(None)
        parts = [ref[first:last, cols] for ref, first, last, _ in self.pieces(at)]
        return parts[0] if len(parts) == 1 else jnp.concatenate(parts, 0)

    def __setitem__(self, at, value):
        for ref, first, last, place in self.pieces(at):
            ref[first:last, :] = value[place : place + last - first, :]


def call(body, outs, scalars, args, name=None, scratch=()):
    vmem = pl.BlockSpec(memory_space=pltpu.VMEM)
    smem = pl.BlockSpec(memory_space=pltpu.SMEM)
    hbm = pl.BlockSpec(memory_space=pltpu.HBM)
    flat = [x for a in args for x in (a if isinstance(a, list) else [a])]
    flat_outs = [x for o in outs for x in (o if isinstance(o, list) else [o])]
    parts = [i for i, a in enumerate(flat) if isinstance(a, Part)]
    specs = [hbm if isinstance(a, Part) else vmem for a in flat]
    arrays = [a.array if isinstance(a, Part) else a for a in flat]
    landing = [pltpu.VMEM(flat[i].rest, flat[i].dtype) for i in parts]
    if parts:
        landing.append(pltpu.SemaphoreType.DMA((len(parts),)))
    first, end = len(scalars), len(scalars) + len(flat) + len(flat_outs) + len(scratch)

    def wrapped(*refs):
        refs = list(refs)
        buffers = refs[end:]
        coming = []
        for k, i in enumerate(parts):
            source = refs[first + i]
            if flat[i].lead:
                source = source.at[flat[i].lead]
            copy = pltpu.make_async_copy(source, buffers[k], buffers[-1].at[k])
            copy.start()
            coming.append(Arriving(buffers[k], copy))
            refs[first + i] = coming[-1]
        given = iter(refs[:end])
        grouped = [next(given) for _ in scalars]
        for x in list(args) + list(outs):
            grouped.append(Rows([next(given) for _ in x]) if isinstance(x, list) else next(given))
        body(*grouped, *given)
        for piece in coming:
            if piece.copy is not None:
                piece.copy.wait()

    got = iter(
        pl.pallas_call(
            wrapped,
            out_shape=tuple(flat_outs),
            in_specs=[smem] * len(scalars) + specs,
            out_specs=tuple(vmem for _ in flat_outs),
            scratch_shapes=list(scratch) + landing,
            compiler_params=pltpu.CompilerParams(vmem_limit_bytes=VMEM_LIMIT),
            cost_estimate=pl.CostEstimate(flops=1, bytes_accessed=1, transcendentals=0),
            name=name,
        )(*scalars, *arrays)
    )
    return [[next(got) for _ in o] if isinstance(o, list) else next(got) for o in outs]


def tie(*groups):
    return lax.optimization_barrier(groups)


def shaped(shape, dtype=BF16):
    return jax.ShapeDtypeStruct(shape, dtype)


class Sizes:
    def __init__(self, vis, qlen):
        self.vis, self.qlen = vis, qlen
        self.qh = qlen // 2
        self.vquart, self.qquart = vis // 4, qlen // 4
        self.vpiece = -(-self.vquart // 8) * 8
        self.vp = 2 * self.vpiece
        self.piece = self.vpiece + self.qquart
        self.half = 2 * self.piece
        self.near = self.half // 2
        self.q1 = self.near - self.vp
        self.q2 = self.half - self.near


def iota(shape, dim):
    return lax.broadcasted_iota(jnp.int32, shape, dim)


def div12(x):
    return (x * 171) >> 11


def patch_of(index, core, sz):
    second = (index >= sz.vp).astype(jnp.int32)
    row = index - second * sz.vp
    half = second + core - 2 * second * core
    late = (row >= sz.vpiece).astype(jnp.int32)
    row = row - late * sz.vpiece
    return jnp.where(row < sz.vquart, row + (2 * late + half) * sz.vquart, -1)


def query_of(index, core, sz):
    far = (index >= 2 * sz.q1).astype(jnp.int32)
    row = index - far * 2 * sz.q1
    size = sz.q1 + far * (sz.q2 - sz.q1)
    second = (row >= size).astype(jnp.int32)
    row = row - second * size + far * sz.q1
    half = second + core - 2 * second * core
    return row + jnp.where(row >= sz.qquart, sz.qquart, 0) + half * sz.qquart


def patch_rows(mine, theirs, sz):
    return jnp.concatenate([mine[0 : sz.vp, :], theirs[0 : sz.vp, :]], 0)


def near_rows(mine, theirs, sz):
    return jnp.concatenate([mine[sz.vp : sz.near, :], theirs[sz.vp : sz.near, :]], 0)


def far_rows(mine, theirs, sz):
    return jnp.concatenate([mine[sz.near :, :], theirs[sz.near :, :]], 0)


def query_rows(mine, theirs, sz):
    return jnp.concatenate([near_rows(mine, theirs, sz), far_rows(mine, theirs, sz)], 0)


def give_patches(mine, theirs, value, sz):
    mine[0 : sz.vp, :] = value[0 : sz.vp]
    theirs[0 : sz.vp, :] = value[sz.vp :]


def give_near(mine, theirs, value, sz):
    mine[sz.vp : sz.near, :] = value[0 : sz.q1]
    theirs[sz.vp : sz.near, :] = value[sz.q1 : 2 * sz.q1]


def window_permutation(sc, sz):
    core, down, right = sc[0], sc[2], sc[3]
    place = iota((sz.vis, sz.vp), 0)
    a = div12(place)
    b = place - a * WIN
    a = a + down
    b = b + right
    a = jnp.where(a >= WIN, a - WIN, a)
    b = jnp.where(b >= WIN, b - WIN, b)
    source = a * WIN + b
    stored = iota((sz.vis, sz.vp), 1)
    mine = (source == patch_of(stored, core, sz)).astype(F32).astype(BF16)
    theirs = (source == patch_of(stored + sz.vp, core, sz)).astype(F32).astype(BF16)
    return mine, theirs


def window_class(index, sc):
    a = div12(index)
    b = index - a * WIN
    return jnp.where(a >= WIN - sc[2], 2, 0) + jnp.where(b >= WIN - sc[3], 1, 0)


def window_mask(sc, sz):
    keys = window_class(iota((sz.vis, 1), 0), sc)
    asks = window_class(iota((1, sz.vis), 1), sc)
    keys = jnp.where(sc[4] > 0, keys, -1)
    return keys == asks


def self_mask(sc, sz, count, base):
    keys = query_of(iota((sz.qlen, 1), 0), sc[0], sz)
    asks = query_of(iota((1, count), 1) + base, sc[0], sz)
    return keys <= jnp.maximum(asks, sc[1] - 1)


def question_mask(sc, sz):
    return query_of(iota((sz.qlen, 1), 0), sc[0], sz) < sc[1]


def patch_pad(sc, sz):
    return patch_of(iota((2 * sz.vp, 1), 0), sc[0], sz) >= 0


def masked(scores, kind, sc, sz, base=0):
    if kind == "self":
        return jnp.where(self_mask(sc, sz, scores.shape[1], base), scores, NEG)
    if kind == "question":
        return jnp.where(question_mask(sc, sz), scores, NEG)
    if kind == "window":
        return jnp.where(window_mask(sc, sz), scores, NEG)
    real = patch_pad(sc, sz)
    return jnp.where(real & (sc[4] > 0), scores, jnp.where(real, NEG, OUT))


def allowed(kind, sc, sz):
    if kind == "self":
        return self_mask(sc, sz, sz.qlen, 0)
    if kind == "question":
        return question_mask(sc, sz)
    if kind == "window":
        return window_mask(sc, sz)
    return patch_pad(sc, sz) & (sc[4] > 0)


SCALE = HDIM**-0.5


def attend(q, k, v, addend, kind, sc, sz, base):
    scores = nt(k, q) * SCALE
    if addend is not None:
        scores = scores + addend
    scores = masked(scores, kind, sc, sz, base)
    top = jnp.max(scores, 0, keepdims=True)
    e = jnp.exp(scores - top)
    inv = 1.0 / jnp.sum(e, 0, keepdims=True)
    o_t = tn(v, (e * inv).astype(BF16))
    return o_t, top, inv


def attend_back(q, k, v, addend, kind, sc, sz, top, inv, do):
    scores = nt(k, q) * SCALE
    if addend is not None:
        scores = scores + addend
    scores = masked(scores, kind, sc, sz)
    p = jnp.exp(scores - top) * inv
    dv = nn(p.astype(BF16), do)
    dp = nt(v, do)
    ds = p * (dp - jnp.sum(p * dp, 0, keepdims=True))
    ds = jnp.where(allowed(kind, sc, sz), ds, 0.0).astype(BF16)
    dk = nn(ds, q) * SCALE
    dq = tn(k, ds) * SCALE
    return dq, dk, dv, ds


def head(ref, part, h, heads):
    start = (part * heads + h) * HDIM
    return ref[:, start : start + HDIM]


def run_heads(q_of, k_of, v_of, bias, kind, sc, sz, o_ref, st_ref, heads, base=0):
    outs = []
    for h in range(heads):
        o_t, top, inv = attend(
            q_of(h), k_of(h), v_of(h), None if bias is None else bias[h], kind, sc, sz, base
        )
        outs.append(o_t)
        st_ref[h : h + 1, :] = top
        st_ref[heads + h : heads + h + 1, :] = inv
    o_ref[...] = jnp.concatenate(outs, 0).T.astype(BF16)


def section1_far(sz, sc, nm, nth, w1, qkvf):
    qkvf[0 : sz.q2, :] = nt(nm[...], w1[...]).astype(BF16)
    qkvf[sz.q2 :, :] = nt(nth[...], w1[...]).astype(BF16)


def section1_near(sz, heads, sc, nm, nth, qkvf, w0, w1, wo0, wo1, bias, pm, pt, nvw, qkvv, ov, stv, qkvn, on, stn, ow):
    vp = sz.vp
    mine, theirs = window_permutation(sc, sz)
    nv = (nn(mine, nm[0:vp, :]) + nn(theirs, nth[0:vp, :])).astype(BF16)
    nvw[...] = nv
    qkvv[...] = nt(nv, w0[...]).astype(BF16)
    run_heads(
        lambda h: head(qkvv, 0, h, heads),
        lambda h: head(qkvv, 1, h, heads),
        lambda h: head(qkvv, 2, h, heads),
        bias, "window", sc, sz, ow, stv, heads,
    )
    ov[0:vp, :] = tn(mine, ow[...]).astype(BF16)
    ov[vp : 2 * vp, :] = tn(theirs, ow[...]).astype(BF16)
    give_patches(pm, pt, nn(ov[...], wo0[...]).astype(BF16), sz)
    qkvn[0 : sz.q1, :] = nt(nm[vp:, :], w1[...]).astype(BF16)
    qkvn[sz.q1 :, :] = nt(nth[vp:, :], w1[...]).astype(BF16)
    every = Rows([qkvn, qkvf])
    run_heads(
        lambda h: head(qkvn, 0, h, heads),
        lambda h: head(every, 1, h, heads),
        lambda h: head(every, 2, h, heads),
        None, "self", sc, sz, on, stn, heads,
    )
    give_near(pm, pt, nn(on[...], wo1[...]).astype(BF16), sz)


def section1_rest(sz, heads, sc, qkvn, qkvf, wo1, pm, pt, of, stf):
    every = Rows([qkvn, qkvf])
    run_heads(
        lambda h: head(qkvf, 0, h, heads),
        lambda h: head(every, 1, h, heads),
        lambda h: head(every, 2, h, heads),
        None, "self", sc, sz, of, stf, heads, 2 * sz.q1,
    )
    pm[...] = nn(of[0 : sz.q2, :], wo1[...]).astype(BF16)
    pt[...] = nn(of[sz.q2 :, :], wo1[...]).astype(BF16)


def section2_near(sz, heads, sc, nm, nth, w2, w3, qv, kvv, qn, kvn, on, stn):
    e = heads * HDIM
    v = patch_rows(nm, nth, sz)
    q = near_rows(nm, nth, sz)
    qv[...] = nt(v, w3[0:e, :]).astype(BF16)
    kvv[...] = nt(v, w2[e:, :]).astype(BF16)
    qn[...] = nt(q, w2[0:e, :]).astype(BF16)
    kvn[...] = nt(q, w3[e:, :]).astype(BF16)
    run_heads(
        lambda h: head(qn, 0, h, heads),
        lambda h: head(kvv, 0, h, heads),
        lambda h: head(kvv, 1, h, heads),
        None, "patch", sc, sz, on, stn, heads,
    )


def section2_far(sz, heads, sc, nm, nth, kvv, w2, w3, wo2, pm, pt, qf, kvf, of, stf):
    e = heads * HDIM
    x = jnp.concatenate([nm[...], nth[...]], 0)
    qf[...] = nt(x, w2[0:e, :]).astype(BF16)
    kvf[...] = nt(x, w3[e:, :]).astype(BF16)
    run_heads(
        lambda h: head(qf, 0, h, heads),
        lambda h: head(kvv, 0, h, heads),
        lambda h: head(kvv, 1, h, heads),
        None, "patch", sc, sz, of, stf, heads,
    )
    pm[...] = nn(of[0 : sz.q2, :], wo2[...]).astype(BF16)
    pt[...] = nn(of[sz.q2 :, :], wo2[...]).astype(BF16)


def section2_rest(sz, heads, sc, qv, kvn, kvf, on, wo2, wo3, pm, pt, ov, stv):
    every = Rows([kvn, kvf])
    give_near(pm, pt, nn(on[...], wo2[...]).astype(BF16), sz)
    run_heads(
        lambda h: head(qv, 0, h, heads),
        lambda h: head(every, 0, h, heads),
        lambda h: head(every, 1, h, heads),
        None, "question", sc, sz, ov, stv, heads,
    )
    give_patches(pm, pt, nn(ov[...], wo3[...]).astype(BF16), sz)


GELU_C = 0.7978845608028654
GELU_A = 0.044715


def section3(sz, layer, spans, nm, nth, wi, bi, wo, pm, pt, g, gp):
    count = g.shape[0] // 2
    for ref, out, base in ((nm, pm, 0), (nth, pt, count)):
        for lo, hi, e in spans:
            h = nn(ref[lo:hi, :], wi[e]) + bi[layer, e : e + 1, :]
            h2 = h * h
            t = jnp.tanh(GELU_C * h * (1.0 + GELU_A * h2))
            half_t = 0.5 + 0.5 * t
            act = (h * half_t).astype(BF16)
            slope = half_t + (0.5 * GELU_C) * h * (1.0 - t * t) * (1.0 + 3.0 * GELU_A * h2)
            g[base + lo : base + hi, :] = act
            gp[base + lo : base + hi, :] = slope.astype(BF16)
            out[lo:hi, :] = nn(act, wo[e]).astype(BF16)


def section3_back(sz, dm, dt, wi, wo, gp, pm, pt, dh):
    vp, half = sz.vp, sz.half
    for ref, out, base in ((dm, pm, 0), (dt, pt, half)):
        for lo, hi, e in ((0, vp, 0), (vp, half, 1)):
            dg = nt(ref[lo:hi, :], wo[e])
            d = (dg * gp[base + lo : base + hi, :].astype(F32)).astype(BF16)
            dh[base + lo : base + hi, :] = d
            out[lo:hi, :] = nt(d, wi[e]).astype(BF16)


def back_heads(q_of, k_of, v_of, bias, kind, sc, sz, st, do_of, ds_ref, heads):
    dqs, dks, dvs = [], [], []
    for h in range(heads):
        dq, dk, dv, ds = attend_back(
            q_of(h), k_of(h), v_of(h), None if bias is None else bias[h], kind, sc, sz,
            st[h : h + 1, :], st[heads + h : heads + h + 1, :], do_of(h),
        )
        dqs.append(dq)
        dks.append(dk)
        dvs.append(dv)
        if ds_ref is not None:
            ds_ref[h] = ds
    dq = jnp.concatenate(dqs, 0).T.astype(BF16)
    dkv = jnp.concatenate(dks + dvs, 1).astype(BF16)
    return dq, dkv


def stats(near, far):
    return jnp.concatenate([near[...], far[...]], 1)


def give_queries(mine, theirs, value, sz):
    give_near(mine, theirs, value[0 : 2 * sz.q1], sz)
    mine[sz.near :, :] = value[2 * sz.q1 : 2 * sz.q1 + sz.q2]
    theirs[sz.near :, :] = value[2 * sz.q1 + sz.q2 :]


def section2_back(
    sz, heads, sc, dm, dt, w2, w3, wo2, wo3, qq, kvv, stn, stf, qv, kvq, stv, pm, pt, dqq, dkvv, dqv, dkvq, doq, dov
):
    e = heads * HDIM
    doq[...] = nt(query_rows(dm, dt, sz), wo2[...]).astype(BF16)
    dov[...] = nt(patch_rows(dm, dt, sz), wo3[...]).astype(BF16)
    dq, dkv = back_heads(
        lambda h: head(qq, 0, h, heads),
        lambda h: head(kvv, 0, h, heads),
        lambda h: head(kvv, 1, h, heads),
        None, "patch", sc, sz, stats(stn, stf), lambda h: head(doq, 0, h, heads), None, heads,
    )
    dqq[...] = dq
    dkvv[...] = dkv
    dq, dkv = back_heads(
        lambda h: head(qv, 0, h, heads),
        lambda h: head(kvq, 0, h, heads),
        lambda h: head(kvq, 1, h, heads),
        None, "question", sc, sz, stv, lambda h: head(dov, 0, h, heads), None, heads,
    )
    dqv[...] = dq
    dkvq[...] = dkv
    give_queries(pm, pt, (nn(dqq[...], w2[0:e, :]) + nn(dkvq[...], w3[e:, :])).astype(BF16), sz)
    give_patches(pm, pt, (nn(dqv[...], w3[0:e, :]) + nn(dkvv[...], w2[e:, :])).astype(BF16), sz)


def section1_back(
    sz, heads, sc, dm, dt, w0, w1, wo0, wo1, bias, qkvv, stv, qkvq, stn, stf, pm, pt, dqkvv, dqkvq, ds, doq, dov
):
    vp = sz.vp
    e = heads * HDIM
    mine, theirs = window_permutation(sc, sz)
    do_m = nt(dm[0:vp, :], wo0[...]).astype(BF16)
    do_t = nt(dt[0:vp, :], wo0[...]).astype(BF16)
    dov[...] = (nn(mine, do_m) + nn(theirs, do_t)).astype(BF16)
    dq, dkv = back_heads(
        lambda h: head(qkvv, 0, h, heads),
        lambda h: head(qkvv, 1, h, heads),
        lambda h: head(qkvv, 2, h, heads),
        bias, "window", sc, sz, stv, lambda h: head(dov, 0, h, heads), ds, heads,
    )
    dqkvv[:, 0:e] = dq
    dqkvv[:, e:] = dkv
    dn = nn(dqkvv[...], w0[...]).astype(BF16)
    pm[0:vp, :] = tn(mine, dn).astype(BF16)
    pt[0:vp, :] = tn(theirs, dn).astype(BF16)
    doq[...] = nt(query_rows(dm, dt, sz), wo1[...]).astype(BF16)
    dq, dkv = back_heads(
        lambda h: head(qkvq, 0, h, heads),
        lambda h: head(qkvq, 1, h, heads),
        lambda h: head(qkvq, 2, h, heads),
        None, "self", sc, sz, stats(stn, stf), lambda h: head(doq, 0, h, heads), None, heads,
    )
    dqkvq[:, 0:e] = dq
    dqkvq[:, e:] = dkv
    give_queries(pm, pt, nn(dqkvq[...], w1[...]).astype(BF16), sz)


def kept_order(order):
    return sorted(range(1 << len(order)), key=lambda r: [(r >> k) & 1 for k in order])


def store_blocks(sc, store, col, value):
    keep, send, scr, order = store
    width = value.shape[1]
    value = value.astype(BF16)
    cols = slice(col, col + width)
    if send is None:
        keep[0, :, cols] = value
        return
    count, rows = keep.shape[0], keep.shape[1]
    scr[:, 0:width] = value
    for slot, relative in enumerate(kept_order(order)):
        owner = relative ^ sc[5]
        block = scr[pl.ds(pl.multiple_of(owner * rows, 16), rows), 0:width]
        if slot < count:
            keep[slot, :, cols] = block
        else:
            send[slot - count, :, cols] = block


def section3_weights(sz, sc, nm, nth, dm, dt, g, dh, db, out):
    vp, half = sz.vp, sz.half
    hid = dh.shape[1]
    for e, lo, hi in ((0, 0, vp), (1, vp, half)):
        into = tn(nm[lo:hi, :], dh[lo:hi, :]) + tn(nth[lo:hi, :], dh[half + lo : half + hi, :])
        away = tn(dm[lo:hi, :], g[lo:hi, :]) + tn(dt[lo:hi, :], g[half + lo : half + hi, :])
        out[:, e * hid : (e + 1) * hid] = into.astype(BF16)
        out[:, (2 + e) * hid : (3 + e) * hid] = away.astype(BF16)
        db[e : e + 1, :] = jnp.sum(dh[lo:hi, :].astype(F32), 0, keepdims=True) + jnp.sum(
            dh[half + lo : half + hi, :].astype(F32), 0, keepdims=True
        )


def section2_weights(sz, heads, sc, nm, nth, dm, dt, dqq, dkvv, dqv, dkvq, oq, ov, store):
    e = heads * HDIM
    nq, nv = query_rows(nm, nth, sz), patch_rows(nm, nth, sz)
    store_blocks(sc, store, 0, tn(nq, dqq[...]))
    store_blocks(sc, store, e, tn(nv, dkvv[...]))
    store_blocks(sc, store, 3 * e, tn(nv, dqv[...]))
    store_blocks(sc, store, 4 * e, tn(nq, dkvq[...]))
    store_blocks(sc, store, 6 * e, tn(query_rows(dm, dt, sz), oq[...]))
    store_blocks(sc, store, 7 * e, tn(patch_rows(dm, dt, sz), ov[...]))


def section1_weights(sz, heads, sc, nm, nth, dm, dt, nvw, dqkvv, dqkvq, oq, ov, store):
    e = heads * HDIM
    store_blocks(sc, store, 0, tn(nvw[...], dqkvv[...]))
    store_blocks(sc, store, 3 * e, tn(query_rows(nm, nth, sz), dqkvq[...]))
    store_blocks(sc, store, 6 * e, tn(patch_rows(dm, dt, sz), ov[...]))
    store_blocks(sc, store, 7 * e, tn(query_rows(dm, dt, sz), oq[...]))


def in_order(sz, chip, own, other, out):
    v, piece = sz.vpiece, sz.piece
    mine, theirs = own[...].astype(F32), other[...].astype(F32)
    first = jnp.where(chip == 0, mine, theirs)
    second = jnp.where(chip == 0, theirs, mine)
    out[0:v, :] = first[0:v]
    out[v : 2 * v, :] = second[0:v]
    out[2 * v : v + piece, :] = first[v:]
    out[v + piece :, :] = second[v:]


def norm_rows(x):
    center = x - jnp.mean(x, -1, keepdims=True)
    inv = lax.rsqrt(jnp.mean(center * center, -1, keepdims=True) + EPS)
    return center * inv, inv


def open_stream(sz, sc, own, other, scale, shift, x, n):
    layer = first = 0
    in_order(sz, sc[6], own, other, x)
    for lo, hi, e in ((0, sz.vp, 0), (sz.vp, sz.half, 1)):
        gain, bias = scale[first + e, layer : layer + 1, :], shift[first + e, layer : layer + 1, :]
        n[lo:hi, :] = (norm_rows(x[lo:hi, :])[0] * gain + bias).astype(BF16)


def open_grad(sz, sc, own, other, grad, dy, sums):
    in_order(sz, sc[6], own, other, grad)
    dy[...] = grad[...].astype(BF16)
    for lo, hi, e in ((0, sz.vp, 0), (sz.vp, sz.half, 1)):
        sums[4 + e : 5 + e, :] = jnp.sum(grad[lo:hi, :], 0, keepdims=True)


def add_norm(spans, layer, first, x, a, b, extra, scale, shift, y, n):
    for lo, hi, e in spans:
        gain, bias = scale[first + e, layer : layer + 1, :], shift[first + e, layer : layer + 1, :]
        value = x[lo:hi, :] + (a[lo:hi, :].astype(F32) + b[lo:hi, :].astype(F32))
        if extra is not None:
            value = value + extra[layer - 1, e : e + 1, :]
        y[lo:hi, :] = value
        n[lo:hi, :] = (norm_rows(value)[0] * gain + bias).astype(BF16)


def norm_back(sz, layer, first, d, a, b, x, scale, out, dy, sums):
    for lo, hi, e in ((0, sz.vp, 0), (sz.vp, sz.half, 1)):
        dn = a[lo:hi, :].astype(F32) + b[lo:hi, :].astype(F32)
        unit, inv = norm_rows(x[lo:hi, :])
        du = dn * scale[first + e, layer : layer + 1, :]
        dx = inv * (
            du
            - jnp.mean(du, -1, keepdims=True)
            - unit * jnp.mean(du * unit, -1, keepdims=True)
        )
        value = d[lo:hi, :] + dx
        out[lo:hi, :] = value
        dy[lo:hi, :] = value.astype(BF16)
        sums[e : e + 1, :] = jnp.sum(dn * unit, 0, keepdims=True)
        sums[2 + e : 3 + e, :] = jnp.sum(dn, 0, keepdims=True)
        sums[4 + e : 5 + e, :] = jnp.sum(value, 0, keepdims=True)


TABLE = SPAN * SPAN
TABLE_PAD = -(-TABLE // 128) * 128
CELLS_PAD = -(-SPAN * WIN // 128) * 128


def spread_matrix():
    cell = iota((TABLE_PAD, CELLS_PAD), 1)
    row = (cell * 171) >> 11
    place = row * SPAN + cell - row * WIN
    return ((iota((TABLE_PAD, CELLS_PAD), 0) == place) & (cell < SPAN * WIN)).astype(F32)


def table_bias(tables, out, spread, rows):
    spread[...] = spread_matrix()
    count = out.shape[0]
    for i in range(count):
        table = tables[i : i + 1, :]
        for b in range(WIN):
            at = i * WIN + b
            rows[at : at + 1, :] = pltpu.roll(table, (TABLE_PAD - (WIN - 1 - b)) % TABLE_PAD, 1)
    cells = jnp.dot(rows[...], spread[...], precision=lax.Precision.HIGHEST, preferred_element_type=F32)
    for a in range(WIN):
        moved = pltpu.roll(cells, (CELLS_PAD - WIN * (WIN - 1 - a)) % CELLS_PAD, 1)
        for i in range(count):
            out[i, WIN * a : WIN * (a + 1), :] = moved[WIN * i : WIN * (i + 1), 0 : WIN * WIN]


def table_grad(ds, spread, out):
    heads = ds.shape[0]
    rows = jnp.zeros((WIN, CELLS_PAD - WIN * WIN), F32)
    every = []
    for h in range(heads):
        grad = ds[h].astype(F32)
        cells = jnp.zeros((WIN, CELLS_PAD), F32)
        for a in range(WIN):
            part = jnp.concatenate([grad[WIN * a : WIN * (a + 1), :], rows], 1)
            cells = cells + pltpu.roll(part, WIN * (WIN - 1 - a), 1)
        every.append(cells)
    places = lax.dot_general(
        jnp.concatenate(every, 0),
        spread[...],
        (((1,), (1,)), ((), ())),
        precision=lax.Precision.HIGHEST,
        preferred_element_type=F32,
    )
    for h in range(heads):
        total = jnp.zeros((1, TABLE_PAD), F32)
        for b in range(WIN):
            total = total + pltpu.roll(places[h * WIN + b : h * WIN + b + 1, :], WIN - 1 - b, 1)
        out[h : h + 1, :] = total


def collect(layers, heads, *refs):
    out = refs[-1]
    out[...] = jnp.zeros(out.shape, F32)
    row = 0
    for layer in range(layers):
        sums1, sums2, sums3, after = refs[6 * layer : 6 * layer + 4]
        for ref, lo, count in ((sums1, 0, 4), (sums2, 0, 4), (sums3, 0, 4), (after, 4, 2)):
            out[row : row + count, :] = ref[lo : lo + count, :]
            row += count
    for layer in range(layers):
        db, table = refs[6 * layer + 4 : 6 * layer + 6]
        out[row : row + 2, :] = db[...]
        row += 2
        out[row : row + heads, 0:TABLE_PAD] = table[0:heads, :]
        row += heads


def deal(layers, heads, rows, scale, shift, out_bias, in_bias, rel):
    for layer in range(layers):
        at = 14 * layer
        for section in range(3):
            for e in range(2):
                scale[2 * section + e, layer : layer + 1, :] = rows[at + 4 * section + e : at + 4 * section + e + 1, :]
                row = at + 4 * section + 2 + e
                shift[2 * section + e, layer : layer + 1, :] = rows[row : row + 1, :]
        out_bias[layer] = rows[at + 12 : at + 14, :]
        at = 14 * layers + (2 + heads) * layer
        in_bias[layer] = rows[at : at + 2, :]
        for h in range(heads):
            rel[h, layer : layer + 1, :] = rows[at + 2 + h : at + 3 + h, 0:TABLE]


def finish_mlp(layers, *refs):
    up, down = refs[layers:]
    hid = up.shape[3]
    for layer in range(layers):
        total = refs[layer][...].astype(F32)
        for e in range(2):
            up[layer, e] = total[:, e * hid : (e + 1) * hid]
            down[layer, e] = total[:, (2 + e) * hid : (3 + e) * hid]


def finish_attn(layers, *refs):
    d_in, d_out = refs[8 * layers :]
    e = d_in.shape[4]
    for layer in range(layers):
        for pair in range(2):
            first = 8 * layer + 4 * pair
            total = sum(r[...].astype(F32) for r in refs[first : first + 4])
            for which in range(2):
                for c in range(3):
                    col = (3 * which + c) * e
                    d_in[layer, 2 * pair + which, c] = total[:, col : col + e]
                col = (6 + which) * e
                d_out[layer, 2 * pair + which] = total[:, col : col + e].T


def on_device(
    dp_size,
    visual,
    queries,
    valid_windows,
    answer_start,
    shifts,
    norm_scale,
    norm_shift,
    attn_in,
    attn_out,
    rel_bias,
    mlp_in,
    mlp_in_bias,
    mlp_out,
    mlp_out_bias,
    grad_visual_out,
    grad_query_out,
):
    layers, width = attn_in.shape[0], attn_in.shape[2]
    edev = attn_in.shape[4]
    heads = edev // HDIM
    hid = mlp_in.shape[3]
    sz = Sizes(4 * visual.shape[1], 4 * queries.shape[1])
    half, vp, qh = sz.half, sz.vp, sz.qh
    vq, qq_ = sz.vquart, sz.qquart
    t_index = lax.axis_index("tensor")
    d_index = lax.axis_index("dp")
    core, chip = t_index % 2, t_index // 2
    swap = [(i, i ^ 1) for i in range(4)]
    cross = [(i, i ^ 2) for i in range(4)]
    block_rows = width // dp_size
    halving = dp_size > 1 and dp_size & (dp_size - 1) == 0 and block_rows % 16 == 0
    bits = dp_size.bit_length() - 1

    def scalars(layer):
        on = layer % 2
        values = [core, answer_start[0], shifts[0, 0] * on, shifts[0, 1] * on, valid_windows[0, 0], d_index, chip, 0]
        return jnp.stack(values).astype(jnp.int32)

    w_in = attn_in.transpose(0, 1, 3, 4, 2).reshape(layers, 4, 3 * edev, width)
    scale, shift = norm_scale.transpose(1, 0, 2), norm_shift.transpose(1, 0, 2)

    def packed(own_v, own_q):
        pad = jnp.zeros((sz.vpiece - vq, width), own_v.dtype)
        return jnp.concatenate([own_v, pad, own_q], 0)

    def piece_of(rows, place):
        v = jnp.where(place == 0, rows[0 : sz.vpiece], rows[sz.vpiece : vp])
        q = jnp.where(place == 0, rows[vp : vp + qq_], rows[vp + qq_ :])
        return jnp.concatenate([v, q], 0)

    def core_swap(x):
        if isinstance(x, list):
            return [core_swap(p) for p in x]
        return lax.ppermute(x, "tensor", swap)

    def across(x):
        return lax.ppermute(x, "tensor", cross)

    def pair_sum(mine, theirs):
        got = core_swap(theirs)
        if not isinstance(got, list):
            return (mine.astype(F32) + got.astype(F32)).astype(BF16)

        def body(a, b, out):
            out[...] = (a[...].astype(F32) + b[...].astype(F32)).astype(BF16)

        return call(body, [shaped(mine.shape)], [], [mine, got], name="pair_sum")[0]

    def pair(x):
        return x, core_swap(x)

    far = half - sz.near
    near_bf, far_bf = shaped((sz.near, width)), shaped((far, width))

    def halved(rows):
        first = -(-rows // 32) * 16
        return [shaped((first, width)), shaped((rows - first, width))]

    near_two, far_two = halved(sz.near), halved(far)
    rows_bf = [shaped((half, width))]
    rows_f = shaped((half, width), F32)
    near_spans = ((0, vp, 0), (vp, sz.near, 1))
    far_spans = ((0, far, 1),)

    def natural(near_part, far_part):
        return Rows(
            [
                (near_part, 0, sz.near),
                (far_part, 0, far),
                (near_part, sz.near, 2 * sz.near),
                (far_part, far, 2 * far),
            ]
        )

    own = packed(visual[0], queries[0])
    other = lax.ppermute(own, "tensor", cross)
    tables = jnp.pad(rel_bias.reshape(layers * heads, TABLE), ((0, 0), (0, TABLE_PAD - TABLE)))
    bias_all, spread = call(
        table_bias,
        [shaped((layers * heads, sz.vis, sz.vis), F32), shaped((TABLE_PAD, CELLS_PAD), F32)],
        [],
        [tables],
        name="table_bias",
        scratch=[pltpu.VMEM((layers * heads * WIN, TABLE_PAD), F32)],
    )
    bias_all = bias_all.reshape(layers, heads, sz.vis, sz.vis)
    scal = [scalars(layer) for layer in range(layers)]
    own_grad = packed(grad_visual_out[0], grad_query_out[0])
    rounded_grad = lax.reduce_precision(own_grad, 8, 7)

    def next_norm(spans, x, a, b, layer, first, extra=False):
        args = [x, a, b] + ([mlp_out_bias] if extra else []) + [scale, shift]

        def body(x, a, b, *rest):
            if not extra:
                rest = (None,) + rest
            add_norm(spans, layer, first, x, a, b, *rest)

        return call(body, [shaped(x.shape, F32), halved(x.shape[0])], [], args, name="norm")

    fetched = {}

    def fetch(layer, section, after):
        if section == 3:
            arrays = [mlp_in, mlp_out]
            blocks = [(0, (layer,)), (1, (layer,))]
        else:
            arrays = [w_in, attn_out]
            first = 2 * (section - 1)
            blocks = [(0, (layer, first)), (0, (layer, first + 1)), (1, (layer, first)), (1, (layer, first + 1))]
        arrays = tie(after, arrays)[1]
        outs = [shaped(arrays[k].shape[len(lead) :]) for k, lead in blocks]
        marked = outs + [shaped((8, 128), F32)]

        def body(one, two, *refs):
            refs[len(outs)][...] = jnp.zeros((8, 128), F32)
            copies = [
                pltpu.make_async_copy((one, two)[k].at[lead], refs[j], refs[-1].at[j])
                for j, (k, lead) in enumerate(blocks)
            ]
            for copy in copies:
                copy.start()
            for copy in copies:
                copy.wait()

        *fetched[layer, section], mark = pl.pallas_call(
            body,
            out_shape=marked,
            in_specs=[pl.BlockSpec(memory_space=pltpu.HBM)] * 2,
            out_specs=[pl.BlockSpec(memory_space=pltpu.VMEM)] * len(marked),
            scratch_shapes=[pltpu.SemaphoreType.DMA((len(outs),))],
            compiler_params=pltpu.CompilerParams(vmem_limit_bytes=VMEM_LIMIT),
            name="fetch",
        )(*arrays)
        return mark

    def fetch_beside(layer, section, a, b):
        fetch(layer, section, a)
        b, fetched[layer, section] = tie(b, fetched[layer, section])
        return b

    mark = fetch(0, 1, own)
    sent_grad = rounded_grad.astype(BF16)
    opening, bias_all, spread = tie(scal[0], bias_all, spread)

    def open_body(sc, own, other, scale, shift, mark, *refs):
        open_stream(sz, sc, own, other, scale, shift, *refs[:-1])
        refs[-1][...] = jnp.zeros(refs[-1].shape, F32)

    (x_near, x_far), pieces, token = call(
        open_body,
        [
            [shaped((sz.near, width), F32), shaped((far, width), F32)],
            near_two + far_two,
            shaped((8, 128), F32),
        ],
        [opening],
        [own, other, scale, shift, mark],
        name="open_stream",
    )
    sent_grad, token = tie(sent_grad, token)
    other_grad = across(sent_grad)
    near_sc, other_grad = tie(scal[0], other_grad)
    n_near, n_far = pieces[0:2], pieces[2:4]

    saved = []
    for layer in range(layers):
        sc = scal[layer]
        w0, w1, wo0, wo1 = fetched[layer, 1]
        if layer > 0:
            got_far, _ = tie(got_far, kept_near)
            got_far, fetched[layer, 1] = tie(got_far, fetched[layer, 1])
            w0, w1, wo0, wo1 = fetched[layer, 1]
            x_far, n_far = next_norm(far_spans, x_far, kept_far, got_far, layer, 0, True)
        t_far = core_swap(n_far)
        first = [token] if layer == 0 else []
        (qkvf,) = call(
            lambda sc, nm, nth, w1, *r: section1_far(sz, sc, nm, nth, w1, r[-1]),
            [shaped((2 * far, 3 * edev))],
            [sc],
            [n_far, t_far, w1] + first,
            name="section1",
        )
        if layer > 0:
            got_near, qkvf = tie(got_near, qkvf)
            x_near, n_near = next_norm(near_spans, x_near, kept_near, got_near, layer, 0, True)
        t_near = core_swap(n_near)
        x1, n1, t1 = [x_near, x_far], n_near + n_far, t_near + t_far
        pm, pt, nvw, qkvv, ov, stv, qkvn, on, stn = call(
            lambda *r: section1_near(sz, heads, *r),
            [
                near_bf,
                near_two,
                shaped((sz.vis, width)),
                shaped((sz.vis, 3 * edev)),
                shaped((2 * vp, edev)),
                shaped((8, sz.vis), F32),
                shaped((2 * sz.q1, 3 * edev)),
                shaped((2 * sz.q1, edev)),
                shaped((8, 2 * sz.q1), F32),
            ],
            [sc],
            [n_near, t_near, qkvf, w0, w1, wo0, wo1, Part(bias_all, layer)],
            name="section1",
            scratch=[pltpu.VMEM((sz.vis, edev), BF16)],
        )
        kept_near = pair_sum(pm, pt)
        got_near = across(kept_near)
        _, later = tie(kept_near, qkvn)
        pm, pt, of, stf = call(
            lambda *r: section1_rest(sz, heads, *r),
            [far_bf, far_two, shaped((2 * far, edev)), shaped((8, 2 * far), F32)],
            [sc if layer else near_sc],
            [later, qkvf, wo1],
            name="section1",
        )
        saved1 = (x1, n1, t1, nvw, qkvv, ov, stv, [qkvn, qkvf], [on, of], stn, stf)
        kept_far = pair_sum(pm, pt)
        got_far = across(kept_far)

        fetch(layer, 2, kept_near)
        got_near, fetched[layer, 2], _ = tie(got_near, fetched[layer, 2], kept_far)
        if layer == 0:
            other_grad, sent_grad, _ = tie(other_grad, sent_grad, kept_far)
            grad, dy, grad_sums = call(
                lambda *r: open_grad(sz, *r),
                [rows_f, rows_bf, shaped((8, width), F32)],
                scal[0:1],
                [sent_grad, other_grad],
                name="open_grad",
            )
            got_near, grad, dy = tie(got_near, grad, dy)
        w2, w3, wo2, wo3 = fetched[layer, 2]
        x_near, n_near = next_norm(near_spans, x_near, kept_near, got_near, layer, 2)
        t_near = core_swap(n_near)
        qv, kvv, qn, kvn, on, stn = call(
            lambda *r: section2_near(sz, heads, *r),
            [
                shaped((2 * vp, edev)),
                shaped((2 * vp, 2 * edev)),
                shaped((2 * sz.q1, edev)),
                shaped((2 * sz.q1, 2 * edev)),
                shaped((2 * sz.q1, edev)),
                shaped((8, 2 * sz.q1), F32),
            ],
            [sc],
            [n_near, t_near, w2, w3],
            name="section2",
        )
        got_far, kvv = tie(got_far, kvv)
        x_far, n_far = next_norm(far_spans, x_far, kept_far, got_far, layer, 2)
        t_far = core_swap(n_far)
        pm, pt, qf, kvf, of, stf = call(
            lambda *r: section2_far(sz, heads, *r),
            [
                far_bf,
                far_two,
                shaped((2 * far, edev)),
                shaped((2 * far, 2 * edev)),
                shaped((2 * far, edev)),
                shaped((8, 2 * far), F32),
            ],
            [sc],
            [n_far, t_far, kvv, w2, w3, wo2],
            name="section2",
        )
        x2, n2, t2 = [x_near, x_far], n_near + n_far, t_near + t_far
        kept_far = pair_sum(pm, pt)
        got_far = across(kept_far)
        _, later = tie(kept_far, qv)
        pm, pt, ov, stv = call(
            lambda *r: section2_rest(sz, heads, *r),
            [near_bf, near_two, shaped((2 * vp, edev)), shaped((8, 2 * vp), F32)],
            [sc],
            [later, kvn, kvf, on, wo2, wo3],
            name="section2",
        )
        saved2 = (x2, n2, t2, [qn, qf], kvv, [on, of], stn, stf, qv, [kvn, kvf], ov, stv)
        kept_near = pair_sum(pm, pt)
        got_near = across(kept_near)

        fetch(layer, 3, kept_far)
        got_far, fetched[layer, 3], _ = tie(got_far, fetched[layer, 3], kept_near)
        up, down = fetched[layer, 3]

        def feed_forward(spans, n, t):
            rows = sum(p.shape[0] for p in n)
            return call(
                lambda *r: section3(sz, layer, spans, *r),
                [shaped((rows, width)), halved(rows)] + [shaped((2 * rows, hid))] * 2,
                [],
                [n, t, up, mlp_in_bias, down],
                name="section3",
            )

        x_far, n_far = next_norm(far_spans, x_far, kept_far, got_far, layer, 4)
        t_far = core_swap(n_far)
        pm, pt, act_far, slope_far = feed_forward(far_spans, n_far, t_far)
        kept_far = pair_sum(pm, pt)
        if layer + 1 < layers:
            got_far = across(kept_far)
        got_near, _ = tie(got_near, kept_far)
        x_near, n_near = next_norm(near_spans, x_near, kept_near, got_near, layer, 4)
        t_near = core_swap(n_near)
        pm, pt, act_near, slope_near = feed_forward(near_spans, n_near, t_near)
        kept_near = pair_sum(pm, pt)
        if layer + 1 < layers:
            got_near = across(kept_near)
            fetch(layer + 1, 1, kept_far)
        x3, n3, t3 = [x_near, x_far], n_near + n_far, t_near + t_far
        saved3 = (x3, n3, t3, (act_near, act_far), (slope_near, slope_far))
        saved.append((saved1, saved2, saved3))
    stream = jnp.concatenate([x_near, x_far], 0)
    last = jnp.concatenate([kept_near, kept_far], 0)
    away = lax.ppermute(piece_of(last, 1 - chip), "tensor", cross)
    out = piece_of(stream, chip) + (piece_of(last, chip).astype(F32) + away.astype(F32))
    out_v = (out[0:vq] + mlp_out_bias[layers - 1, 0]).astype(BF16)
    out_q = (out[sz.vpiece :] + mlp_out_bias[layers - 1, 1]).astype(BF16)

    bias_sums = grad_sums

    def whole_sum(rows):
        return lax.psum_scatter(rows, "dp", scatter_dimension=0, tiled=True)

    def shares(mine, theirs):
        kept = [pair_sum(m, t) for m, t in zip(mine, theirs)]
        return kept, [across(k) for k in kept]

    class Reduction:
        def __init__(self, outs, order):
            self.order = order
            if halving:
                self.parts, self.step = [outs[0]], 0
                self.ready = outs[1]
                self.move()
            else:
                self.sum = whole_sum(outs[0][0])
                self.step = bits

        def move(self):
            bit = 1 << self.order[self.step]
            got = lax.ppermute(self.ready, "dp", [(i, i ^ bit) for i in range(dp_size)])
            self.parts.append(got)
            self.step += 1

        def advance(self):
            count = 1 << (bits - 1 - self.step)
            self.ready = sum(p[count : 2 * count].astype(F32) for p in self.parts).astype(BF16)
            self.move()

        def pieces(self):
            if not halving:
                zero = jnp.zeros_like(self.sum)
                return [self.sum, zero, zero, zero]
            lead = [Part(p, 0) for p in self.parts]
            while len(lead) < 4:
                lead.append(jnp.zeros(lead[0].rest, BF16))
            return lead

    def close(grad, a, b, kept, layer, first):
        return call(
            lambda *r: norm_back(sz, layer, first, *r),
            [rows_f, rows_bf, shaped((8, width), F32)],
            [],
            [grad, a, b, kept[0], scale],
            name="norm_back",
        )

    straight = tuple(range(bits))
    turned = straight[1:] + straight[:1]

    def weights(body, extra_outs, orders, columns, args, wide, name):
        outs = []
        for _ in orders:
            if halving:
                outs += [shaped((dp_size // 2, block_rows, columns))] * 2
            else:
                outs += [shaped((1, width, columns))]
        lead = 1 + len(args) + len(extra_outs)
        each = 2 if halving else 1

        def wrapped(*refs):
            stores = []
            for k, order in enumerate(orders):
                given = refs[lead + k * each : lead + (k + 1) * each]
                stores.append((given[0], given[1] if halving else None, refs[-1], order))
            body(*refs[:lead], *stores)

        got = call(
            wrapped,
            list(extra_outs) + outs,
            [scal[0]],
            args,
            name=name,
            scratch=[pltpu.VMEM((width, wide), BF16)],
        )
        extra, rest = got[: len(extra_outs)], got[len(extra_outs) :]
        return extra, [Reduction(rest[k * each : (k + 1) * each], order) for k, order in enumerate(orders)]

    reductions = []
    feeds = []
    arrivals = {}
    if halving and bits == 3 and layers == 2:
        arrivals = {2: [0], 3: [0, 1], 4: [1], 5: [2]}

    def window(kept, args):
        return tie(kept, list(args))[1]

    def seal(index, got, extra, made):
        due = [reductions[g] for g in arrivals.get(index, ()) if reductions[g].step < bits]
        firsts = [r.parts[0] for r in made] if halving else []
        extra, firsts, parts = tie(list(extra), firsts, [r.parts for r in due])
        for r, p in zip(due, parts):
            r.parts = list(p)
            r.advance()
        got, extra, firsts = tie(got, extra, firsts)
        for r, part in zip(made, firsts):
            r.parts[0] = part
        reductions.extend(made)
        return got, extra

    grads = [None] * layers
    index = 0
    for layer in reversed(range(layers)):
        sc = scal[layer]
        kept1, kept2, kept3 = saved[layer]
        dm, dt = pair(dy)
        _, nm, nth, act, slope = kept3
        up, down = fetched[layer, 3]
        pm, pt, dh = call(
            lambda dm, dt, wi, wo, near_part, far_part, *r: section3_back(
                sz, dm, dt, wi, wo, natural(near_part, far_part), *r
            ),
            [rows_bf, rows_bf, shaped((2 * half, hid))],
            [],
            [dm, dt, up, down, *slope],
            name="section3_back",
        )
        a, b = shares(pm, pt)
        args = window(a, [nm, nth, dm, dt, *act, dh])
        db, feed = call(
            lambda sc, nm, nth, dm, dt, near_part, far_part, *r: section3_weights(
                sz, sc, nm, nth, dm, dt, natural(near_part, far_part), *r
            ),
            [shaped((2, hid), F32), shaped((width, 4 * hid))],
            [sc],
            args,
            name="section3_weights",
        )
        feeds.append(whole_sum(feed))
        b, (db,) = seal(index, b, [db], [])
        index += 1
        out_bias_sums = bias_sums
        grad, dy, sums3 = close(grad, a, b, kept3, layer, 4)

        dm, dt = pair(dy)
        _, nm, nth, qq, kvv, oq, stn, stf, qv, kvq, ov, stv = kept2
        part = call(
            lambda *r: section2_back(sz, heads, *r),
            [
                rows_bf,
                rows_bf,
                shaped((sz.qlen, edev)),
                shaped((2 * vp, 2 * edev)),
                shaped((2 * vp, edev)),
                shaped((sz.qlen, 2 * edev)),
            ],
            [sc],
            [
                dm, dt, *fetched[layer, 2],
                qq, kvv, stn, stf, qv, kvq, stv,
            ],
            name="section2_back",
            scratch=[pltpu.VMEM((sz.qlen, edev), BF16), pltpu.VMEM((2 * vp, edev), BF16)],
        )
        a, b = shares(part[0], part[1])
        args = window(a, [nm, nth, dm, dt, part[2], part[3], part[4], part[5], oq, ov])
        _, made = weights(
            lambda *r: section2_weights(sz, heads, *r), [], [straight], 8 * edev, args, 2 * edev, "section2_weights"
        )
        b, _ = seal(index, b, [], made)
        index += 1
        grad, dy, sums2 = close(grad, a, b, kept2, layer, 2)

        dm, dt = pair(dy)
        _, nm, nth, nvw, qkvv, ov, stv, qkvq, oq, stn, stf = kept1
        part = call(
            lambda *r: section1_back(sz, heads, *r),
            [
                rows_bf,
                rows_bf,
                shaped((sz.vis, 3 * edev)),
                shaped((sz.qlen, 3 * edev)),
                shaped((heads, sz.vis, sz.vis)),
            ],
            [sc],
            [
                dm, dt, *fetched[layer, 1],
                Part(bias_all, layer), qkvv, stv, qkvq, stn, stf,
            ],
            name="section1_back",
            scratch=[pltpu.VMEM((sz.qlen, edev), BF16), pltpu.VMEM((sz.vis, edev), BF16)],
        )
        a, b = shares(part[0], part[1])
        args = window(a, [nm, nth, dm, dt, nvw, part[2], part[3], oq, ov])
        _, made = weights(
            lambda *r: section1_weights(sz, heads, *r), [], [straight], 8 * edev, args, 3 * edev, "section1_weights"
        )
        b, _ = seal(index, b, [], made)
        (table,) = call(table_grad, [shaped((8, TABLE_PAD), F32)], [], [part[4], spread], name="table_grad")
        index += 1
        grad, dy, sums1 = close(grad, a, b, kept1, layer, 0)
        bias_sums = sums1
        grads[layer] = (sums1, sums2, sums3, out_bias_sums, db, table)

    if halving:
        for r in reductions:
            while r.step < bits:
                r.advance()

    own_total = piece_of(grad, chip) + (own_grad - rounded_grad)
    grad_v, grad_q = own_total[0:vq], own_total[sz.vpiece :]

    def summed(x, axis, size, steps):
        for bit in steps:
            x = x + lax.ppermute(x, axis, [(i, i ^ bit) for i in range(size)])
        return x

    per_norm = 14 * layers
    count = -(-(per_norm + (2 + heads) * layers) // 8) * 8
    (rows,) = call(
        lambda *r: collect(layers, heads, *r),
        [shaped((count, width), F32)],
        [],
        [x for g in grads for x in g],
        name="collect",
    )
    twice = lax.ppermute(rows, "tensor", swap)
    rows = rows + jnp.where(iota((count, 1), 0) < per_norm, twice, 0.0)
    rows = summed(rows, "dp", dp_size, [1 << k for k in range(bits)])
    scale_total, shift_total, out_bias_total, in_bias_total, rel_total = call(
        lambda *r: deal(layers, heads, *r),
        [shaped((6, layers, width), F32)] * 2
        + [shaped((layers, 2, width), F32), shaped((layers, 2, hid), F32), shaped((heads, layers, TABLE), F32)],
        [],
        [rows],
        name="deal",
    )

    d_up, d_down = call(
        lambda *r: finish_mlp(layers, *r),
        [shaped((layers, 2, block_rows, hid), F32)] * 2,
        [],
        feeds[::-1],
        name="finish_mlp",
    )
    sums = [reductions[2 * (layers - 1 - layer) : 2 * (layers - layer)] for layer in range(layers)]
    d_in, d_out = call(
        lambda *r: finish_attn(layers, *r),
        [shaped((layers, 4, 3, block_rows, edev), F32), shaped((layers, 4, edev, block_rows), F32)],
        [],
        [p for r in sums for p in r[1].pieces() + r[0].pieces()],
        name="finish_attn",
    )
    return (
        out_v[None],
        out_q[None],
        grad_v[None],
        grad_q[None],
        scale_total.transpose(1, 0, 2),
        shift_total.transpose(1, 0, 2),
        d_in.transpose(0, 1, 3, 2, 4),
        d_out,
        rel_total.transpose(1, 0, 2),
        d_up,
        in_bias_total,
        d_down.transpose(0, 1, 3, 2),
        out_bias_total,
    )


def solution(mesh):
    dp_size = mesh.shape["dp"]
    return jax.shard_map(
        lambda *args: on_device(dp_size, *args),
        mesh=mesh,
        in_specs=(
            P("dp", "tensor", None),
            P("dp", "tensor", None),
            P("dp", None),
            P("dp"),
            P("dp", None),
            P(),
            P(),
            P(None, None, None, None, "tensor"),
            P(None, None, "tensor", None),
            P(None, "tensor", None),
            P(None, None, None, "tensor"),
            P(None, None, "tensor"),
            P(None, None, "tensor", None),
            P(),
            P("dp", "tensor", None),
            P("dp", "tensor", None),
        ),
        out_specs=(
            P("dp", "tensor", None),
            P("dp", "tensor", None),
            P("dp", "tensor", None),
            P("dp", "tensor", None),
            P(),
            P(),
            P(None, None, "dp", None, "tensor"),
            P(None, None, "tensor", "dp"),
            P(None, "tensor", None),
            P(None, None, "dp", "tensor"),
            P(None, None, "tensor"),
            P(None, None, "tensor", "dp"),
            P(),
        ),
        check_vma=False,
    )
```

```python
import jax
import jax.numpy as jnp
from jax import lax
from jax.experimental import pallas as pl
from jax.experimental.pallas import tpu as pltpu
from jax.sharding import PartitionSpec as P

HDIM = 64
WIN = 12
SPAN = 2 * WIN - 1
EPS = 1e-05
NEG = -1000000000.0
OUT = -1e30
F32 = jnp.float32
BF16 = jnp.bfloat16
VMEM_LIMIT = 20 * 2**20


def nn(a, b):
    return lax.dot_general(a, b, (((1,), (0,)), ((), ())), preferred_element_type=F32)


def nt(a, b):
    return lax.dot_general(a, b, (((1,), (1,)), ((), ())), preferred_element_type=F32)


def tn(a, b):
    return lax.dot_general(a, b, (((0,), (0,)), ((), ())), preferred_element_type=F32)


class Part:
    def __init__(self, array, *lead):
        self.array, self.lead = array, lead
        self.rest = array.shape[len(lead) :]
        self.dtype = array.dtype
        self.size = 1
        for n in self.rest:
            self.size *= n


class Arriving:
    def __init__(self, ref, copy):
        self.ref, self.copy, self.shape = ref, copy, ref.shape

    def __getitem__(self, at):
        if self.copy is not None:
            self.copy.wait()
            self.copy = None
        return self.ref[at]


class Rows:
    def __init__(self, refs):
        self.spans = [r if isinstance(r, tuple) else (r, 0, r.shape[0]) for r in refs]

    def pieces(self, at):
        rows = at[0] if isinstance(at, tuple) else slice(None)
        total = sum(end - start for _, start, end in self.spans)
        lo, hi, _ = rows.indices(total)
        base = 0
        for ref, start, end in self.spans:
            first, last = max(lo - base, 0), min(hi - base, end - start)
            if first < last:
                yield ref, start + first, start + last, base + first - lo
            base += end - start

    def __getitem__(self, at):
        cols = at[1] if isinstance(at, tuple) else slice(None)
        parts = [ref[first:last, cols] for ref, first, last, _ in self.pieces(at)]
        return parts[0] if len(parts) == 1 else jnp.concatenate(parts, 0)

    def __setitem__(self, at, value):
        for ref, first, last, place in self.pieces(at):
            ref[first:last, :] = value[place : place + last - first, :]


def call(body, outs, scalars, args, name=None, scratch=()):
    vmem = pl.BlockSpec(memory_space=pltpu.VMEM)
    smem = pl.BlockSpec(memory_space=pltpu.SMEM)
    hbm = pl.BlockSpec(memory_space=pltpu.HBM)
    flat = [x for a in args for x in (a if isinstance(a, list) else [a])]
    flat_outs = [x for o in outs for x in (o if isinstance(o, list) else [o])]
    parts = [i for i, a in enumerate(flat) if isinstance(a, Part)]
    specs = [hbm if isinstance(a, Part) else vmem for a in flat]
    arrays = [a.array if isinstance(a, Part) else a for a in flat]
    landing = [pltpu.VMEM(flat[i].rest, flat[i].dtype) for i in parts]
    if parts:
        landing.append(pltpu.SemaphoreType.DMA((len(parts),)))
    first, end = len(scalars), len(scalars) + len(flat) + len(flat_outs) + len(scratch)

    def wrapped(*refs):
        refs = list(refs)
        buffers = refs[end:]
        coming = []
        for k, i in enumerate(parts):
            source = refs[first + i]
            if flat[i].lead:
                source = source.at[flat[i].lead]
            copy = pltpu.make_async_copy(source, buffers[k], buffers[-1].at[k])
            copy.start()
            coming.append(Arriving(buffers[k], copy))
            refs[first + i] = coming[-1]
        given = iter(refs[:end])
        grouped = [next(given) for _ in scalars]
        for x in list(args) + list(outs):
            grouped.append(Rows([next(given) for _ in x]) if isinstance(x, list) else next(given))
        body(*grouped, *given)
        for piece in coming:
            if piece.copy is not None:
                piece.copy.wait()

    got = iter(
        pl.pallas_call(
            wrapped,
            out_shape=tuple(flat_outs),
            in_specs=[smem] * len(scalars) + specs,
            out_specs=tuple(vmem for _ in flat_outs),
            scratch_shapes=list(scratch) + landing,
            compiler_params=pltpu.CompilerParams(vmem_limit_bytes=VMEM_LIMIT),
            cost_estimate=pl.CostEstimate(flops=1, bytes_accessed=1, transcendentals=0),
            name=name,
        )(*scalars, *arrays)
    )
    return [[next(got) for _ in o] if isinstance(o, list) else next(got) for o in outs]


def tie(*groups):
    return lax.optimization_barrier(groups)


def shaped(shape, dtype=BF16):
    return jax.ShapeDtypeStruct(shape, dtype)


class Sizes:
    def __init__(self, vis, qlen):
        self.vis, self.qlen = vis, qlen
        self.qh = qlen // 2
        self.vquart, self.qquart = vis // 4, qlen // 4
        self.vpiece = -(-self.vquart // 8) * 8
        self.vp = 2 * self.vpiece
        self.piece = self.vpiece + self.qquart
        self.half = 2 * self.piece
        self.near = self.half // 2
        self.q1 = self.near - self.vp
        self.q2 = self.half - self.near


def iota(shape, dim):
    return lax.broadcasted_iota(jnp.int32, shape, dim)


def div12(x):
    return (x * 171) >> 11


def patch_of(index, core, sz):
    second = (index >= sz.vp).astype(jnp.int32)
    row = index - second * sz.vp
    half = second + core - 2 * second * core
    late = (row >= sz.vpiece).astype(jnp.int32)
    row = row - late * sz.vpiece
    return jnp.where(row < sz.vquart, row + (2 * late + half) * sz.vquart, -1)


def query_of(index, core, sz):
    far = (index >= 2 * sz.q1).astype(jnp.int32)
    row = index - far * 2 * sz.q1
    size = sz.q1 + far * (sz.q2 - sz.q1)
    second = (row >= size).astype(jnp.int32)
    row = row - second * size + far * sz.q1
    half = second + core - 2 * second * core
    return row + jnp.where(row >= sz.qquart, sz.qquart, 0) + half * sz.qquart


def patch_rows(mine, theirs, sz):
    return jnp.concatenate([mine[0 : sz.vp, :], theirs[0 : sz.vp, :]], 0)


def near_rows(mine, theirs, sz):
    return jnp.concatenate([mine[sz.vp : sz.near, :], theirs[sz.vp : sz.near, :]], 0)


def far_rows(mine, theirs, sz):
    return jnp.concatenate([mine[sz.near :, :], theirs[sz.near :, :]], 0)


def query_rows(mine, theirs, sz):
    return jnp.concatenate([near_rows(mine, theirs, sz), far_rows(mine, theirs, sz)], 0)


def give_patches(mine, theirs, value, sz):
    mine[0 : sz.vp, :] = value[0 : sz.vp]
    theirs[0 : sz.vp, :] = value[sz.vp :]


def give_near(mine, theirs, value, sz):
    mine[sz.vp : sz.near, :] = value[0 : sz.q1]
    theirs[sz.vp : sz.near, :] = value[sz.q1 : 2 * sz.q1]


def window_permutation(sc, sz):
    core, down, right = sc[0], sc[2], sc[3]
    place = iota((sz.vis, sz.vp), 0)
    a = div12(place)
    b = place - a * WIN
    a = a + down
    b = b + right
    a = jnp.where(a >= WIN, a - WIN, a)
    b = jnp.where(b >= WIN, b - WIN, b)
    source = a * WIN + b
    stored = iota((sz.vis, sz.vp), 1)
    mine = (source == patch_of(stored, core, sz)).astype(F32).astype(BF16)
    theirs = (source == patch_of(stored + sz.vp, core, sz)).astype(F32).astype(BF16)
    return mine, theirs


def window_class(index, sc):
    a = div12(index)
    b = index - a * WIN
    return jnp.where(a >= WIN - sc[2], 2, 0) + jnp.where(b >= WIN - sc[3], 1, 0)


def window_mask(sc, sz):
    keys = window_class(iota((sz.vis, 1), 0), sc)
    asks = window_class(iota((1, sz.vis), 1), sc)
    keys = jnp.where(sc[4] > 0, keys, -1)
    return keys == asks


def self_mask(sc, sz, count, base):
    keys = query_of(iota((sz.qlen, 1), 0), sc[0], sz)
    asks = query_of(iota((1, count), 1) + base, sc[0], sz)
    return keys <= jnp.maximum(asks, sc[1] - 1)


def question_mask(sc, sz):
    return query_of(iota((sz.qlen, 1), 0), sc[0], sz) < sc[1]


def patch_pad(sc, sz):
    return patch_of(iota((2 * sz.vp, 1), 0), sc[0], sz) >= 0


def masked(scores, kind, sc, sz, base=0):
    if kind == "self":
        return jnp.where(self_mask(sc, sz, scores.shape[1], base), scores, NEG)
    if kind == "question":
        return jnp.where(question_mask(sc, sz), scores, NEG)
    if kind == "window":
        return jnp.where(window_mask(sc, sz), scores, NEG)
    real = patch_pad(sc, sz)
    return jnp.where(real & (sc[4] > 0), scores, jnp.where(real, NEG, OUT))


def allowed(kind, sc, sz):
    if kind == "self":
        return self_mask(sc, sz, sz.qlen, 0)
    if kind == "question":
        return question_mask(sc, sz)
    if kind == "window":
        return window_mask(sc, sz)
    return patch_pad(sc, sz) & (sc[4] > 0)


SCALE = HDIM**-0.5


def scaled(q):
    return (q.astype(F32) * SCALE).astype(BF16)


def attend(q, k, v, addend, kind, sc, sz, base):
    scores = nt(k, scaled(q))
    if addend is not None:
        scores = scores + addend
    scores = masked(scores, kind, sc, sz, base)
    top = jnp.max(scores, 0, keepdims=True)
    e = jnp.exp(scores - top)
    inv = 1.0 / jnp.sum(e, 0, keepdims=True)
    o_t = tn(v, (e * inv).astype(BF16))
    return o_t, top, inv


def attend_back(q, k, v, addend, kind, sc, sz, top, inv, do):
    q = scaled(q)
    scores = nt(k, q)
    if addend is not None:
        scores = scores + addend
    scores = masked(scores, kind, sc, sz)
    p = jnp.exp(scores - top) * inv
    dv = nn(p.astype(BF16), do)
    dp = nt(v, do)
    ds = p * (dp - jnp.sum(p * dp, 0, keepdims=True))
    if kind in ("patch", "window"):
        ds = jnp.where(allowed(kind, sc, sz), ds, 0.0)
    ds = ds.astype(BF16)
    dk = nn(ds, q)
    dq = tn(k, ds) * SCALE
    return dq, dk, dv, ds


def head(ref, part, h, heads):
    start = (part * heads + h) * HDIM
    return ref[:, start : start + HDIM]


def run_heads(q_of, k_of, v_of, bias, kind, sc, sz, o_ref, st_ref, heads, base=0):
    outs = []
    for h in range(heads):
        o_t, top, inv = attend(
            q_of(h), k_of(h), v_of(h), None if bias is None else bias[h], kind, sc, sz, base
        )
        outs.append(o_t)
        st_ref[h : h + 1, :] = top
        st_ref[heads + h : heads + h + 1, :] = inv
    o_ref[...] = jnp.concatenate(outs, 0).T.astype(BF16)


def section1_far(sz, sc, nm, nth, w1, qkvf):
    qkvf[0 : sz.q2, :] = nt(nm[...], w1[...]).astype(BF16)
    qkvf[sz.q2 :, :] = nt(nth[...], w1[...]).astype(BF16)


def section1_near(sz, heads, sc, nm, nth, qkvf, w0, w1, wo0, wo1, bias, pm, pt, nvw, qkvv, ov, stv, qkvn, on, stn, ow):
    vp = sz.vp
    mine, theirs = window_permutation(sc, sz)
    nv = (nn(mine, nm[0:vp, :]) + nn(theirs, nth[0:vp, :])).astype(BF16)
    nvw[...] = nv
    qkvv[...] = nt(nv, w0[...]).astype(BF16)
    run_heads(
        lambda h: head(qkvv, 0, h, heads),
        lambda h: head(qkvv, 1, h, heads),
        lambda h: head(qkvv, 2, h, heads),
        bias, "window", sc, sz, ow, stv, heads,
    )
    ov[0:vp, :] = tn(mine, ow[...]).astype(BF16)
    ov[vp : 2 * vp, :] = tn(theirs, ow[...]).astype(BF16)
    give_patches(pm, pt, nn(ov[...], wo0[...]).astype(BF16), sz)
    qkvn[0 : sz.q1, :] = nt(nm[vp:, :], w1[...]).astype(BF16)
    qkvn[sz.q1 :, :] = nt(nth[vp:, :], w1[...]).astype(BF16)
    every = Rows([qkvn, qkvf])
    run_heads(
        lambda h: head(qkvn, 0, h, heads),
        lambda h: head(every, 1, h, heads),
        lambda h: head(every, 2, h, heads),
        None, "self", sc, sz, on, stn, heads,
    )
    give_near(pm, pt, nn(on[...], wo1[...]).astype(BF16), sz)


def section1_rest(sz, heads, sc, qkvn, qkvf, wo1, pm, pt, of, stf):
    every = Rows([qkvn, qkvf])
    run_heads(
        lambda h: head(qkvf, 0, h, heads),
        lambda h: head(every, 1, h, heads),
        lambda h: head(every, 2, h, heads),
        None, "self", sc, sz, of, stf, heads, 2 * sz.q1,
    )
    pm[...] = nn(of[0 : sz.q2, :], wo1[...]).astype(BF16)
    pt[...] = nn(of[sz.q2 :, :], wo1[...]).astype(BF16)


def section2_near(sz, heads, sc, nm, nth, w2, w3, qv, kvv, qn, kvn, on, stn):
    e = heads * HDIM
    v = patch_rows(nm, nth, sz)
    q = near_rows(nm, nth, sz)
    qv[...] = nt(v, w3[0:e, :]).astype(BF16)
    kvv[...] = nt(v, w2[e:, :]).astype(BF16)
    qn[...] = nt(q, w2[0:e, :]).astype(BF16)
    kvn[...] = nt(q, w3[e:, :]).astype(BF16)
    run_heads(
        lambda h: head(qn, 0, h, heads),
        lambda h: head(kvv, 0, h, heads),
        lambda h: head(kvv, 1, h, heads),
        None, "patch", sc, sz, on, stn, heads,
    )


def section2_far(sz, heads, sc, nm, nth, kvv, w2, w3, wo2, pm, pt, qf, kvf, of, stf):
    e = heads * HDIM
    x = jnp.concatenate([nm[...], nth[...]], 0)
    qf[...] = nt(x, w2[0:e, :]).astype(BF16)
    kvf[...] = nt(x, w3[e:, :]).astype(BF16)
    run_heads(
        lambda h: head(qf, 0, h, heads),
        lambda h: head(kvv, 0, h, heads),
        lambda h: head(kvv, 1, h, heads),
        None, "patch", sc, sz, of, stf, heads,
    )
    pm[...] = nn(of[0 : sz.q2, :], wo2[...]).astype(BF16)
    pt[...] = nn(of[sz.q2 :, :], wo2[...]).astype(BF16)


def section2_rest(sz, heads, sc, qv, kvn, kvf, on, wo2, wo3, pm, pt, ov, stv):
    every = Rows([kvn, kvf])
    give_near(pm, pt, nn(on[...], wo2[...]).astype(BF16), sz)
    run_heads(
        lambda h: head(qv, 0, h, heads),
        lambda h: head(every, 0, h, heads),
        lambda h: head(every, 1, h, heads),
        None, "question", sc, sz, ov, stv, heads,
    )
    give_patches(pm, pt, nn(ov[...], wo3[...]).astype(BF16), sz)


GELU_C = 0.7978845608028654
GELU_A = 0.044715


def section3(sz, layer, spans, nm, nth, wi, bi, wo, pm, pt, g, gp):
    count = g.shape[0] // 2
    for ref, out, base in ((nm, pm, 0), (nth, pt, count)):
        for lo, hi, e in spans:
            h = nn(ref[lo:hi, :], wi[e]) + bi[layer, e : e + 1, :]
            h2 = h * h
            t = jnp.tanh(GELU_C * h * (1.0 + GELU_A * h2))
            half_t = 0.5 + 0.5 * t
            act = (h * half_t).astype(BF16)
            slope = half_t + (0.5 * GELU_C) * h * (1.0 - t * t) * (1.0 + 3.0 * GELU_A * h2)
            g[base + lo : base + hi, :] = act
            gp[base + lo : base + hi, :] = slope.astype(BF16)
            out[lo:hi, :] = nn(act, wo[e]).astype(BF16)


def section3_back(sz, dm, dt, wi, wo, gp, pm, pt, dh):
    vp, half = sz.vp, sz.half
    for ref, out, base in ((dm, pm, 0), (dt, pt, half)):
        for lo, hi, e in ((0, vp, 0), (vp, half, 1)):
            dg = nt(ref[lo:hi, :], wo[e])
            d = (dg * gp[base + lo : base + hi, :].astype(F32)).astype(BF16)
            dh[base + lo : base + hi, :] = d
            out[lo:hi, :] = nt(d, wi[e]).astype(BF16)


def back_heads(q_of, k_of, v_of, bias, kind, sc, sz, st, do_of, ds_ref, heads):
    dqs, dks, dvs = [], [], []
    for h in range(heads):
        dq, dk, dv, ds = attend_back(
            q_of(h), k_of(h), v_of(h), None if bias is None else bias[h], kind, sc, sz,
            st[h : h + 1, :], st[heads + h : heads + h + 1, :], do_of(h),
        )
        dqs.append(dq)
        dks.append(dk)
        dvs.append(dv)
        if ds_ref is not None:
            ds_ref[h] = ds
    dq = jnp.concatenate(dqs, 0).T.astype(BF16)
    dkv = jnp.concatenate(dks + dvs, 1).astype(BF16)
    return dq, dkv


def stats(near, far):
    return jnp.concatenate([near[...], far[...]], 1)


def give_queries(mine, theirs, value, sz):
    give_near(mine, theirs, value[0 : 2 * sz.q1], sz)
    mine[sz.near :, :] = value[2 * sz.q1 : 2 * sz.q1 + sz.q2]
    theirs[sz.near :, :] = value[2 * sz.q1 + sz.q2 :]


def section2_back(
    sz, heads, sc, dm, dt, w2, w3, wo2, wo3, qq, kvv, stn, stf, qv, kvq, stv, pm, pt, dqq, dkvv, dqv, dkvq, doq, dov
):
    e = heads * HDIM
    doq[...] = nt(query_rows(dm, dt, sz), wo2[...]).astype(BF16)
    dov[...] = nt(patch_rows(dm, dt, sz), wo3[...]).astype(BF16)
    dq, dkv = back_heads(
        lambda h: head(qq, 0, h, heads),
        lambda h: head(kvv, 0, h, heads),
        lambda h: head(kvv, 1, h, heads),
        None, "patch", sc, sz, stats(stn, stf), lambda h: head(doq, 0, h, heads), None, heads,
    )
    dqq[...] = dq
    dkvv[...] = dkv
    dq, dkv = back_heads(
        lambda h: head(qv, 0, h, heads),
        lambda h: head(kvq, 0, h, heads),
        lambda h: head(kvq, 1, h, heads),
        None, "question", sc, sz, stv, lambda h: head(dov, 0, h, heads), None, heads,
    )
    dqv[...] = dq
    dkvq[...] = dkv
    give_queries(pm, pt, (nn(dqq[...], w2[0:e, :]) + nn(dkvq[...], w3[e:, :])).astype(BF16), sz)
    give_patches(pm, pt, (nn(dqv[...], w3[0:e, :]) + nn(dkvv[...], w2[e:, :])).astype(BF16), sz)


def section1_back(
    sz, heads, sc, dm, dt, w0, w1, wo0, wo1, bias, qkvv, stv, qkvq, stn, stf, pm, pt, dqkvv, dqkvq, ds, doq, dov
):
    vp = sz.vp
    e = heads * HDIM
    mine, theirs = window_permutation(sc, sz)
    do_m = nt(dm[0:vp, :], wo0[...]).astype(BF16)
    do_t = nt(dt[0:vp, :], wo0[...]).astype(BF16)
    dov[...] = (nn(mine, do_m) + nn(theirs, do_t)).astype(BF16)
    dq, dkv = back_heads(
        lambda h: head(qkvv, 0, h, heads),
        lambda h: head(qkvv, 1, h, heads),
        lambda h: head(qkvv, 2, h, heads),
        bias, "window", sc, sz, stv, lambda h: head(dov, 0, h, heads), ds, heads,
    )
    dqkvv[:, 0:e] = dq
    dqkvv[:, e:] = dkv
    dn = nn(dqkvv[...], w0[...]).astype(BF16)
    pm[0:vp, :] = tn(mine, dn).astype(BF16)
    pt[0:vp, :] = tn(theirs, dn).astype(BF16)
    doq[...] = nt(query_rows(dm, dt, sz), wo1[...]).astype(BF16)
    dq, dkv = back_heads(
        lambda h: head(qkvq, 0, h, heads),
        lambda h: head(qkvq, 1, h, heads),
        lambda h: head(qkvq, 2, h, heads),
        None, "self", sc, sz, stats(stn, stf), lambda h: head(doq, 0, h, heads), None, heads,
    )
    dqkvq[:, 0:e] = dq
    dqkvq[:, e:] = dkv
    give_queries(pm, pt, nn(dqkvq[...], w1[...]).astype(BF16), sz)


def kept_order(order):
    return sorted(range(1 << len(order)), key=lambda r: [(r >> k) & 1 for k in order])


def store_blocks(sc, store, col, value):
    keep, send, scr, order = store
    width = value.shape[1]
    value = value.astype(BF16)
    cols = slice(col, col + width)
    if send is None:
        keep[0, :, cols] = value
        return
    count, rows = keep.shape[0], keep.shape[1]
    scr[:, 0:width] = value
    for slot, relative in enumerate(kept_order(order)):
        owner = relative ^ sc[5]
        block = scr[pl.ds(pl.multiple_of(owner * rows, 16), rows), 0:width]
        if slot < count:
            keep[slot, :, cols] = block
        else:
            send[slot - count, :, cols] = block


def section3_weights(sz, sc, nm, nth, dm, dt, g, dh, db, out):
    vp, half = sz.vp, sz.half
    hid = dh.shape[1]
    for e, lo, hi in ((0, 0, vp), (1, vp, half)):
        into = tn(nm[lo:hi, :], dh[lo:hi, :]) + tn(nth[lo:hi, :], dh[half + lo : half + hi, :])
        away = tn(dm[lo:hi, :], g[lo:hi, :]) + tn(dt[lo:hi, :], g[half + lo : half + hi, :])
        out[:, e * hid : (e + 1) * hid] = into.astype(BF16)
        out[:, (2 + e) * hid : (3 + e) * hid] = away.astype(BF16)
        db[e : e + 1, :] = jnp.sum(dh[lo:hi, :].astype(F32), 0, keepdims=True) + jnp.sum(
            dh[half + lo : half + hi, :].astype(F32), 0, keepdims=True
        )


def section2_weights(sz, heads, sc, nm, nth, dm, dt, dqq, dkvv, dqv, dkvq, oq, ov, store):
    e = heads * HDIM
    nq, nv = query_rows(nm, nth, sz), patch_rows(nm, nth, sz)
    store_blocks(sc, store, 0, tn(nq, dqq[...]))
    store_blocks(sc, store, e, tn(nv, dkvv[...]))
    store_blocks(sc, store, 3 * e, tn(nv, dqv[...]))
    store_blocks(sc, store, 4 * e, tn(nq, dkvq[...]))
    store_blocks(sc, store, 6 * e, tn(query_rows(dm, dt, sz), oq[...]))
    store_blocks(sc, store, 7 * e, tn(patch_rows(dm, dt, sz), ov[...]))


def section1_weights(sz, heads, sc, nm, nth, dm, dt, nvw, dqkvv, dqkvq, oq, ov, store):
    e = heads * HDIM
    store_blocks(sc, store, 0, tn(nvw[...], dqkvv[...]))
    store_blocks(sc, store, 3 * e, tn(query_rows(nm, nth, sz), dqkvq[...]))
    store_blocks(sc, store, 6 * e, tn(patch_rows(dm, dt, sz), ov[...]))
    store_blocks(sc, store, 7 * e, tn(query_rows(dm, dt, sz), oq[...]))


def in_order(sz, chip, own, other, out):
    v, piece = sz.vpiece, sz.piece
    mine, theirs = own[...].astype(F32), other[...].astype(F32)
    first = jnp.where(chip == 0, mine, theirs)
    second = jnp.where(chip == 0, theirs, mine)
    out[0:v, :] = first[0:v]
    out[v : 2 * v, :] = second[0:v]
    out[2 * v : v + piece, :] = first[v:]
    out[v + piece :, :] = second[v:]


def norm_rows(x):
    center = x - jnp.mean(x, -1, keepdims=True)
    inv = lax.rsqrt(jnp.mean(center * center, -1, keepdims=True) + EPS)
    return center * inv, inv


def open_stream(sz, sc, own, other, scale, shift, x, n):
    layer = first = 0
    in_order(sz, sc[6], own, other, x)
    for lo, hi, e in ((0, sz.vp, 0), (sz.vp, sz.half, 1)):
        gain, bias = scale[first + e, layer : layer + 1, :], shift[first + e, layer : layer + 1, :]
        n[lo:hi, :] = (norm_rows(x[lo:hi, :])[0] * gain + bias).astype(BF16)


def open_grad(sz, sc, own, other, grad, dy, sums):
    in_order(sz, sc[6], own, other, grad)
    dy[...] = grad[...].astype(BF16)
    for lo, hi, e in ((0, sz.vp, 0), (sz.vp, sz.half, 1)):
        sums[4 + e : 5 + e, :] = jnp.sum(grad[lo:hi, :], 0, keepdims=True)


def add_norm(spans, layer, first, x, a, b, extra, scale, shift, y, n):
    for lo, hi, e in spans:
        gain, bias = scale[first + e, layer : layer + 1, :], shift[first + e, layer : layer + 1, :]
        value = x[lo:hi, :] + (a[lo:hi, :].astype(F32) + b[lo:hi, :].astype(F32))
        if extra is not None:
            value = value + extra[layer - 1, e : e + 1, :]
        y[lo:hi, :] = value
        n[lo:hi, :] = (norm_rows(value)[0] * gain + bias).astype(BF16)


def norm_back(sz, layer, first, d, a, b, x, scale, out, dy, sums):
    for lo, hi, e in ((0, sz.vp, 0), (sz.vp, sz.half, 1)):
        dn = a[lo:hi, :].astype(F32) + b[lo:hi, :].astype(F32)
        unit, inv = norm_rows(x[lo:hi, :])
        du = dn * scale[first + e, layer : layer + 1, :]
        dx = inv * (
            du
            - jnp.mean(du, -1, keepdims=True)
            - unit * jnp.mean(du * unit, -1, keepdims=True)
        )
        value = d[lo:hi, :] + dx
        out[lo:hi, :] = value
        dy[lo:hi, :] = value.astype(BF16)
        sums[e : e + 1, :] = jnp.sum(dn * unit, 0, keepdims=True)
        sums[2 + e : 3 + e, :] = jnp.sum(dn, 0, keepdims=True)
        sums[4 + e : 5 + e, :] = jnp.sum(value, 0, keepdims=True)


TABLE = SPAN * SPAN
TABLE_PAD = -(-TABLE // 128) * 128
CELLS_PAD = -(-SPAN * WIN // 128) * 128


def spread_matrix():
    cell = iota((TABLE_PAD, CELLS_PAD), 1)
    row = (cell * 171) >> 11
    place = row * SPAN + cell - row * WIN
    return ((iota((TABLE_PAD, CELLS_PAD), 0) == place) & (cell < SPAN * WIN)).astype(F32)


def table_bias(tables, out, spread, rows):
    spread[...] = spread_matrix()
    count = out.shape[0]
    for i in range(count):
        table = tables[i : i + 1, :]
        for b in range(WIN):
            at = i * WIN + b
            rows[at : at + 1, :] = pltpu.roll(table, (TABLE_PAD - (WIN - 1 - b)) % TABLE_PAD, 1)
    cells = jnp.dot(rows[...], spread[...], precision=lax.Precision.HIGHEST, preferred_element_type=F32)
    for a in range(WIN):
        moved = pltpu.roll(cells, (CELLS_PAD - WIN * (WIN - 1 - a)) % CELLS_PAD, 1)
        for i in range(count):
            out[i, WIN * a : WIN * (a + 1), :] = moved[WIN * i : WIN * (i + 1), 0 : WIN * WIN]


def table_grad(ds, spread, out):
    heads = ds.shape[0]
    rows = jnp.zeros((WIN, CELLS_PAD - WIN * WIN), F32)
    every = []
    for h in range(heads):
        grad = ds[h].astype(F32)
        cells = jnp.zeros((WIN, CELLS_PAD), F32)
        for a in range(WIN):
            part = jnp.concatenate([grad[WIN * a : WIN * (a + 1), :], rows], 1)
            cells = cells + pltpu.roll(part, WIN * (WIN - 1 - a), 1)
        every.append(cells)
    places = lax.dot_general(
        jnp.concatenate(every, 0),
        spread[...],
        (((1,), (1,)), ((), ())),
        precision=lax.Precision.HIGHEST,
        preferred_element_type=F32,
    )
    for h in range(heads):
        total = jnp.zeros((1, TABLE_PAD), F32)
        for b in range(WIN):
            total = total + pltpu.roll(places[h * WIN + b : h * WIN + b + 1, :], WIN - 1 - b, 1)
        out[h : h + 1, :] = total


def collect(layers, heads, *refs):
    out = refs[-1]
    out[...] = jnp.zeros(out.shape, F32)
    row = 0
    for layer in range(layers):
        sums1, sums2, sums3, after = refs[6 * layer : 6 * layer + 4]
        for ref, lo, count in ((sums1, 0, 4), (sums2, 0, 4), (sums3, 0, 4), (after, 4, 2)):
            out[row : row + count, :] = ref[lo : lo + count, :]
            row += count
    for layer in range(layers):
        db, table = refs[6 * layer + 4 : 6 * layer + 6]
        out[row : row + 2, :] = db[...]
        row += 2
        out[row : row + heads, 0:TABLE_PAD] = table[0:heads, :]
        row += heads


def deal(layers, heads, rows, scale, shift, out_bias, in_bias, rel):
    for layer in range(layers):
        at = 14 * layer
        for section in range(3):
            for e in range(2):
                scale[2 * section + e, layer : layer + 1, :] = rows[at + 4 * section + e : at + 4 * section + e + 1, :]
                row = at + 4 * section + 2 + e
                shift[2 * section + e, layer : layer + 1, :] = rows[row : row + 1, :]
        out_bias[layer] = rows[at + 12 : at + 14, :]
        at = 14 * layers + (2 + heads) * layer
        in_bias[layer] = rows[at : at + 2, :]
        for h in range(heads):
            rel[h, layer : layer + 1, :] = rows[at + 2 + h : at + 3 + h, 0:TABLE]


def finish_mlp(layers, *refs):
    up, down = refs[layers:]
    hid = up.shape[3]
    for layer in range(layers):
        total = refs[layer][...].astype(F32)
        for e in range(2):
            up[layer, e] = total[:, e * hid : (e + 1) * hid]
            down[layer, e] = total[:, (2 + e) * hid : (3 + e) * hid]


def finish_attn(layers, *refs):
    d_in, d_out = refs[8 * layers :]
    e = d_in.shape[4]
    for layer in range(layers):
        for pair in range(2):
            first = 8 * layer + 4 * pair
            total = sum(r[...].astype(F32) for r in refs[first : first + 4])
            for which in range(2):
                for c in range(3):
                    col = (3 * which + c) * e
                    d_in[layer, 2 * pair + which, c] = total[:, col : col + e]
                col = (6 + which) * e
                d_out[layer, 2 * pair + which] = total[:, col : col + e].T


def on_device(
    dp_size,
    visual,
    queries,
    valid_windows,
    answer_start,
    shifts,
    norm_scale,
    norm_shift,
    attn_in,
    attn_out,
    rel_bias,
    mlp_in,
    mlp_in_bias,
    mlp_out,
    mlp_out_bias,
    grad_visual_out,
    grad_query_out,
):
    layers, width = attn_in.shape[0], attn_in.shape[2]
    edev = attn_in.shape[4]
    heads = edev // HDIM
    hid = mlp_in.shape[3]
    sz = Sizes(4 * visual.shape[1], 4 * queries.shape[1])
    half, vp, qh = sz.half, sz.vp, sz.qh
    vq, qq_ = sz.vquart, sz.qquart
    t_index = lax.axis_index("tensor")
    d_index = lax.axis_index("dp")
    core, chip = t_index % 2, t_index // 2
    swap = [(i, i ^ 1) for i in range(4)]
    cross = [(i, i ^ 2) for i in range(4)]
    block_rows = width // dp_size
    halving = dp_size > 1 and dp_size & (dp_size - 1) == 0 and block_rows % 16 == 0
    bits = dp_size.bit_length() - 1

    def scalars(layer):
        on = layer % 2
        values = [core, answer_start[0], shifts[0, 0] * on, shifts[0, 1] * on, valid_windows[0, 0], d_index, chip, 0]
        return jnp.stack(values).astype(jnp.int32)

    w_in = attn_in.transpose(0, 1, 3, 4, 2).reshape(layers, 4, 3 * edev, width)
    scale, shift = norm_scale.transpose(1, 0, 2), norm_shift.transpose(1, 0, 2)

    def packed(own_v, own_q):
        pad = jnp.zeros((sz.vpiece - vq, width), own_v.dtype)
        return jnp.concatenate([own_v, pad, own_q], 0)

    def piece_of(rows, place):
        v = jnp.where(place == 0, rows[0 : sz.vpiece], rows[sz.vpiece : vp])
        q = jnp.where(place == 0, rows[vp : vp + qq_], rows[vp + qq_ :])
        return jnp.concatenate([v, q], 0)

    def core_swap(x):
        if isinstance(x, list):
            return [core_swap(p) for p in x]
        return lax.ppermute(x, "tensor", swap)

    def across(x):
        return lax.ppermute(x, "tensor", cross)

    def pair_sum(mine, theirs):
        got = core_swap(theirs)
        if not isinstance(got, list):
            return (mine.astype(F32) + got.astype(F32)).astype(BF16)

        def body(a, b, out):
            out[...] = (a[...].astype(F32) + b[...].astype(F32)).astype(BF16)

        return call(body, [shaped(mine.shape)], [], [mine, got], name="pair_sum")[0]

    def pair(x):
        return x, core_swap(x)

    far = half - sz.near
    near_bf, far_bf = shaped((sz.near, width)), shaped((far, width))

    def halved(rows):
        first = -(-rows // 32) * 16
        return [shaped((first, width)), shaped((rows - first, width))]

    near_two, far_two = halved(sz.near), halved(far)
    rows_bf = [shaped((half, width))]
    rows_f = shaped((half, width), F32)
    near_spans = ((0, vp, 0), (vp, sz.near, 1))
    far_spans = ((0, far, 1),)

    def natural(near_part, far_part):
        return Rows(
            [
                (near_part, 0, sz.near),
                (far_part, 0, far),
                (near_part, sz.near, 2 * sz.near),
                (far_part, far, 2 * far),
            ]
        )

    own = packed(visual[0], queries[0])
    other = lax.ppermute(own, "tensor", cross)
    tables = jnp.pad(rel_bias.reshape(layers * heads, TABLE), ((0, 0), (0, TABLE_PAD - TABLE)))
    bias_all, spread = call(
        table_bias,
        [shaped((layers * heads, sz.vis, sz.vis), F32), shaped((TABLE_PAD, CELLS_PAD), F32)],
        [],
        [tables],
        name="table_bias",
        scratch=[pltpu.VMEM((layers * heads * WIN, TABLE_PAD), F32)],
    )
    bias_all = bias_all.reshape(layers, heads, sz.vis, sz.vis)
    scal = [scalars(layer) for layer in range(layers)]
    own_grad = packed(grad_visual_out[0], grad_query_out[0])
    rounded_grad = lax.reduce_precision(own_grad, 8, 7)

    def next_norm(spans, x, a, b, layer, first, extra=False):
        args = [x, a, b] + ([mlp_out_bias] if extra else []) + [scale, shift]

        def body(x, a, b, *rest):
            if not extra:
                rest = (None,) + rest
            add_norm(spans, layer, first, x, a, b, *rest)

        return call(body, [shaped(x.shape, F32), halved(x.shape[0])], [], args, name="norm")

    fetched = {}

    def fetch(layer, section, after):
        if section == 3:
            arrays = [mlp_in, mlp_out]
            blocks = [(0, (layer,)), (1, (layer,))]
        else:
            arrays = [w_in, attn_out]
            first = 2 * (section - 1)
            blocks = [(0, (layer, first)), (0, (layer, first + 1)), (1, (layer, first)), (1, (layer, first + 1))]
        arrays = tie(after, arrays)[1]
        outs = [shaped(arrays[k].shape[len(lead) :]) for k, lead in blocks]
        marked = outs + [shaped((8, 128), F32)]

        def body(one, two, *refs):
            refs[len(outs)][...] = jnp.zeros((8, 128), F32)
            copies = [
                pltpu.make_async_copy((one, two)[k].at[lead], refs[j], refs[-1].at[j])
                for j, (k, lead) in enumerate(blocks)
            ]
            for copy in copies:
                copy.start()
            for copy in copies:
                copy.wait()

        *fetched[layer, section], mark = pl.pallas_call(
            body,
            out_shape=marked,
            in_specs=[pl.BlockSpec(memory_space=pltpu.HBM)] * 2,
            out_specs=[pl.BlockSpec(memory_space=pltpu.VMEM)] * len(marked),
            scratch_shapes=[pltpu.SemaphoreType.DMA((len(outs),))],
            compiler_params=pltpu.CompilerParams(vmem_limit_bytes=VMEM_LIMIT),
            name="fetch",
        )(*arrays)
        return mark

    def fetch_beside(layer, section, a, b):
        fetch(layer, section, a)
        b, fetched[layer, section] = tie(b, fetched[layer, section])
        return b

    mark = fetch(0, 1, own)
    sent_grad = rounded_grad.astype(BF16)
    opening, bias_all, spread = tie(scal[0], bias_all, spread)

    def open_body(sc, own, other, scale, shift, mark, *refs):
        open_stream(sz, sc, own, other, scale, shift, *refs[:-1])
        refs[-1][...] = jnp.zeros(refs[-1].shape, F32)

    (x_near, x_far), pieces, token = call(
        open_body,
        [
            [shaped((sz.near, width), F32), shaped((far, width), F32)],
            near_two + far_two,
            shaped((8, 128), F32),
        ],
        [opening],
        [own, other, scale, shift, mark],
        name="open_stream",
    )
    sent_grad, token = tie(sent_grad, token)
    other_grad = across(sent_grad)
    near_sc, other_grad = tie(scal[0], other_grad)
    n_near, n_far = pieces[0:2], pieces[2:4]

    saved = []
    for layer in range(layers):
        sc = scal[layer]
        w0, w1, wo0, wo1 = fetched[layer, 1]
        if layer > 0:
            got_far, _ = tie(got_far, kept_near)
            got_far, fetched[layer, 1] = tie(got_far, fetched[layer, 1])
            w0, w1, wo0, wo1 = fetched[layer, 1]
            x_far, n_far = next_norm(far_spans, x_far, kept_far, got_far, layer, 0, True)
        t_far = core_swap(n_far)
        first = [token] if layer == 0 else []
        (qkvf,) = call(
            lambda sc, nm, nth, w1, *r: section1_far(sz, sc, nm, nth, w1, r[-1]),
            [shaped((2 * far, 3 * edev))],
            [sc],
            [n_far, t_far, w1] + first,
            name="section1",
        )
        if layer > 0:
            got_near, qkvf = tie(got_near, qkvf)
            x_near, n_near = next_norm(near_spans, x_near, kept_near, got_near, layer, 0, True)
        t_near = core_swap(n_near)
        x1, n1, t1 = [x_near, x_far], n_near + n_far, t_near + t_far
        pm, pt, nvw, qkvv, ov, stv, qkvn, on, stn = call(
            lambda *r: section1_near(sz, heads, *r),
            [
                near_bf,
                near_two,
                shaped((sz.vis, width)),
                shaped((sz.vis, 3 * edev)),
                shaped((2 * vp, edev)),
                shaped((8, sz.vis), F32),
                shaped((2 * sz.q1, 3 * edev)),
                shaped((2 * sz.q1, edev)),
                shaped((8, 2 * sz.q1), F32),
            ],
            [sc],
            [n_near, t_near, qkvf, w0, w1, wo0, wo1, Part(bias_all, layer)],
            name="section1",
            scratch=[pltpu.VMEM((sz.vis, edev), BF16)],
        )
        kept_near = pair_sum(pm, pt)
        got_near = across(kept_near)
        _, later = tie(kept_near, qkvn)
        pm, pt, of, stf = call(
            lambda *r: section1_rest(sz, heads, *r),
            [far_bf, far_two, shaped((2 * far, edev)), shaped((8, 2 * far), F32)],
            [sc if layer else near_sc],
            [later, qkvf, wo1],
            name="section1",
        )
        saved1 = (x1, n1, t1, nvw, qkvv, ov, stv, [qkvn, qkvf], [on, of], stn, stf)
        kept_far = pair_sum(pm, pt)
        got_far = across(kept_far)

        fetch(layer, 2, kept_near)
        got_near, fetched[layer, 2], _ = tie(got_near, fetched[layer, 2], kept_far)
        if layer == 0:
            other_grad, sent_grad, _ = tie(other_grad, sent_grad, kept_far)
            grad, dy, grad_sums = call(
                lambda *r: open_grad(sz, *r),
                [rows_f, rows_bf, shaped((8, width), F32)],
                scal[0:1],
                [sent_grad, other_grad],
                name="open_grad",
            )
            got_near, grad, dy = tie(got_near, grad, dy)
        w2, w3, wo2, wo3 = fetched[layer, 2]
        x_near, n_near = next_norm(near_spans, x_near, kept_near, got_near, layer, 2)
        t_near = core_swap(n_near)
        qv, kvv, qn, kvn, on, stn = call(
            lambda *r: section2_near(sz, heads, *r),
            [
                shaped((2 * vp, edev)),
                shaped((2 * vp, 2 * edev)),
                shaped((2 * sz.q1, edev)),
                shaped((2 * sz.q1, 2 * edev)),
                shaped((2 * sz.q1, edev)),
                shaped((8, 2 * sz.q1), F32),
            ],
            [sc],
            [n_near, t_near, w2, w3],
            name="section2",
        )
        got_far, kvv = tie(got_far, kvv)
        x_far, n_far = next_norm(far_spans, x_far, kept_far, got_far, layer, 2)
        t_far = core_swap(n_far)
        pm, pt, qf, kvf, of, stf = call(
            lambda *r: section2_far(sz, heads, *r),
            [
                far_bf,
                far_two,
                shaped((2 * far, edev)),
                shaped((2 * far, 2 * edev)),
                shaped((2 * far, edev)),
                shaped((8, 2 * far), F32),
            ],
            [sc],
            [n_far, t_far, kvv, w2, w3, wo2],
            name="section2",
        )
        x2, n2, t2 = [x_near, x_far], n_near + n_far, t_near + t_far
        kept_far = pair_sum(pm, pt)
        got_far = across(kept_far)
        _, later = tie(kept_far, qv)
        pm, pt, ov, stv = call(
            lambda *r: section2_rest(sz, heads, *r),
            [near_bf, near_two, shaped((2 * vp, edev)), shaped((8, 2 * vp), F32)],
            [sc],
            [later, kvn, kvf, on, wo2, wo3],
            name="section2",
        )
        saved2 = (x2, n2, t2, [qn, qf], kvv, [on, of], stn, stf, qv, [kvn, kvf], ov, stv)
        kept_near = pair_sum(pm, pt)
        got_near = across(kept_near)

        fetch(layer, 3, kept_far)
        got_far, fetched[layer, 3], _ = tie(got_far, fetched[layer, 3], kept_near)
        up, down = fetched[layer, 3]

        def feed_forward(spans, n, t):
            rows = sum(p.shape[0] for p in n)
            return call(
                lambda *r: section3(sz, layer, spans, *r),
                [shaped((rows, width)), halved(rows)] + [shaped((2 * rows, hid))] * 2,
                [],
                [n, t, up, mlp_in_bias, down],
                name="section3",
            )

        x_far, n_far = next_norm(far_spans, x_far, kept_far, got_far, layer, 4)
        t_far = core_swap(n_far)
        pm, pt, act_far, slope_far = feed_forward(far_spans, n_far, t_far)
        kept_far = pair_sum(pm, pt)
        if layer + 1 < layers:
            got_far = across(kept_far)
        got_near, _ = tie(got_near, kept_far)
        x_near, n_near = next_norm(near_spans, x_near, kept_near, got_near, layer, 4)
        t_near = core_swap(n_near)
        pm, pt, act_near, slope_near = feed_forward(near_spans, n_near, t_near)
        kept_near = pair_sum(pm, pt)
        if layer + 1 < layers:
            got_near = across(kept_near)
            fetch(layer + 1, 1, kept_far)
        x3, n3, t3 = [x_near, x_far], n_near + n_far, t_near + t_far
        saved3 = (x3, n3, t3, (act_near, act_far), (slope_near, slope_far))
        saved.append((saved1, saved2, saved3))
    stream = jnp.concatenate([x_near, x_far], 0)
    last = jnp.concatenate([kept_near, kept_far], 0)
    away = lax.ppermute(piece_of(last, 1 - chip), "tensor", cross)
    out = piece_of(stream, chip) + (piece_of(last, chip).astype(F32) + away.astype(F32))
    out_v = (out[0:vq] + mlp_out_bias[layers - 1, 0]).astype(BF16)
    out_q = (out[sz.vpiece :] + mlp_out_bias[layers - 1, 1]).astype(BF16)

    bias_sums = grad_sums

    def whole_sum(rows):
        return lax.psum_scatter(rows, "dp", scatter_dimension=0, tiled=True)

    def shares(mine, theirs):
        kept = [pair_sum(m, t) for m, t in zip(mine, theirs)]
        return kept, [across(k) for k in kept]

    class Reduction:
        def __init__(self, outs, order):
            self.order = order
            if halving:
                self.parts, self.step = [outs[0]], 0
                self.ready = outs[1]
                self.move()
            else:
                self.sum = whole_sum(outs[0][0])
                self.step = bits

        def move(self):
            bit = 1 << self.order[self.step]
            got = lax.ppermute(self.ready, "dp", [(i, i ^ bit) for i in range(dp_size)])
            self.parts.append(got)
            self.step += 1

        def advance(self):
            count = 1 << (bits - 1 - self.step)
            self.ready = sum(p[count : 2 * count].astype(F32) for p in self.parts).astype(BF16)
            self.move()

        def pieces(self):
            if not halving:
                zero = jnp.zeros_like(self.sum)
                return [self.sum, zero, zero, zero]
            lead = [Part(p, 0) for p in self.parts]
            while len(lead) < 4:
                lead.append(jnp.zeros(lead[0].rest, BF16))
            return lead

    def close(grad, a, b, kept, layer, first):
        return call(
            lambda *r: norm_back(sz, layer, first, *r),
            [rows_f, rows_bf, shaped((8, width), F32)],
            [],
            [grad, a, b, kept[0], scale],
            name="norm_back",
        )

    straight = tuple(range(bits))
    turned = straight[1:] + straight[:1]

    def weights(body, extra_outs, orders, columns, args, wide, name):
        outs = []
        for _ in orders:
            if halving:
                outs += [shaped((dp_size // 2, block_rows, columns))] * 2
            else:
                outs += [shaped((1, width, columns))]
        lead = 1 + len(args) + len(extra_outs)
        each = 2 if halving else 1

        def wrapped(*refs):
            stores = []
            for k, order in enumerate(orders):
                given = refs[lead + k * each : lead + (k + 1) * each]
                stores.append((given[0], given[1] if halving else None, refs[-1], order))
            body(*refs[:lead], *stores)

        got = call(
            wrapped,
            list(extra_outs) + outs,
            [scal[0]],
            args,
            name=name,
            scratch=[pltpu.VMEM((width, wide), BF16)],
        )
        extra, rest = got[: len(extra_outs)], got[len(extra_outs) :]
        return extra, [Reduction(rest[k * each : (k + 1) * each], order) for k, order in enumerate(orders)]

    reductions = []
    feeds = []
    arrivals = {}
    if halving and bits == 3 and layers == 2:
        arrivals = {2: [0], 3: [0, 1], 4: [1], 5: [2]}

    def window(kept, args):
        return tie(kept, list(args))[1]

    def seal(index, got, extra, made):
        due = [reductions[g] for g in arrivals.get(index, ()) if reductions[g].step < bits]
        firsts = [r.parts[0] for r in made] if halving else []
        extra, firsts, parts = tie(list(extra), firsts, [r.parts for r in due])
        for r, p in zip(due, parts):
            r.parts = list(p)
            r.advance()
        got, extra, firsts = tie(got, extra, firsts)
        for r, part in zip(made, firsts):
            r.parts[0] = part
        reductions.extend(made)
        return got, extra

    grads = [None] * layers
    index = 0
    for layer in reversed(range(layers)):
        sc = scal[layer]
        kept1, kept2, kept3 = saved[layer]
        dm, dt = pair(dy)
        _, nm, nth, act, slope = kept3
        up, down = fetched[layer, 3]
        pm, pt, dh = call(
            lambda dm, dt, wi, wo, near_part, far_part, *r: section3_back(
                sz, dm, dt, wi, wo, natural(near_part, far_part), *r
            ),
            [rows_bf, rows_bf, shaped((2 * half, hid))],
            [],
            [dm, dt, up, down, *slope],
            name="section3_back",
        )
        a, b = shares(pm, pt)
        args = window(a, [nm, nth, dm, dt, *act, dh])
        db, feed = call(
            lambda sc, nm, nth, dm, dt, near_part, far_part, *r: section3_weights(
                sz, sc, nm, nth, dm, dt, natural(near_part, far_part), *r
            ),
            [shaped((2, hid), F32), shaped((width, 4 * hid))],
            [sc],
            args,
            name="section3_weights",
        )
        feeds.append(whole_sum(feed))
        b, (db,) = seal(index, b, [db], [])
        index += 1
        out_bias_sums = bias_sums
        grad, dy, sums3 = close(grad, a, b, kept3, layer, 4)

        dm, dt = pair(dy)
        _, nm, nth, qq, kvv, oq, stn, stf, qv, kvq, ov, stv = kept2
        part = call(
            lambda *r: section2_back(sz, heads, *r),
            [
                rows_bf,
                rows_bf,
                shaped((sz.qlen, edev)),
                shaped((2 * vp, 2 * edev)),
                shaped((2 * vp, edev)),
                shaped((sz.qlen, 2 * edev)),
            ],
            [sc],
            [
                dm, dt, *fetched[layer, 2],
                qq, kvv, stn, stf, qv, kvq, stv,
            ],
            name="section2_back",
            scratch=[pltpu.VMEM((sz.qlen, edev), BF16), pltpu.VMEM((2 * vp, edev), BF16)],
        )
        a, b = shares(part[0], part[1])
        args = window(a, [nm, nth, dm, dt, part[2], part[3], part[4], part[5], oq, ov])
        _, made = weights(
            lambda *r: section2_weights(sz, heads, *r), [], [straight], 8 * edev, args, 2 * edev, "section2_weights"
        )
        b, _ = seal(index, b, [], made)
        index += 1
        grad, dy, sums2 = close(grad, a, b, kept2, layer, 2)

        dm, dt = pair(dy)
        _, nm, nth, nvw, qkvv, ov, stv, qkvq, oq, stn, stf = kept1
        part = call(
            lambda *r: section1_back(sz, heads, *r),
            [
                rows_bf,
                rows_bf,
                shaped((sz.vis, 3 * edev)),
                shaped((sz.qlen, 3 * edev)),
                shaped((heads, sz.vis, sz.vis)),
            ],
            [sc],
            [
                dm, dt, *fetched[layer, 1],
                Part(bias_all, layer), qkvv, stv, qkvq, stn, stf,
            ],
            name="section1_back",
            scratch=[pltpu.VMEM((sz.qlen, edev), BF16), pltpu.VMEM((sz.vis, edev), BF16)],
        )
        a, b = shares(part[0], part[1])
        args = window(a, [nm, nth, dm, dt, nvw, part[2], part[3], oq, ov])
        _, made = weights(
            lambda *r: section1_weights(sz, heads, *r), [], [straight], 8 * edev, args, 3 * edev, "section1_weights"
        )
        b, _ = seal(index, b, [], made)
        (table,) = call(table_grad, [shaped((8, TABLE_PAD), F32)], [], [part[4], spread], name="table_grad")
        index += 1
        grad, dy, sums1 = close(grad, a, b, kept1, layer, 0)
        bias_sums = sums1
        grads[layer] = (sums1, sums2, sums3, out_bias_sums, db, table)

    if halving:
        for r in reductions:
            while r.step < bits:
                r.advance()

    own_total = piece_of(grad, chip) + (own_grad - rounded_grad)
    grad_v, grad_q = own_total[0:vq], own_total[sz.vpiece :]

    def summed(x, axis, size, steps):
        for bit in steps:
            x = x + lax.ppermute(x, axis, [(i, i ^ bit) for i in range(size)])
        return x

    per_norm = 14 * layers
    count = -(-(per_norm + (2 + heads) * layers) // 8) * 8
    (rows,) = call(
        lambda *r: collect(layers, heads, *r),
        [shaped((count, width), F32)],
        [],
        [x for g in grads for x in g],
        name="collect",
    )
    twice = lax.ppermute(rows, "tensor", swap)
    rows = rows + jnp.where(iota((count, 1), 0) < per_norm, twice, 0.0)
    rows = summed(rows, "dp", dp_size, [1 << k for k in range(bits)])
    scale_total, shift_total, out_bias_total, in_bias_total, rel_total = call(
        lambda *r: deal(layers, heads, *r),
        [shaped((6, layers, width), F32)] * 2
        + [shaped((layers, 2, width), F32), shaped((layers, 2, hid), F32), shaped((heads, layers, TABLE), F32)],
        [],
        [rows],
        name="deal",
    )

    d_up, d_down = call(
        lambda *r: finish_mlp(layers, *r),
        [shaped((layers, 2, block_rows, hid), F32)] * 2,
        [],
        feeds[::-1],
        name="finish_mlp",
    )
    sums = [reductions[2 * (layers - 1 - layer) : 2 * (layers - layer)] for layer in range(layers)]
    d_in, d_out = call(
        lambda *r: finish_attn(layers, *r),
        [shaped((layers, 4, 3, block_rows, edev), F32), shaped((layers, 4, edev, block_rows), F32)],
        [],
        [p for r in sums for p in r[1].pieces() + r[0].pieces()],
        name="finish_attn",
    )
    return (
        out_v[None],
        out_q[None],
        grad_v[None],
        grad_q[None],
        scale_total.transpose(1, 0, 2),
        shift_total.transpose(1, 0, 2),
        d_in.transpose(0, 1, 3, 2, 4),
        d_out,
        rel_total.transpose(1, 0, 2),
        d_up,
        in_bias_total,
        d_down.transpose(0, 1, 3, 2),
        out_bias_total,
    )


def solution(mesh):
    dp_size = mesh.shape["dp"]
    return jax.shard_map(
        lambda *args: on_device(dp_size, *args),
        mesh=mesh,
        in_specs=(
            P("dp", "tensor", None),
            P("dp", "tensor", None),
            P("dp", None),
            P("dp"),
            P("dp", None),
            P(),
            P(),
            P(None, None, None, None, "tensor"),
            P(None, None, "tensor", None),
            P(None, "tensor", None),
            P(None, None, None, "tensor"),
            P(None, None, "tensor"),
            P(None, None, "tensor", None),
            P(),
            P("dp", "tensor", None),
            P("dp", "tensor", None),
        ),
        out_specs=(
            P("dp", "tensor", None),
            P("dp", "tensor", None),
            P("dp", "tensor", None),
            P("dp", "tensor", None),
            P(),
            P(),
            P(None, None, "dp", None, "tensor"),
            P(None, None, "tensor", "dp"),
            P(None, "tensor", None),
            P(None, None, "dp", "tensor"),
            P(None, None, "tensor"),
            P(None, None, "tensor", "dp"),
            P(),
        ),
        check_vma=False,
    )
```
